32 devices in a mesh: section: 2 (over x), replica: 2 (over core), shard: 8 (over z, y).
Axes of the slice: x: 2, y: 2, z: 4, core: 2. Of those that a mesh axis runs over, the one named last changes fastest.
Arguments:
- tokens: bfloat16 [4, 1024, 768], P('replica', 'shard'), may hold values from -6 to 6
- cotangent: bfloat16 [4, 1024, 768], P('replica', 'shard'), may hold values from -6 to 6
- group_order: int32 [4, 8], P('replica'), may hold values from 0 to 7, each once within a row
- norm_gains: bfloat16 [2, 2, 768], P('section', None, 'shard'), may hold values from 0.099609375 to 1.8984375
- norm_biases: bfloat16 [2, 2, 768], P('section', None, 'shard'), may hold values from -3 to 3
- w_qkv: bfloat16 [2, 768, 2304], P('section', 'shard'), may hold values from -0.21875 to 0.21875
- qv_bias: bfloat16 [2, 2, 768], P('section', None, 'shard'), may hold values from -3 to 3
- w_out: bfloat16 [2, 768, 768], P('section', 'shard'), may hold values from -1.25 to 1.25
- out_bias: bfloat16 [2, 768], P('section', 'shard'), may hold values from -3 to 3
- w_fc: bfloat16 [2, 768, 3072], P('section', 'shard'), may hold values from -0.21875 to 0.21875
- fc_bias: bfloat16 [2, 3072], P('section', 'shard'), may hold values from -3 to 3
- w_proj: bfloat16 [2, 3072, 768], P('section', 'shard'), may hold values from -0.109375 to 0.109375
- proj_bias: bfloat16 [2, 768], P('section', 'shard'), may hold values from -3 to 3
Outputs:
- acts: bfloat16 [2, 4, 1024, 768], P('section', 'replica', 'shard')
- in_grads: float32 [2, 4, 1024, 768], P('section', 'replica', 'shard')
- norm_gains_grad: float32 [2, 2, 768], P('section', None, 'shard')
- norm_biases_grad: float32 [2, 2, 768], P('section', None, 'shard')
- w_qkv_grad: float32 [2, 768, 2304], P('section', 'shard')
- qv_bias_grad: float32 [2, 2, 768], P('section', None, 'shard')
- w_out_grad: float32 [2, 768, 768], P('section', 'shard')
- out_bias_grad: float32 [2, 768], P('section', 'shard')
- w_fc_grad: float32 [2, 768, 3072], P('section', 'shard')
- fc_bias_grad: float32 [2, 3072], P('section', 'shard')
- w_proj_grad: float32 [2, 3072, 768], P('section', 'shard')
- proj_bias_grad: float32 [2, 768], P('section', 'shard')
The draws below stay inside these ranges and needn't reach their ends.
Inputs may be any that keep to these rules, and one draw needn't show every extreme that they name: Each row of group_order holds every number 0 to 7 once.
All inputs are finite; a program needn't handle non-finite values.
Results may differ from the reference program's by a relative error of at most 0.02.
Values may be sent and summed in bfloat16 or wider, within the bound.
No kernel may reach another device: no remote copies, remote signals or barrier semaphores. Data moves between devices by JAX's collectives and lax.ppermute only.
A program may use at most 192 MiB of HBM per device.

```python
import math
import jax
import jax.numpy as jnp
from jax import lax

D = 768
HEADS = 12
HEAD = 64
FF = 3072
SEG_DEV = 128
LAYERS = 2
SEQS = 4
SEQ_LEN = 1024
N_SHARD = 8


def levels(own_key, shape, pieces, least, largest):
    level, own = 1.0, jax.random.fold_in(own_key, 6)
    for axis_at, blocks in pieces:
        heights = jnp.exp(jax.random.uniform(jax.random.fold_in(own, axis_at), (blocks,), jnp.float32, least / len(pieces), largest / len(pieces)))
        level = level * jnp.repeat(heights, shape[axis_at] // blocks).reshape([-1 if axis == axis_at else 1 for axis in range(len(shape))])
    return level


def scatter_about(own_key, shape, deviation, bound, cuts=(), kind=jnp.bfloat16):
    result = jax.random.normal(own_key, shape, jnp.float32) * deviation
    if len(cuts) > 0:
        result = levels(own_key, shape, cuts, -0.22, 0.18) * result
    return jnp.clip(result, min=-bound, max=bound).astype(kind)


def setup_inputs(seed: int = 0) -> dict:
    keys = jax.random.split(jax.random.key(seed), 14)
    tokens = scatter_about(keys[0], (SEQS, SEQ_LEN, D), 1.0, 6.0, ((0, 2), (1, 8)))
    cotangent = scatter_about(keys[1], (SEQS, SEQ_LEN, D), 1.0, 6.0, ((0, 2), (1, 8)))
    group_order = jax.vmap(lambda own: jax.random.permutation(own, N_SHARD))(jax.random.split(keys[2], SEQS)).reshape((SEQS, N_SHARD)).astype(jnp.int32)
    norm_gains = jnp.clip(1.0 + 0.18 * jax.random.normal(keys[3], (LAYERS, 2, D), jnp.float32), 0.099609375, 1.8984375).astype(jnp.bfloat16)
    norm_biases = scatter_about(keys[4], (LAYERS, 2, D), 0.5, 3.0, ((0, 2), (2, 8)))
    w_qkv = scatter_about(keys[5], (LAYERS, D, 3 * D), D ** -0.5, 0.21875, ((0, 2), (1, 8)))
    qv_bias = scatter_about(keys[6], (LAYERS, 2, D), 0.5, 3.0, ((0, 2), (2, 8)))
    w_out = scatter_about(keys[7], (LAYERS, D, D), (D // 32) ** -0.5, 1.25, ((0, 2), (1, 8)))
    out_bias = scatter_about(keys[8], (LAYERS, D), 0.5, 3.0, ((0, 2), (1, 8)))
    w_fc = scatter_about(keys[9], (LAYERS, D, FF), D ** -0.5, 0.21875, ((0, 2), (1, 8)))
    fc_bias = scatter_about(keys[10], (LAYERS, FF), 0.5, 3.0, ((0, 2), (1, 8)))
    w_proj = scatter_about(keys[11], (LAYERS, FF, D), FF ** -0.5, 0.109375, ((0, 2), (1, 8)))
    proj_bias = scatter_about(keys[12], (LAYERS, D), 0.5, 3.0, ((0, 2), (1, 8)))
    return dict(tokens=tokens, cotangent=cotangent, group_order=group_order, norm_gains=norm_gains, norm_biases=norm_biases, w_qkv=w_qkv, qv_bias=qv_bias, w_out=w_out, out_bias=out_bias, w_fc=w_fc, fc_bias=fc_bias, w_proj=w_proj, proj_bias=proj_bias)


EPSILON = 1e-05
SCALING = 0.125
HIGHEST = lax.Precision.HIGHEST

@jax.custom_vjp
def low(v):
    return lax.optimization_barrier(v.astype(jnp.bfloat16)).astype(jnp.float32)

@jax.custom_vjp
def low_back(v):
    return v

def low_keep(v):
    return (low(v), None)

def low_pass(kept, grad):
    return (grad,)

def back_keep(v):
    return (v, None)

def back_low(kept, grad):
    return (low(grad),)
low.defvjp(low_keep, low_pass)
low_back.defvjp(back_keep, back_low)

def normalize(values, gain_row, offset):
    average = lax.optimization_barrier(jnp.mean(values, axis=-1, keepdims=True))
    centred = values - average
    variance = lax.optimization_barrier(jnp.mean(centred * centred, axis=-1, keepdims=True))
    return centred * lax.rsqrt(variance + EPSILON) * gain_row + offset

def attention(queries, all_keys, all_values, positions):
    length = queries.shape[0]
    query_rows = math.gcd(length, 512)
    key_heads = all_keys.reshape(length, HEADS, HEAD)
    value_heads = all_values.reshape(length, HEADS, HEAD)

    def one_block(query_pair):
        query_block, query_pos = query_pair
        scores = jnp.einsum('ihd,jhd->hij', query_block, key_heads, precision=HIGHEST) * SCALING
        scores = low_back(scores)
        visible = positions[None, None, :] <= query_pos[None, :, None]
        weights = jax.nn.softmax(jnp.where(visible, scores, -1e+30), axis=-1)
        attended = jnp.einsum('hij,jhd->ihd', low(weights), value_heads, precision=HIGHEST)
        return attended.reshape(query_rows, HEADS * HEAD)
    blocks = lax.map(jax.checkpoint(one_block), (queries.reshape(length // query_rows, query_rows, HEADS, HEAD), positions.reshape(length // query_rows, query_rows)))
    return blocks.reshape(length, HEADS * HEAD)

def layer_step(inputs, positions, params):
    gain_rows, offset_rows, w_qkv, qv_bias, w_out, out_bias, w_fc, fc_bias, w_proj, proj_bias = params
    model_width = inputs.shape[1]
    normed = low(normalize(inputs, gain_rows[0], offset_rows[0]))
    joined = jnp.dot(normed, w_qkv, precision=HIGHEST)
    queries = low(low_back(joined[:, :model_width] + qv_bias[0]))
    key_local = low(low_back(joined[:, model_width:2 * model_width]))
    value_local = low(low_back(joined[:, 2 * model_width:] + qv_bias[1]))
    attended = low(low_back(attention(queries, key_local, value_local, positions)))
    middle = inputs + low_back(jnp.dot(attended, w_out, precision=HIGHEST) + out_bias)
    normed_two = low(normalize(middle, gain_rows[1], offset_rows[1]))
    hidden = low_back(jnp.dot(normed_two, w_fc, precision=HIGHEST) + fc_bias)
    active = low(jax.nn.gelu(hidden, approximate=True))
    return middle + low_back(jnp.dot(active, w_proj, precision=HIGHEST) + proj_bias)

def forward(weights, tokens, probes, positions):
    current = tokens
    outputs = []
    for layer_index in range(LAYERS):
        layer_weights = tuple((member[layer_index] for member in weights))
        if layer_index > 0:
            current = low(low_back(current))
        current = current + probes[layer_index]
        current = lax.map(lambda seq_pair: layer_step(seq_pair[0], seq_pair[1], layer_weights), (current, positions))
        outputs.append(current)
    return jnp.stack(outputs)

def reference(tokens, cotangent, group_order, norm_gains, norm_biases, w_qkv, qv_bias, w_out, out_bias, w_fc, fc_bias, w_proj, proj_bias):
    weights = tuple((member.astype(jnp.float32) for member in (norm_gains, norm_biases, w_qkv, qv_bias, w_out, out_bias, w_fc, fc_bias, w_proj, proj_bias)))
    offsets = jnp.arange(SEG_DEV, dtype=jnp.int32)
    positions = (group_order[:, :, None] * SEG_DEV + offsets[None, None, :]).reshape(SEQS, SEQ_LEN).astype(jnp.int32)
    inputs = tokens.astype(jnp.float32)
    probes = jnp.zeros((LAYERS, SEQS, SEQ_LEN, D), jnp.float32)
    outputs, pullback = jax.vjp(lambda wts, prb: forward(wts, inputs, prb, positions), weights, probes)
    upstream = jnp.zeros((LAYERS, SEQS, SEQ_LEN, D), jnp.float32).at[LAYERS - 1].set(cotangent.astype(jnp.float32))
    weight_grads, in_grads = pullback(upstream)
    return (outputs.astype(jnp.bfloat16), in_grads, weight_grads[0], weight_grads[1], weight_grads[2], weight_grads[3], weight_grads[4], weight_grads[5], weight_grads[6], weight_grads[7], weight_grads[8], weight_grads[9])
```

```python
import math

import jax
import jax.numpy as jnp
import numpy as np
from jax import lax
from jax.sharding import PartitionSpec as P

HEADS = 12
HEAD = 64
EPSILON = 1e-05
SCALING = 0.125
FLOOR = -1e30
LOW = jnp.bfloat16
F32 = jnp.float32


def ring_order(count):
    return list(range(0, count, 2)) + list(range(count - 1, 0, -2))


def ring_pairs(count):
    order = ring_order(count)
    right = [(order[i], order[(i + 1) % count]) for i in range(count)]
    return right, [(b, a) for a, b in right]


def ring_gather(chunk, count):
    right, left = ring_pairs(count)
    got = {0: chunk}
    from_left = from_right = chunk
    cut = chunk.shape[0] // 32 * 16
    for step in range(1, count // 2 + 1):
        if step == count // 2:
            got[step] = jnp.concatenate(
                [
                    lax.ppermute(from_left[:cut], "shard", right),
                    lax.ppermute(from_right[cut:], "shard", left),
                ],
                axis=0,
            )
        else:
            from_left = lax.ppermute(from_left, "shard", right)
            from_right = lax.ppermute(from_right, "shard", left)
            got[count - step] = from_left
            got[step] = from_right
    return [got[k] for k in range(count)]


def ring_scatter(piece, rows, count):
    right, left = ring_pairs(count)
    cut = rows // 32 * 16
    half = count // 2
    far = piece(half)
    to_right = lax.ppermute(far[:cut], "shard", right)
    to_left = lax.ppermute(far[cut:], "shard", left)
    for distance in range(half - 1, 0, -1):
        first, second = piece(distance), piece(count - distance)
        if distance == half - 1:
            first = jnp.concatenate([add_low(first[:cut], to_right), first[cut:]], axis=0)
            second = jnp.concatenate([second[:cut], add_low(second[cut:], to_left)], axis=0)
        else:
            first = add_low(first, to_right)
            second = add_low(second, to_left)
        to_right = lax.ppermute(first, "shard", right)
        to_left = lax.ppermute(second, "shard", left)
    return piece(0).astype(F32) + to_right.astype(F32) + to_left.astype(F32)


def add_low(a, b):
    return (a.astype(F32) + b.astype(F32)).astype(LOW)


def swap(x, axis):
    return lax.ppermute(x, axis, [(0, 1), (1, 0)])


def normalize(values, gain_row, offset):
    average = jnp.mean(values, axis=-1, keepdims=True)
    centred = values - average
    variance = jnp.mean(centred * centred, axis=-1, keepdims=True)
    return centred * lax.rsqrt(variance + EPSILON) * gain_row + offset


def gelu_tanh(values):
    return jax.nn.gelu(values, approximate=True)


def dot(a, b):
    return jnp.dot(a, b, preferred_element_type=F32)


def dot_t(a, b):
    return jnp.einsum("tc,dc->td", a, b, preferred_element_type=F32)


def dot_rows(a, b):
    return jnp.einsum("ta,tb->ab", a, b, preferred_element_type=F32)


class Plan:
    def __init__(self, count, segment):
        self.count = count
        self.segment = segment
        self.splits = count // math.gcd(HEADS, count)
        self.units = HEADS * self.splits // count
        self.part = segment // self.splits
        self.first = [self.units * q // self.splits for q in range(count)]
        self.slots = max(
            (self.units * q + self.units - 1) // self.splits - self.first[q] + 1
            for q in range(count)
        )
        self.groups = [
            [r * count + h * (count // 2) + i for r in range(2) for i in range(count // 2)]
            for h in range(2)
        ]

    def exchange(self, blocks):
        return lax.all_to_all(
            blocks, ("replica", "shard"), 0, 0, tiled=True, axis_index_groups=self.groups
        )

    def pack_units(self, heads):
        parts = heads.reshape(self.splits, self.part, HEADS, HEAD)
        parts = parts.transpose(2, 0, 1, 3).reshape(
            self.count, self.units * self.part, HEAD
        )
        return self.fold(parts)

    def fold(self, parts):
        rows = parts.shape[1] // 2
        return jnp.concatenate([parts[:, :rows], parts[:, rows:]], axis=2)

    def unfold(self, folded):
        return jnp.concatenate([folded[..., :HEAD], folded[..., HEAD:]], axis=1)

    def unpack_units(self, folded):
        parts = self.unfold(folded).reshape(HEADS, self.splits, self.part, HEAD)
        return parts.transpose(1, 2, 0, 3).reshape(self.segment, HEADS * HEAD)

    def gather_units(self, folded):
        parts = self.unfold(folded).reshape(self.count, self.units, self.part, HEAD)
        return parts.transpose(1, 0, 2, 3).reshape(self.units, self.count * self.part, HEAD)

    def scatter_units(self, values):
        parts = values.reshape(self.units, self.count, self.part, HEAD).transpose(1, 0, 2, 3)
        return self.fold(parts.reshape(self.count, self.units * self.part, HEAD))

    def head_slots(self, rows):
        blocks = []
        for q in range(self.count):
            cols = []
            for slot in range(self.slots):
                head = min(self.first[q] + slot, HEADS - 1)
                cols.append(rows[:, head * HEAD : (head + 1) * HEAD])
            blocks.append(jnp.concatenate(cols, axis=1))
        return jnp.stack(blocks)

    def sum_slots(self, blocks):
        cols = []
        for head in range(HEADS):
            total = None
            for q in range(self.count):
                last = (self.units * (q + 1) - 1) // self.splits
                if self.first[q] <= head <= last:
                    slot = head - self.first[q]
                    term = blocks[q, :, slot * HEAD : (slot + 1) * HEAD].astype(F32)
                    total = term if total is None else total + term
            cols.append(total)
        return jnp.concatenate(cols, axis=1)


def widen(units, slot, slots):
    wide = jnp.concatenate([units] * slots, axis=2)
    lane_slot = jnp.arange(slots * HEAD, dtype=jnp.int32) // HEAD
    return jnp.where(lane_slot[None, None, :] == slot[:, None, None], wide, jnp.zeros_like(wide))


def narrow(wide, slot, slots):
    lane_slot = jnp.arange(slots * HEAD, dtype=jnp.int32) // HEAD
    wide = jnp.where(lane_slot[None, None, :] == slot[:, None, None], wide, jnp.zeros_like(wide))
    return sum(wide[:, :, s * HEAD : (s + 1) * HEAD] for s in range(slots))


def attend_forward(queries, keys, values, query_pos, key_pos):
    scores = jnp.einsum("uid,jd->uij", queries, keys, preferred_element_type=F32) * SCALING
    visible = key_pos[None, None, :] <= query_pos[:, :, None]
    scores = jnp.where(visible, scores, FLOOR)
    highest = jnp.max(scores, axis=-1, keepdims=True)
    terms = jnp.exp(scores - highest)
    total = jnp.sum(terms, axis=-1, keepdims=True)
    weights = (terms / total).astype(LOW)
    attended = jnp.einsum("uij,jd->uid", weights, values, preferred_element_type=F32)
    return attended, highest + jnp.log(total)


def attend_backward(queries, keys, values, query_pos, key_pos, log_total, grad, row_dots):
    scores = jnp.einsum("uid,jd->uij", queries, keys, preferred_element_type=F32) * SCALING
    visible = key_pos[None, None, :] <= query_pos[:, :, None]
    weights = jnp.where(visible, jnp.exp(scores - log_total), 0.0)
    grad_weights = jnp.einsum("uid,jd->uij", grad, values, preferred_element_type=F32)
    grad_scores = (weights * (grad_weights - row_dots)).astype(LOW)
    grad_queries = (
        jnp.einsum("uij,jd->uid", grad_scores, keys, preferred_element_type=F32) * SCALING
    )
    grad_keys = (
        jnp.einsum("uij,uid->jd", grad_scores, queries, preferred_element_type=F32) * SCALING
    )
    grad_values = jnp.einsum("uij,uid->jd", weights.astype(LOW), grad, preferred_element_type=F32)
    return grad_queries, grad_keys, grad_values


def layer_forward(inputs, weights, plan, place):
    normed = normalize(inputs, weights["gains"][0], weights["offsets"][0]).astype(LOW)
    queries = (dot(normed, weights["q"]) + weights["q_bias"]).astype(LOW)
    keys = dot(normed, weights["k"]).astype(LOW)
    values = (dot(normed, weights["v"]) + weights["v_bias"]).astype(LOW)
    segment = inputs.shape[0]
    width = plan.slots * HEAD
    sent = jnp.concatenate(
        [
            plan.head_slots(keys),
            plan.head_slots(values),
            plan.pack_units(queries.reshape(segment, HEADS, HEAD)).reshape(
                plan.count, -1, width
            ),
        ],
        axis=1,
    )
    arrived = plan.exchange(sent)
    length = plan.count * segment
    all_keys = arrived[:, :segment].reshape(length, width)
    all_values = arrived[:, segment : 2 * segment].reshape(length, width)
    units = plan.gather_units(arrived[:, 2 * segment :].reshape(plan.count, -1, 2 * HEAD))
    units = widen(units, place["slot"], plan.slots)
    attended, log_total = attend_forward(
        units, all_keys, all_values, place["query_pos"], place["key_pos"]
    )
    attended = narrow(attended, place["slot"], plan.slots)
    returned = plan.exchange(plan.scatter_units(attended.astype(LOW)))
    attended_low = plan.unpack_units(returned)
    middle = inputs + dot(attended_low, weights["o"]) + weights["out_bias"]
    normed_two = normalize(middle, weights["gains"][1], weights["offsets"][1]).astype(LOW)
    hidden = dot(normed_two, weights["fc"]) + weights["fc_bias"]
    active = gelu_tanh(hidden).astype(LOW)
    output = middle + dot(active, weights["proj"]) + weights["proj_bias"]
    saved = dict(
        inputs=inputs, normed=normed, units=units, keys=all_keys, values=all_values,
        attended=attended, log_total=log_total, attended_low=attended_low, middle=middle,
        normed_two=normed_two, hidden=hidden, active=active,
    )
    return output, saved


def layer_backward(arriving, saved, weights, plan, place):
    segment, model_width = arriving.shape
    grad_branch = arriving.astype(LOW)
    grad_active = dot_t(grad_branch, weights["proj"])
    grad_hidden = jax.vjp(gelu_tanh, saved["hidden"])[1](grad_active)[0].astype(LOW)
    grad_normed_two = dot_t(grad_hidden, weights["fc"])
    grad_middle_norm, gain_two, offset_two = jax.vjp(
        normalize, saved["middle"], weights["gains"][1], weights["offsets"][1]
    )[1](grad_normed_two)
    grads = dict(
        proj=dot_rows(saved["active"], grad_branch),
        proj_bias=jnp.sum(grad_branch.astype(F32), axis=0),
        fc=dot_rows(saved["normed_two"], grad_hidden),
        fc_bias=jnp.sum(grad_hidden.astype(F32), axis=0),
    )
    grad_middle = arriving + grad_middle_norm
    grad_out = grad_middle.astype(LOW)
    grad_attended = dot_t(grad_out, weights["o"]).astype(LOW)
    arrived = plan.exchange(plan.pack_units(grad_attended.reshape(segment, HEADS, HEAD)))
    grad_units = plan.gather_units(arrived)
    row_dots = jnp.sum(grad_units.astype(F32) * saved["attended"], axis=-1, keepdims=True)
    grad_queries, grad_keys, grad_values = attend_backward(
        saved["units"], saved["keys"], saved["values"], place["query_pos"], place["key_pos"],
        saved["log_total"], widen(grad_units, place["slot"], plan.slots), row_dots,
    )
    grad_queries = narrow(grad_queries, place["slot"], plan.slots).astype(LOW)
    width = plan.slots * HEAD
    sent = jnp.concatenate(
        [
            grad_keys.astype(LOW).reshape(plan.count, segment, width),
            grad_values.astype(LOW).reshape(plan.count, segment, width),
            plan.scatter_units(grad_queries).reshape(plan.count, -1, width),
        ],
        axis=1,
    )
    returned = plan.exchange(sent)
    grad_k = plan.sum_slots(returned[:, :segment]).astype(LOW)
    grad_v = plan.sum_slots(returned[:, segment : 2 * segment]).astype(LOW)
    grad_q = plan.unpack_units(returned[:, 2 * segment :].reshape(plan.count, -1, 2 * HEAD))
    grad_normed = (
        dot_t(grad_q, weights["q"]) + dot_t(grad_k, weights["k"]) + dot_t(grad_v, weights["v"])
    )
    grad_input_norm, gain_one, offset_one = jax.vjp(
        normalize, saved["inputs"], weights["gains"][0], weights["offsets"][0]
    )[1](grad_normed)
    grads.update(
        gains=jnp.stack([gain_one, gain_two]),
        offsets=jnp.stack([offset_one, offset_two]),
        q=dot_rows(saved["normed"], grad_q),
        k=dot_rows(saved["normed"], grad_k),
        v=dot_rows(saved["normed"], grad_v),
        qv_bias=jnp.stack([jnp.sum(grad_q.astype(F32), axis=0), jnp.sum(grad_v.astype(F32), axis=0)]),
        o=dot_rows(saved["attended_low"], grad_out),
        out_bias=jnp.sum(grad_out.astype(F32), axis=0),
    )
    return grad_middle + grad_input_norm, grads


def on_device(
    tokens, cotangent, group_order, norm_gains, norm_biases, w_qkv, qv_bias, w_out, out_bias,
    w_fc, fc_bias, w_proj, proj_bias,
):
    count = lax.axis_size("shard")
    section = lax.axis_index("section")
    replica = lax.axis_index("replica")
    shard = lax.axis_index("shard")
    segment, model_width = tokens.shape[1], tokens.shape[2]
    rows = w_qkv.shape[1]
    half = count // 2
    plan = Plan(count, segment)
    order = ring_order(count)
    position_of = np.argsort(np.array(order))
    position = jnp.asarray(position_of, jnp.int32)[shard]
    order_table = jnp.asarray(order, jnp.int32)

    def owner(offset):
        return order_table[lax.rem(position + offset, count)]

    home = shard // half
    keeps = home == replica
    crossing = []
    for s in range(half):
        crossing += [(count + s, s + half), (s + half, count + s)]

    def reshard(x):
        moved = lax.ppermute(x, ("replica", "shard"), crossing)
        return jnp.where(keeps, x, moved)

    def pick(x):
        return lax.dynamic_index_in_dim(x, section, 0, keepdims=False)

    order_row = pick(group_order).astype(LOW)
    order_row = jnp.broadcast_to(
        jnp.concatenate([order_row, jnp.zeros((model_width - count,), LOW)])[None], (16, model_width)
    )
    packed = reshard(jnp.concatenate([pick(tokens), order_row], axis=0))
    current = packed[:segment].astype(F32)
    blocks_at = packed[segment, :count].astype(jnp.int32)
    upstream = reshard(pick(cotangent))
    seat = replica * half + lax.rem(shard, half)
    key_pos = (
        blocks_at[:, None] * segment + jnp.arange(segment, dtype=jnp.int32)[None, :]
    )
    unit_ids = plan.units * seat + jnp.arange(plan.units, dtype=jnp.int32)
    unit_part = lax.rem(unit_ids, plan.splits)
    parts_pos = key_pos.reshape(count, plan.splits, plan.part)
    query_pos = jnp.stack(
        [
            lax.dynamic_index_in_dim(parts_pos, unit_part[u], 1, keepdims=False).reshape(-1)
            for u in range(plan.units)
        ]
    )
    place = dict(
        slot=unit_ids // plan.splits - (plan.units * seat) // plan.splits,
        query_pos=query_pos,
        key_pos=key_pos.reshape(-1),
    )

    small = jnp.concatenate(
        [
            norm_gains[0], norm_biases[0], qv_bias[0], out_bias, fc_bias.reshape(4, rows), proj_bias,
        ],
        axis=0,
    ).reshape(-1)
    small_rows = -(-small.shape[0] // (16 * model_width)) * 16
    small = jnp.concatenate(
        [small, jnp.zeros((small_rows * model_width - small.shape[0],), LOW)]
    ).reshape(small_rows, model_width)
    qkv = w_qkv[0]
    attn_sets = (
        jnp.concatenate([qkv[:, :model_width], qkv[:, model_width : 2 * model_width], small], axis=0),
        jnp.concatenate([qkv[:, 2 * model_width :], w_out[0], small], axis=0),
    )
    fc_blocks = w_fc[0].reshape(rows, 4, model_width).transpose(1, 0, 2).reshape(4 * rows, model_width)
    ffn_sets = (fc_blocks, w_proj[0])

    def gathered(sets):
        own = jnp.where(replica == 0, sets[0], sets[1])
        other_layer = swap(own, "section")
        layers = []
        for layer in range(2):
            chunk = jnp.where(section == layer, own, other_layer)
            chunks = ring_gather(chunk, count)
            buffer = jnp.zeros((2, count) + chunk.shape, LOW)
            for offset in range(count):
                twin = swap(chunks[offset], "replica")
                at = owner(offset)
                buffer = lax.dynamic_update_slice(buffer, chunks[offset][None, None], (replica, at, 0, 0))
                buffer = lax.dynamic_update_slice(buffer, twin[None, None], (1 - replica, at, 0, 0))
            layers.append(buffer)
        return layers

    attn = gathered(attn_sets)
    ffn = gathered(ffn_sets)

    def block(buffer, which, at):
        return buffer[which, :, at * rows : (at + 1) * rows].reshape(count * rows, model_width)

    def unpacked(layer):
        a, f = attn[layer], ffn[layer]
        vec = a[0, :, 2 * rows :].reshape(count, -1)[:, : 12 * rows].reshape(count, 12, rows).astype(F32)

        def row(i):
            return vec[:, i].reshape(-1)

        return dict(
            q=block(a, 0, 0), k=block(a, 0, 1), v=block(a, 1, 0), o=block(a, 1, 1),
            fc=jnp.concatenate([block(f, 0, i) for i in range(4)], axis=1),
            proj=f[1].reshape(count * 4 * rows, model_width),
            gains=(row(0), row(1)), offsets=(row(2), row(3)), q_bias=row(4), v_bias=row(5),
            out_bias=row(6), fc_bias=vec[:, 7:11].reshape(-1), proj_bias=row(11),
        )

    weights = [unpacked(0), unpacked(1)]
    outputs, states = [], []
    for layer in range(2):
        output, saved = layer_forward(current, weights[layer], plan, place)
        outputs.append(output.astype(LOW))
        states.append(saved)
        current = outputs[-1].astype(F32)
    grad_inputs, totals = [None, None], [None, None]
    arriving = upstream.astype(F32)

    def pieces(attn_rows, layer_grads, which):
        pass

    def blocks_of(grad, cols):
        return grad.astype(LOW).reshape(count, -1, cols)

    def scattered(sets):
        own = jnp.where(replica == 0, sets[0], sets[1])
        other = jnp.where(replica == 0, sets[1], sets[0])
        paired = add_low(own, swap(other, "replica"))
        return ring_scatter(
            lambda k: lax.dynamic_index_in_dim(paired, owner(k), 0, keepdims=False),
            paired.shape[1], count,
        )

    scattered_attn, scattered_ffn = [None, None], [None, None]
    for layer in (1, 0):
        grad_input, grads = layer_backward(arriving, states[layer], weights[layer], plan, place)
        grad_inputs[layer] = grad_input
        arriving = grad_input.astype(LOW).astype(F32)
        vec = jnp.concatenate(
            [
                grads["gains"], grads["offsets"], grads["qv_bias"], grads["out_bias"][None],
            ], axis=0,
        ).reshape(7, count, rows).transpose(1, 0, 2)
        vec = jnp.concatenate(
            [vec, grads["fc_bias"].reshape(count, 4, rows), grads["proj_bias"].reshape(count, 1, rows)],
            axis=1,
        ).astype(LOW).reshape(count, 12 * rows)
        vec = jnp.concatenate(
            [vec, jnp.zeros((count, small_rows * model_width - 12 * rows), LOW)], axis=1
        ).reshape(count, small_rows, model_width)
        scattered_ffn[layer] = scattered(
            (
                jnp.concatenate(
                    [blocks_of(grads["fc"][:, i * model_width : (i + 1) * model_width], model_width) for i in range(4)],
                    axis=1,
                ),
                blocks_of(grads["proj"], model_width),
            )
        )
        scattered_attn[layer] = scattered(
            (
                jnp.concatenate([blocks_of(grads["q"], model_width), blocks_of(grads["k"], model_width), vec], axis=1),
                jnp.concatenate([blocks_of(grads["v"], model_width), blocks_of(grads["o"], model_width), vec], axis=1),
            )
        )

    def finished(parts):
        own = jnp.where(section == 0, parts[0], parts[1])
        other = jnp.where(section == 0, parts[1], parts[0]).astype(LOW)
        total = (own + swap(other, "section").astype(F32)).astype(LOW)
        twin = swap(total, "replica")
        return (
            jnp.where(replica == 0, total, twin).astype(F32),
            jnp.where(replica == 0, twin, total).astype(F32),
        )

    ffn_total = finished(scattered_ffn)
    attn_total = finished(scattered_attn)
    fc_grad = ffn_total[0].reshape(4, rows, model_width).transpose(1, 0, 2).reshape(rows, 4 * model_width)
    proj_grad = ffn_total[1]
    qkv_grad = jnp.concatenate(
        [attn_total[0][:rows], attn_total[0][rows : 2 * rows], attn_total[1][:rows]], axis=1
    )
    out_grad = attn_total[1][rows : 2 * rows]
    vec = attn_total[0][2 * rows :].reshape(-1)[: 12 * rows].reshape(12, rows)

    def by_owner(per_layer):
        low = [reshard(v.astype(LOW)) for v in per_layer]
        own = jnp.where(section == 0, low[0], low[1])
        other = jnp.where(section == 0, low[1], low[0])
        got = swap(other, "section")
        return jnp.stack([jnp.where(section == 0, own, got), jnp.where(section == 0, got, own)])[None]

    acts = by_owner(outputs)
    in_grads = by_owner(grad_inputs).astype(F32)
    return (
        acts,
        in_grads,
        vec[0:2][None],
        vec[2:4][None],
        qkv_grad[None],
        vec[4:6][None],
        out_grad[None],
        vec[6][None],
        fc_grad[None],
        vec[7:11].reshape(1, 4 * rows),
        proj_grad[None],
        vec[11][None],
    )


def solution(mesh):
    in_specs = (
        P("replica", "shard", None),
        P("replica", "shard", None),
        P("replica", None),
        P("section", None, "shard"),
        P("section", None, "shard"),
        P("section", "shard", None),
        P("section", None, "shard"),
        P("section", "shard", None),
        P("section", "shard"),
        P("section", "shard", None),
        P("section", "shard"),
        P("section", "shard", None),
        P("section", "shard"),
    )
    out_specs = (
        P("section", "replica", "shard", None),
        P("section", "replica", "shard", None),
        P("section", None, "shard"),
        P("section", None, "shard"),
        P("section", "shard", None),
        P("section", None, "shard"),
        P("section", "shard", None),
        P("section", "shard"),
        P("section", "shard", None),
        P("section", "shard"),
        P("section", "shard", None),
        P("section", "shard"),
    )
    return jax.shard_map(
        on_device, mesh=mesh, in_specs=in_specs, out_specs=out_specs, check_vma=False
    )
```

```python
import math
from types import SimpleNamespace as Bag

import jax
import jax.numpy as jnp
import numpy as np
from jax import lax
from jax.experimental import pallas as pl
from jax.experimental.pallas import tpu as pltpu
from jax.sharding import PartitionSpec as P

HEADS = 12
HEAD = 64
EPSILON = 1e-05
SCALING = 0.125
FLOOR = -1e30
SECTION, REPLICA, SHARD = "section", "replica", "shard"
LOW = jnp.bfloat16
F32 = jnp.float32


def ring_order(count):
    return list(range(0, count, 2)) + list(range(count - 1, 0, -2))


def ring_pairs(count):
    order = ring_order(count)
    right = [(order[i], order[(i + 1) % count]) for i in range(count)]
    return right, [(b, a) for a, b in right]


def ring_gather(chunk, count):
    right, left = ring_pairs(count)
    got = {0: chunk}
    from_left = from_right = chunk
    cut = chunk.shape[0] // 32 * 16
    for step in range(1, count // 2 + 1):
        if step == count // 2:
            got[step] = jnp.concatenate(
                [
                    lax.ppermute(from_left[:cut], SHARD, right),
                    lax.ppermute(from_right[cut:], SHARD, left),
                ],
                axis=0,
            )
        else:
            from_left = lax.ppermute(from_left, SHARD, right)
            from_right = lax.ppermute(from_right, SHARD, left)
            got[count - step] = from_left
            got[step] = from_right
    return [got[k] for k in range(count)]


def ring_scatter(piece, rows, count):
    right, left = ring_pairs(count)
    cut = rows // 32 * 16
    half = count // 2
    far = piece(half)
    to_right = lax.ppermute(far[:cut], SHARD, right)
    to_left = lax.ppermute(far[cut:], SHARD, left)
    for distance in range(half - 1, 0, -1):
        first, second = piece(distance), piece(count - distance)
        if distance == half - 1:
            first = jnp.concatenate([add_low(first[:cut], to_right), first[cut:]], axis=0)
            second = jnp.concatenate([second[:cut], add_low(second[cut:], to_left)], axis=0)
        else:
            first = add_low(first, to_right)
            second = add_low(second, to_left)
        to_right = lax.ppermute(first, SHARD, right)
        to_left = lax.ppermute(second, SHARD, left)
    return piece(0).astype(F32) + to_right.astype(F32) + to_left.astype(F32)


def add_low(a, b):
    return (a.astype(F32) + b.astype(F32)).astype(LOW)


def swap(x, axis):
    return lax.ppermute(x, axis, [(0, 1), (1, 0)])


def normalize(values, gain_row, offset):
    average = jnp.mean(values, axis=-1, keepdims=True)
    centred = values - average
    variance = jnp.mean(centred * centred, axis=-1, keepdims=True)
    return centred * lax.rsqrt(variance + EPSILON) * gain_row + offset


def gelu_tanh(values):
    return jax.nn.gelu(values, approximate=True)


def dot(a, b):
    return jnp.dot(a, b, preferred_element_type=F32)


def dot_t(a, b):
    return lax.dot_general(a, b, (((1,), (1,)), ((), ())), preferred_element_type=F32)


def dot_rows(a, b):
    return lax.dot_general(a, b, (((0,), (0,)), ((), ())), preferred_element_type=F32)


class Plan:
    def __init__(self, count, segment):
        self.count = count
        self.segment = segment
        self.splits = count // math.gcd(HEADS, count)
        self.units = HEADS * self.splits // count
        self.part = segment // self.splits
        self.first = [self.units * q // self.splits for q in range(count)]
        self.slots = max(
            (self.units * q + self.units - 1) // self.splits - self.first[q] + 1
            for q in range(count)
        )
        self.groups = [
            [r * count + h * (count // 2) + i for r in range(2) for i in range(count // 2)]
            for h in range(2)
        ]

    def exchange(self, blocks):
        return lax.all_to_all(
            blocks, (REPLICA, SHARD), 0, 0, tiled=True, axis_index_groups=self.groups
        )

    def pack_units(self, heads):
        parts = heads.reshape(self.splits, self.part, HEADS, HEAD)
        parts = parts.transpose(2, 0, 1, 3).reshape(
            self.count, self.units * self.part, HEAD
        )
        return self.fold(parts)

    def fold(self, parts):
        rows = parts.shape[1] // 2
        return jnp.concatenate([parts[:, :rows], parts[:, rows:]], axis=2)

    def unfold(self, folded):
        return jnp.concatenate([folded[..., :HEAD], folded[..., HEAD:]], axis=1)

    def unpack_units(self, folded):
        parts = self.unfold(folded).reshape(HEADS, self.splits, self.part, HEAD)
        return parts.transpose(1, 2, 0, 3).reshape(self.segment, HEADS * HEAD)

    def gather_units(self, folded):
        parts = self.unfold(folded).reshape(self.count, self.units, self.part, HEAD)
        return parts.transpose(1, 0, 2, 3).reshape(self.units, self.count * self.part, HEAD)

    def scatter_units(self, values):
        parts = values.reshape(self.units, self.count, self.part, HEAD).transpose(1, 0, 2, 3)
        return self.fold(parts.reshape(self.count, self.units * self.part, HEAD))

    def head_slots(self, rows):
        blocks = []
        for q in range(self.count):
            cols = []
            for slot in range(self.slots):
                head = min(self.first[q] + slot, HEADS - 1)
                cols.append(rows[:, head * HEAD : (head + 1) * HEAD])
            blocks.append(jnp.concatenate(cols, axis=1))
        return jnp.stack(blocks)

    def sum_slots(self, blocks):
        cols = []
        for head in range(HEADS):
            total = None
            for q in range(self.count):
                last = (self.units * (q + 1) - 1) // self.splits
                if self.first[q] <= head <= last:
                    slot = head - self.first[q]
                    term = blocks[q, :, slot * HEAD : (slot + 1) * HEAD].astype(F32)
                    total = term if total is None else total + term
            cols.append(total)
        return jnp.concatenate(cols, axis=1)


def over(a, b, dim_a, dim_b):
    return lax.dot_general(a, b, (((dim_a,), (dim_b,)), ((), ())), preferred_element_type=F32)


def over_units(a, b):
    return lax.dot_general(a, b, (((0, 1), (0, 1)), ((), ())), preferred_element_type=F32)


def widen(units, slot, slots):
    wide = jnp.concatenate([units] * slots, axis=2)
    lane_slot = jnp.arange(slots * HEAD, dtype=jnp.int32) // HEAD
    return jnp.where(lane_slot[None, None, :] == slot[:, None, None], wide, jnp.zeros_like(wide))


def narrow(wide, slot, slots):
    lane_slot = jnp.arange(slots * HEAD, dtype=jnp.int32) // HEAD
    wide = jnp.where(lane_slot[None, None, :] == slot[:, None, None], wide, jnp.zeros_like(wide))
    return sum(wide[:, :, s * HEAD : (s + 1) * HEAD] for s in range(slots))


def attend_forward(queries, keys, values, query_pos, key_pos):
    scores = over(queries, keys, 2, 1) * SCALING
    visible = key_pos[None, None, :] <= query_pos[:, :, None]
    scores = jnp.where(visible, scores, FLOOR)
    highest = jnp.max(scores, axis=-1, keepdims=True)
    terms = jnp.exp(scores - highest)
    total = jnp.sum(terms, axis=-1, keepdims=True)
    weights = (terms / total).astype(LOW)
    attended = over(weights, values, 2, 0)
    return attended, highest + jnp.log(total)


def attend_backward(queries, keys, values, query_pos, key_pos, log_total, grad, row_dots):
    scores = over(queries, keys, 2, 1) * SCALING
    visible = key_pos[None, None, :] <= query_pos[:, :, None]
    weights = jnp.where(visible, jnp.exp(scores - log_total), 0.0)
    grad_weights = over(grad, values, 2, 1)
    grad_scores = (weights * (grad_weights - row_dots)).astype(LOW)
    grad_queries = (
        over(grad_scores, keys, 2, 0) * SCALING
    )
    grad_keys = (
        over_units(grad_scores, queries) * SCALING
    )
    grad_values = over_units(weights.astype(LOW), grad)
    return grad_queries, grad_keys, grad_values


def layer_forward(inputs, weights, plan, place):
    normed = normalize(inputs, weights.gains[0], weights.offsets[0]).astype(LOW)
    queries = (dot(normed, weights.q) + weights.q_bias).astype(LOW)
    keys = dot(normed, weights.k).astype(LOW)
    values = (dot(normed, weights.v) + weights.v_bias).astype(LOW)
    segment = inputs.shape[0]
    width = plan.slots * HEAD
    sent = jnp.concatenate(
        [
            plan.head_slots(keys),
            plan.head_slots(values),
            plan.pack_units(queries.reshape(segment, HEADS, HEAD)).reshape(
                plan.count, -1, width
            ),
        ],
        axis=1,
    )
    arrived = plan.exchange(sent)
    length = plan.count * segment
    all_keys = arrived[:, :segment].reshape(length, width)
    all_values = arrived[:, segment : 2 * segment].reshape(length, width)
    units = plan.gather_units(arrived[:, 2 * segment :].reshape(plan.count, -1, 2 * HEAD))
    units = widen(units, place.slot, plan.slots)
    attended, log_total = attend_forward(
        units, all_keys, all_values, place.query_pos, place.key_pos
    )
    attended = narrow(attended, place.slot, plan.slots)
    returned = plan.exchange(plan.scatter_units(attended.astype(LOW)))
    attended_low = plan.unpack_units(returned)
    middle = inputs + dot(attended_low, weights.o) + weights.out_bias
    normed_two = normalize(middle, weights.gains[1], weights.offsets[1]).astype(LOW)
    hidden = dot(normed_two, weights.fc) + weights.fc_bias
    active = gelu_tanh(hidden).astype(LOW)
    output = middle + dot(active, weights.proj) + weights.proj_bias
    saved = Bag(
        inputs=inputs, normed=normed, units=units, keys=all_keys, values=all_values,
        attended=attended, log_total=log_total, attended_low=attended_low, middle=middle,
        normed_two=normed_two, hidden=hidden, active=active,
    )
    return output, saved


def layer_backward(arriving, saved, weights, plan, place):
    segment, model_width = arriving.shape
    grad_branch = arriving.astype(LOW)
    grad_active = dot_t(grad_branch, weights.proj)
    grad_hidden = jax.vjp(gelu_tanh, saved.hidden)[1](grad_active)[0].astype(LOW)
    grad_normed_two = dot_t(grad_hidden, weights.fc)
    grad_middle_norm, gain_two, offset_two = jax.vjp(
        normalize, saved.middle, weights.gains[1], weights.offsets[1]
    )[1](grad_normed_two)
    grads = Bag(
        proj=dot_rows(saved.active, grad_branch),
        proj_bias=jnp.sum(grad_branch.astype(F32), axis=0),
        fc=dot_rows(saved.normed_two, grad_hidden),
        fc_bias=jnp.sum(grad_hidden.astype(F32), axis=0),
    )
    grad_middle = arriving + grad_middle_norm
    grad_out = grad_middle.astype(LOW)
    grad_attended = dot_t(grad_out, weights.o).astype(LOW)
    arrived = plan.exchange(plan.pack_units(grad_attended.reshape(segment, HEADS, HEAD)))
    grad_units = plan.gather_units(arrived)
    row_dots = jnp.sum(grad_units.astype(F32) * saved.attended, axis=-1, keepdims=True)
    grad_queries, grad_keys, grad_values = attend_backward(
        saved.units, saved.keys, saved.values, place.query_pos, place.key_pos,
        saved.log_total, widen(grad_units, place.slot, plan.slots), row_dots,
    )
    grad_queries = narrow(grad_queries, place.slot, plan.slots).astype(LOW)
    width = plan.slots * HEAD
    sent = jnp.concatenate(
        [
            grad_keys.astype(LOW).reshape(plan.count, segment, width),
            grad_values.astype(LOW).reshape(plan.count, segment, width),
            plan.scatter_units(grad_queries).reshape(plan.count, -1, width),
        ],
        axis=1,
    )
    returned = plan.exchange(sent)
    grad_k = plan.sum_slots(returned[:, :segment]).astype(LOW)
    grad_v = plan.sum_slots(returned[:, segment : 2 * segment]).astype(LOW)
    grad_q = plan.unpack_units(returned[:, 2 * segment :].reshape(plan.count, -1, 2 * HEAD))
    grad_normed = (
        dot_t(grad_q, weights.q) + dot_t(grad_k, weights.k) + dot_t(grad_v, weights.v)
    )
    grad_input_norm, gain_one, offset_one = jax.vjp(
        normalize, saved.inputs, weights.gains[0], weights.offsets[0]
    )[1](grad_normed)
    grads = Bag(
        proj=grads.proj, proj_bias=grads.proj_bias, fc=grads.fc, fc_bias=grads.fc_bias,
        gains=jnp.stack([gain_one, gain_two]),
        offsets=jnp.stack([offset_one, offset_two]),
        q=dot_rows(saved.normed, grad_q),
        k=dot_rows(saved.normed, grad_k),
        v=dot_rows(saved.normed, grad_v),
        qv_bias=jnp.stack([jnp.sum(grad_q.astype(F32), axis=0), jnp.sum(grad_v.astype(F32), axis=0)]),
        o=dot_rows(saved.attended_low, grad_out),
        out_bias=jnp.sum(grad_out.astype(F32), axis=0),
    )
    return grad_middle + grad_input_norm, grads


def on_device(
    tokens, cotangent, group_order, norm_gains, norm_biases, w_qkv, qv_bias, w_out, out_bias,
    w_fc, fc_bias, w_proj, proj_bias,
):
    count = lax.axis_size(SHARD)
    section = lax.axis_index(SECTION)
    replica = lax.axis_index(REPLICA)
    shard = lax.axis_index(SHARD)
    segment, model_width = tokens.shape[1], tokens.shape[2]
    rows = w_qkv.shape[1]
    half = count // 2
    plan = Plan(count, segment)
    order = ring_order(count)
    position_of = np.argsort(np.array(order))
    position = jnp.asarray(position_of, jnp.int32)[shard]
    order_table = jnp.asarray(order, jnp.int32)

    def owner(offset):
        return order_table[lax.rem(position + offset, count)]

    home = shard // half
    keeps = home == replica
    crossing = []
    for s in range(half):
        crossing += [(count + s, s + half), (s + half, count + s)]

    def reshard(x):
        moved = lax.ppermute(x, (REPLICA, SHARD), crossing)
        return jnp.where(keeps, x, moved)

    def pick(x):
        return lax.dynamic_index_in_dim(x, section, 0, keepdims=False)

    order_row = pick(group_order).astype(LOW)
    order_row = jnp.broadcast_to(
        jnp.concatenate([order_row, jnp.zeros((model_width - count,), LOW)])[None], (16, model_width)
    )
    packed = reshard(jnp.concatenate([pick(tokens), order_row], axis=0))
    current = packed[:segment].astype(F32)
    blocks_at = packed[segment, :count].astype(jnp.int32)
    upstream = reshard(pick(cotangent))
    seat = replica * half + lax.rem(shard, half)
    key_pos = (
        blocks_at[:, None] * segment + jnp.arange(segment, dtype=jnp.int32)[None, :]
    )
    unit_ids = plan.units * seat + jnp.arange(plan.units, dtype=jnp.int32)
    unit_part = lax.rem(unit_ids, plan.splits)
    parts_pos = key_pos.reshape(count, plan.splits, plan.part)
    query_pos = jnp.stack(
        [
            lax.dynamic_index_in_dim(parts_pos, unit_part[u], 1, keepdims=False).reshape(-1)
            for u in range(plan.units)
        ]
    )
    place = Bag(
        slot=unit_ids // plan.splits - (plan.units * seat) // plan.splits,
        query_pos=query_pos,
        key_pos=key_pos.reshape(-1),
    )

    small = jnp.concatenate(
        [
            norm_gains[0], norm_biases[0], qv_bias[0], out_bias, fc_bias.reshape(4, rows), proj_bias,
        ],
        axis=0,
    ).reshape(-1)
    small_rows = -(-small.shape[0] // (16 * model_width)) * 16
    small = jnp.concatenate(
        [small, jnp.zeros((small_rows * model_width - small.shape[0],), LOW)]
    ).reshape(small_rows, model_width)
    qkv = w_qkv[0]
    attn_sets = (
        jnp.concatenate([qkv[:, :model_width], qkv[:, model_width : 2 * model_width], small], axis=0),
        jnp.concatenate([qkv[:, 2 * model_width :], w_out[0], small], axis=0),
    )
    fc_blocks = w_fc[0].reshape(rows, 4, model_width).transpose(1, 0, 2).reshape(4 * rows, model_width)
    ffn_sets = (fc_blocks, w_proj[0])

    def gathered(sets):
        own = jnp.where(replica == 0, sets[0], sets[1])
        other_layer = swap(own, SECTION)
        layers = []
        for layer in range(2):
            chunk = jnp.where(section == layer, own, other_layer)
            chunks = ring_gather(chunk, count)
            buffer = jnp.zeros((2, count) + chunk.shape, LOW)
            for offset in range(count):
                twin = swap(chunks[offset], REPLICA)
                at = owner(offset)
                buffer = lax.dynamic_update_slice(buffer, chunks[offset][None, None], (replica, at, 0, 0))
                buffer = lax.dynamic_update_slice(buffer, twin[None, None], (1 - replica, at, 0, 0))
            layers.append(buffer)
        return layers

    attn = gathered(attn_sets)
    ffn = gathered(ffn_sets)

    def block(buffer, which, at):
        return buffer[which, :, at * rows : (at + 1) * rows].reshape(count * rows, model_width)

    def unpacked(layer):
        a, f = attn[layer], ffn[layer]
        vec = a[0, :, 2 * rows :].reshape(count, -1)[:, : 12 * rows].reshape(count, 12, rows).astype(F32)

        def row(i):
            return vec[:, i].reshape(-1)

        return Bag(
            q=block(a, 0, 0), k=block(a, 0, 1), v=block(a, 1, 0), o=block(a, 1, 1),
            fc=jnp.concatenate([block(f, 0, i) for i in range(4)], axis=1),
            proj=f[1].reshape(count * 4 * rows, model_width),
            gains=(row(0), row(1)), offsets=(row(2), row(3)), q_bias=row(4), v_bias=row(5),
            out_bias=row(6), fc_bias=vec[:, 7:11].reshape(-1), proj_bias=row(11),
        )

    weights = [unpacked(0), unpacked(1)]
    outputs, states = [], []
    for layer in range(2):
        output, saved = layer_forward(current, weights[layer], plan, place)
        outputs.append(output.astype(LOW))
        states.append(saved)
        current = outputs[-1].astype(F32)
    grad_inputs, totals = [None, None], [None, None]
    arriving = upstream.astype(F32)

    def pieces(attn_rows, layer_grads, which):
        pass

    def blocks_of(grad, cols):
        return grad.astype(LOW).reshape(count, -1, cols)

    def scattered(sets):
        own = jnp.where(replica == 0, sets[0], sets[1])
        other = jnp.where(replica == 0, sets[1], sets[0])
        paired = add_low(own, swap(other, REPLICA))
        return ring_scatter(
            lambda k: lax.dynamic_index_in_dim(paired, owner(k), 0, keepdims=False),
            paired.shape[1], count,
        )

    scattered_attn, scattered_ffn = [None, None], [None, None]
    for layer in (1, 0):
        grad_input, grads = layer_backward(arriving, states[layer], weights[layer], plan, place)
        grad_inputs[layer] = grad_input
        arriving = grad_input.astype(LOW).astype(F32)
        vec = jnp.concatenate(
            [
                grads.gains, grads.offsets, grads.qv_bias, grads.out_bias[None],
            ], axis=0,
        ).reshape(7, count, rows).transpose(1, 0, 2)
        vec = jnp.concatenate(
            [vec, grads.fc_bias.reshape(count, 4, rows), grads.proj_bias.reshape(count, 1, rows)],
            axis=1,
        ).astype(LOW).reshape(count, 12 * rows)
        vec = jnp.concatenate(
            [vec, jnp.zeros((count, small_rows * model_width - 12 * rows), LOW)], axis=1
        ).reshape(count, small_rows, model_width)
        scattered_ffn[layer] = scattered(
            (
                jnp.concatenate(
                    [blocks_of(grads.fc[:, i * model_width : (i + 1) * model_width], model_width) for i in range(4)],
                    axis=1,
                ),
                blocks_of(grads.proj, model_width),
            )
        )
        scattered_attn[layer] = scattered(
            (
                jnp.concatenate([blocks_of(grads.q, model_width), blocks_of(grads.k, model_width), vec], axis=1),
                jnp.concatenate([blocks_of(grads.v, model_width), blocks_of(grads.o, model_width), vec], axis=1),
            )
        )

    def finished(parts):
        own = jnp.where(section == 0, parts[0], parts[1])
        other = jnp.where(section == 0, parts[1], parts[0]).astype(LOW)
        total = (own + swap(other, SECTION).astype(F32)).astype(LOW)
        twin = swap(total, REPLICA)
        return (
            jnp.where(replica == 0, total, twin).astype(F32),
            jnp.where(replica == 0, twin, total).astype(F32),
        )

    ffn_total = finished(scattered_ffn)
    attn_total = finished(scattered_attn)
    fc_grad = ffn_total[0].reshape(4, rows, model_width).transpose(1, 0, 2).reshape(rows, 4 * model_width)
    proj_grad = ffn_total[1]
    qkv_grad = jnp.concatenate(
        [attn_total[0][:rows], attn_total[0][rows : 2 * rows], attn_total[1][:rows]], axis=1
    )
    out_grad = attn_total[1][rows : 2 * rows]
    vec = attn_total[0][2 * rows :].reshape(-1)[: 12 * rows].reshape(12, rows)

    def by_owner(per_layer):
        low = [reshard(v.astype(LOW)) for v in per_layer]
        own = jnp.where(section == 0, low[0], low[1])
        other = jnp.where(section == 0, low[1], low[0])
        got = swap(other, SECTION)
        return jnp.stack([jnp.where(section == 0, own, got), jnp.where(section == 0, got, own)])[None]

    acts = by_owner(outputs)
    in_grads = by_owner(grad_inputs).astype(F32)
    return (
        acts,
        in_grads,
        vec[0:2][None],
        vec[2:4][None],
        qkv_grad[None],
        vec[4:6][None],
        out_grad[None],
        vec[6][None],
        fc_grad[None],
        vec[7:11].reshape(1, 4 * rows),
        proj_grad[None],
        vec[11][None],
    )


ANY = pl.BlockSpec(memory_space=pl.ANY)
VMEM = pl.BlockSpec(memory_space=pltpu.VMEM)
SMEM = pl.BlockSpec(memory_space=pltpu.SMEM)
PAIR = 2 * HEAD
VMEM_LIMIT = 60 * 2**20
MEMORY_RATE = 3.69e6


def mm(a, b):
    return lax.dot_general(a, b, (((1,), (0,)), ((), ())), preferred_element_type=F32)


def mm_nt(a, b):
    return lax.dot_general(a, b, (((1,), (1,)), ((), ())), preferred_element_type=F32)


def mm_tn(a, b):
    return lax.dot_general(a, b, (((0,), (0,)), ((), ())), preferred_element_type=F32)


def call(body, micros, operands, specs, outs, scratch, saves=(), keep=True):
    outs = list(outs) + (list(saves) if keep else [])
    spare = [] if keep else [pltpu.VMEM(shape, kind) for shape, kind, _ in saves]
    return pl.pallas_call(
        body,
        in_specs=specs,
        out_specs=[VMEM if space is None else ANY for _, _, space in outs],
        out_shape=[jax.ShapeDtypeStruct(shape, kind) for shape, kind, _ in outs],
        scratch_shapes=spare + scratch,
        compiler_params=pltpu.CompilerParams(vmem_limit_bytes=VMEM_LIMIT),
        cost_estimate=pl.CostEstimate(
            flops=0, bytes_accessed=int(micros * MEMORY_RATE), transcendentals=0
        ),
    )(*operands)


SEATS = 4


def low_lanes(shape):
    return lax.broadcasted_iota(jnp.int32, shape, len(shape) - 1) % PAIR < HEAD


def turn(tile):
    return pltpu.roll(tile, HEAD, 1)


def tiles_of(values, seat):
    at = 3 * seat // 2
    pair, single = (at, at + 1) if seat % 2 == 0 else (at + 1, at)
    return [values[:, t * PAIR : (t + 1) * PAIR] for t in (pair, single)]


def join(first, second, seat):
    low = low_lanes(first.shape)
    if seat % 2 == 0:
        return jnp.where(low, first, turn(second))
    return jnp.where(low, turn(first), second)


def fold(tile, seat):
    half = tile.shape[0] // 2
    return join(tile[:half], tile[half:], seat)


def split(tile, seat):
    low = low_lanes(tile.shape)
    turned = turn(tile)
    if seat % 2 == 0:
        return jnp.where(low, tile, 0.0), jnp.where(low, turned, 0.0)
    return jnp.where(low, 0.0, turned), jnp.where(low, 0.0, tile)


def unfold(tile, seat):
    return jnp.concatenate(split(tile, seat), axis=0)


def whole_rows(pairs, singles):
    tiles = []
    for even in range(0, SEATS, 2):
        tiles += [pairs[even], singles[even] + singles[even + 1], pairs[even + 1]]
    return jnp.concatenate(tiles, axis=1)


def start_all(copies):
    for copy in copies:
        copy.start()
    return copies


def wait_all(copies):
    for copy in copies:
        copy.wait()


def to_seats(scratch, outs, idx, count, sems):
    return start_all(
        [
            pltpu.make_async_copy(scratch.at[idx[count + 2 + k]], outs[k], sems.at[k])
            for k in range(SEATS)
        ]
    )


def from_seats(ins, scratch, idx, count, sems):
    return start_all(
        [
            pltpu.make_async_copy(ins[k], scratch.at[idx[count + 2 + k]], sems.at[k])
            for k in range(SEATS)
        ]
    )


def in_order(refs, scratch, at, sems, outward):
    copies = []
    for k in range(SEATS):
        for p in range(2):
            ends = refs[k].at[p], scratch.at[at[2 * k + p]]
            if outward:
                ends = ends[::-1]
            copies.append(pltpu.make_async_copy(*ends, sems.at[2 * k + p]))
    return start_all(copies)


def block_rows(segment):
    return 4 * segment + segment // 2


class Loader:
    def __init__(self, sems):
        self.sems = sems
        self.used = 0
        self.waits = {}

    def load(self, idx, count, own, twin, targets):
        slots = {}
        for which in (0, 1):
            for at, (offset, rows, ref, key) in enumerate(targets[which]):
                for k in range(count):
                    slots[which, at, k] = self.used
                    self.waits.setdefault(key, []).append((ref, self.used))
                    self.used += 1
        for rep in (0, 1):
            @pl.when(idx[count] == rep)
            def _():
                for which in (0, 1):
                    chunks = own if which == rep else twin
                    for at, (offset, rows, ref, key) in enumerate(targets[which]):
                        for k in range(count):
                            if len(chunks) == 1:
                                chunk, place = chunks[0].at[k], k
                            else:
                                chunk, place = chunks[k], idx[k]
                            pltpu.make_async_copy(
                                chunk.at[pl.ds(offset, rows)], ref.at[place],
                                self.sems.at[slots[which, at, k]],
                            ).start()

    def wait(self, key):
        for ref, slot in self.waits[key]:
            pltpu.make_async_copy(ref.at[0], ref.at[0], self.sems.at[slot]).wait()


def flat(ref):
    return ref[...].reshape(-1, ref.shape[-1])


def centre(values):
    average = jnp.mean(values, axis=-1, keepdims=True)
    centred = values - average
    scale = lax.rsqrt(jnp.mean(centred * centred, axis=-1, keepdims=True) + EPSILON)
    return centred * scale, scale


def centre_back(grad, hat, scale):
    return scale * (
        grad
        - jnp.mean(grad, axis=-1, keepdims=True)
        - hat * jnp.mean(grad * hat, axis=-1, keepdims=True)
    )


GELU_A, GELU_B = math.sqrt(2 / math.pi), 0.044715


NOTE = 16


def note_rows(small, width):
    rows = small.shape[1]
    hidden = jnp.pad(small[7:11].reshape(1, 4 * rows), ((0, 0), (0, width - 4 * rows)))
    others = jnp.concatenate([small[:7], small[11:]], axis=0)
    others = jnp.pad(others, ((0, NOTE - 9), (0, width - rows)))
    return jnp.concatenate([others, hidden], axis=0)


def read_notes(notes, count, width):
    rows = width // count
    total = None
    hidden = []
    for s in range(count):
        note = notes[s].astype(F32)
        moved = pltpu.roll(note, s * rows, 1) if s else note
        total = moved if total is None else total + moved
        at = (4 * rows * s) % width
        hidden.append(pltpu.roll(note[8:], at, 1)[NOTE - 9 :] if at else note[8:][NOTE - 9 :])
    per = width // (4 * rows)
    lines = [sum(hidden[b * per + i] for i in range(per)) for b in range(4)]
    return [total[:8]] + lines


def project_kernel(count, segment, inputs, hopped, attn, idx, keep):
    width = inputs[0].shape[1]
    rows = width // count
    given = [] if hopped is None else [hopped]
    tall = block_rows(segment)

    def body(idx, first, second, *rest):
        arrived, rest = rest[: len(given)], rest[len(given) :]
        chunks, rest = rest[: 2 * count], rest[2 * count :]
        outs, rest = rest[:SEATS], rest[SEATS:]
        vec, chosen, normed, blocks, wq, wk, wv, notes, sems, out_sems = rest
        loader = Loader(sems)
        loader.load(
            idx, count, chunks[:count], chunks[count:],
            [
                [(0, rows, wq, 0), (rows, rows, wk, 1), (2 * rows, NOTE, notes, 3)],
                [(0, rows, wv, 2)],
            ],
        )
        values = jnp.concatenate([first[:segment], second[:segment]], axis=0).astype(F32)
        if given:
            values = jnp.where(idx[count + 1] == 0, values, arrived[0][...].astype(F32))
        chosen[...] = values.astype(LOW)
        hat, _ = centre(values)
        loader.wait(3)
        lines = read_notes([notes[s] for s in range(count)], count, width)
        vec[0:8] = lines[0]
        for b in range(4):
            vec[8 + b : 9 + b] = lines[1 + b]
        low = (hat * vec[0:1] + vec[2:3]).astype(LOW)
        normed[...] = low
        loader.wait(0)
        queries = mm(low, flat(wq)) + vec[4:5]
        loader.wait(1)
        keys = mm(low, flat(wk))
        loader.wait(2)
        values = mm(low, flat(wv)) + vec[5:6]
        for d in range(SEATS):
            (qp, qs), (kp, ks), (vp, vs) = [tiles_of(x, d) for x in (queries, keys, values)]
            both = join(qs, ks, d)
            for p in range(2):
                span = slice(p * segment, (p + 1) * segment)
                for at, tile in enumerate((qp, kp, vp, both)):
                    blocks[d, p, at * segment : (at + 1) * segment] = tile[span].astype(LOW)
                blocks[d, p, 4 * segment :] = fold(vs[span], d).astype(LOW)
        wait_all(to_seats(blocks, outs, idx, count, out_sems))

    weight = pltpu.VMEM((count, rows, width), LOW)
    return call(
        body, 7, [idx, *inputs, *given, *attn[0], *attn[1]],
        [SMEM, VMEM, VMEM] + [VMEM] * len(given) + [ANY] * (2 * count),
        [((2, tall, PAIR), LOW, True)] * SEATS
        + [((12, width), F32, None), ((2 * segment, width), LOW, None)],
        [
            pltpu.VMEM((SEATS, 2, tall, PAIR), LOW), weight, weight, weight,
            pltpu.VMEM((count, NOTE, width), LOW), pltpu.SemaphoreType.DMA((4 * count,)),
            pltpu.SemaphoreType.DMA((SEATS,)),
        ],
        [((2 * segment, width), LOW, None)], keep,
    )


def read_heads(blocks, segment):
    def joined(at):
        return jnp.concatenate(
            [blocks[i, at * segment : (at + 1) * segment] for i in range(blocks.shape[0])], axis=0
        )

    third = joined(3).astype(F32)
    low = low_lanes(third.shape)
    values = [unfold(blocks[i, 4 * segment :].astype(F32), 0) for i in range(blocks.shape[0])]
    return (
        (joined(0), joined(1), joined(2)),
        (
            jnp.where(low, third, 0.0).astype(LOW), turn(third).astype(LOW),
            jnp.concatenate(values, axis=0).astype(LOW),
        ),
    )


def stacked(rows):
    low = low_lanes(rows.shape)
    zero = jnp.zeros_like(rows)
    return jnp.concatenate([jnp.where(low, rows, zero), jnp.where(low, zero, rows)], axis=0)


def unstacked(rows):
    half = rows.shape[0] // 2
    return jnp.where(low_lanes((half, PAIR)), rows[:half], rows[half:])


def earlier(rows, step):
    row = lax.broadcasted_iota(jnp.int32, (rows, step), 0) % step
    return lax.broadcasted_iota(jnp.int32, (rows, step), 1) <= row


def attend_kernel(count, segment, arrived, at, keep):
    length, step = count * segment, 2 * segment
    tall = block_rows(segment)
    short = segment + segment // 2

    def body(at, *rest):
        ins, outs, rest = rest[:SEATS], rest[SEATS : 2 * SEATS], rest[2 * SEATS :]
        attended, total, blocks, backs, sems, out_sems = rest
        wait_all(in_order(ins, blocks, at, sems, False))
        heads = read_heads(blocks, segment)
        for i in range(length // step):
            span = slice(i * step, (i + 1) * step)
            logs = []
            for g, (queries, keys, values) in enumerate(heads):
                query = queries[span] * SCALING
                if g == 0:
                    query = stacked(query)
                mask = earlier(query.shape[0], step)
                near = jnp.where(mask, mm_nt(query, keys[span]), FLOOR)
                highest = jnp.max(near, axis=-1, keepdims=True)
                if i > 0:
                    far = mm_nt(query, keys[: i * step])
                    highest = jnp.maximum(highest, jnp.max(far, axis=-1, keepdims=True))
                    far = jnp.exp(far - highest)
                near = jnp.exp(near - highest)
                denominator = jnp.sum(near, axis=-1, keepdims=True)
                result = mm(near.astype(LOW), values[span])
                if i > 0:
                    denominator += jnp.sum(far, axis=-1, keepdims=True)
                    result += mm(far.astype(LOW), values[: i * step])
                result = result * (1.0 / denominator)
                log = highest + jnp.log(denominator)
                if g == 0:
                    result = unstacked(result)
                    logs += [log[:step], log[step:]]
                else:
                    logs.append(log)
                attended[g, span] = result
                for p in range(2):
                    tile = result[p * segment : (p + 1) * segment]
                    if g == 0:
                        backs[2 * i + p, :segment] = tile.astype(LOW)
                    else:
                        backs[2 * i + p, segment:] = fold(tile, 0).astype(LOW)
            lane = lax.broadcasted_iota(jnp.int32, (step, PAIR), 1)
            total[span] = jnp.where(lane == 0, logs[0], jnp.where(lane == 1, logs[1], logs[2]))
        wait_all(in_order(outs, backs, at, out_sems, True))

    return call(
        body, 9, [at, *arrived], [SMEM] + [ANY] * SEATS,
        [((2, short, PAIR), LOW, True)] * SEATS,
        [
            pltpu.VMEM((count, tall, PAIR), LOW), pltpu.VMEM((count, short, PAIR), LOW),
            pltpu.SemaphoreType.DMA((2 * SEATS,)), pltpu.SemaphoreType.DMA((2 * SEATS,)),
        ],
        [((2, length, PAIR), F32, None), ((length, PAIR), F32, None)], keep,
    )


def attend_back_kernel(count, segment, arrived, grads, attended, total, at, ties):
    length, step = count * segment, 2 * segment
    tall = block_rows(segment)
    short = segment + segment // 2

    def body(at, attended, total, *rest):
        ins, grad_ins, rest = rest[:SEATS], rest[SEATS : 2 * SEATS], rest[2 * SEATS + len(ties) :]
        outs, rest = rest[:SEATS], rest[SEATS:]
        blocks, grads, backs, of_keys, of_values, sems, grad_sems, out_sems = rest
        first = in_order(ins, blocks, at, sems, False)
        second = in_order(grad_ins, grads, at, grad_sems, False)
        wait_all(first)
        heads = read_heads(blocks, segment)
        wait_all(second)
        for i in reversed(range(length // step)):
            span = slice(i * step, (i + 1) * step)
            third = None
            for g, (queries, keys, values) in enumerate(heads):
                query = queries[span] * SCALING
                if g == 0:
                    grad = jnp.concatenate([grads[2 * i + p, :segment] for p in range(2)], axis=0)
                    dots = grad.astype(F32) * attended[0, span]
                    low = low_lanes(dots.shape)
                    dots = jnp.concatenate([jnp.where(low, dots, 0.0), jnp.where(low, 0.0, dots)], axis=0)
                    log = jnp.concatenate([total[span, 0:1], total[span, 1:2]], axis=0)
                    query, grad = stacked(query), stacked(grad)
                else:
                    grad = jnp.concatenate(
                        [unfold(grads[2 * i + p, segment:].astype(F32), 0) for p in range(2)], axis=0
                    )
                    dots = grad * attended[1, span]
                    grad = grad.astype(LOW)
                    log = total[span, 2:3]
                dots = jnp.sum(dots, axis=-1, keepdims=True)
                parts = [(span, True)] + ([(slice(0, i * step), False)] if i > 0 else [])
                of_queries = None
                for keyed, near in parts:
                    weights = jnp.exp(mm_nt(query, keys[keyed]) - log)
                    if near:
                        weights = jnp.where(earlier(query.shape[0], step), weights, 0.0)
                    grad_scores = (weights * (mm_nt(grad, values[keyed]) - dots)).astype(LOW)
                    term = mm(grad_scores, keys[keyed])
                    of_queries = term if of_queries is None else of_queries + term
                    key_term = mm_tn(grad_scores, query)
                    value_term = mm_tn(weights.astype(LOW), grad)
                    if i == length // step - 1:
                        of_keys[g, keyed] = key_term
                        of_values[g, keyed] = value_term
                    else:
                        of_keys[g, keyed] += key_term
                        of_values[g, keyed] += value_term
                of_queries = of_queries * SCALING
                if g == 0:
                    of_queries = unstacked(of_queries)
                    for p in range(2):
                        backs[2 * i + p, :segment] = of_queries[p * segment : (p + 1) * segment].astype(LOW)
                else:
                    third = of_queries
            low = low_lanes((segment, PAIR))
            for p in range(2):
                own = slice(i * step + p * segment, i * step + (p + 1) * segment)
                block = backs.at[2 * i + p]
                block[segment : 2 * segment] = of_keys[0, own].astype(LOW)
                block[2 * segment : 3 * segment] = of_values[0, own].astype(LOW)
                block[3 * segment : 4 * segment] = join(
                    third[p * segment : (p + 1) * segment], of_keys[1, own], 0
                ).astype(LOW)
                block[4 * segment :] = fold(of_values[1, own], 0).astype(LOW)
        wait_all(in_order(outs, backs, at, out_sems, True))

    return call(
        body, 14, [at, attended, total, *arrived, *grads, *ties],
        [SMEM, VMEM, VMEM] + [ANY] * (2 * SEATS + len(ties)),
        [((2, tall, PAIR), LOW, True)] * SEATS,
        [
            pltpu.VMEM((count, tall, PAIR), LOW), pltpu.VMEM((count, short, PAIR), LOW),
            pltpu.VMEM((count, tall, PAIR), LOW), pltpu.VMEM((2, length, PAIR), F32),
            pltpu.VMEM((2, length, PAIR), F32), pltpu.SemaphoreType.DMA((2 * SEATS,)),
            pltpu.SemaphoreType.DMA((2 * SEATS,)), pltpu.SemaphoreType.DMA((2 * SEATS,)),
        ],
    )


def feed_kernel(count, segment, returned, inputs, vec, attn, ffn, idx, keep):
    width = inputs.shape[1]
    rows, tokens = width // count, 2 * segment
    short = segment + segment // 2

    def body(idx, x, vec, *rest):
        back, rest = rest[:SEATS], rest[SEATS:]
        chunks, rest = rest[: 4 * count], rest[4 * count :]
        output, attended, middle, normed, slope, active, blocks, wo, wf, wp, sems, in_sems = rest
        copies = from_seats(back, blocks, idx, count, in_sems)
        loader = Loader(sems)
        loader.load(idx, count, chunks[:count], chunks[count : 2 * count], [[], [(rows, rows, wo, 5)]])
        loader.load(
            idx, count, chunks[2 * count : 3 * count], chunks[3 * count :],
            [[(b * rows, rows, wf.at[b], b) for b in range(4)], [(b * rows, rows, wp.at[:, b], 4) for b in range(4)]],
        )
        wait_all(copies)
        low = read_returned(blocks, segment).astype(LOW)
        attended[...] = low
        loader.wait(5)
        mid = x[...].astype(F32) + mm(low, flat(wo)) + vec[6:7]
        middle[...] = mid
        hat, _ = centre(mid)
        low = (hat * vec[1:2] + vec[3:4]).astype(LOW)
        normed[...] = low
        for b in range(4):
            loader.wait(b)
            span = slice(b * width, (b + 1) * width)
            u = mm(low, flat(wf.at[b])) + vec[8 + b : 9 + b]
            square = u * u
            t = jnp.tanh(u * (GELU_A + GELU_A * GELU_B * square))
            half = 0.5 + 0.5 * t
            active[:, span] = (u * half).astype(LOW)
            if keep:
                slope[:, span] = (
                    half + u * (0.5 - 0.5 * t * t) * (GELU_A + 3.0 * GELU_A * GELU_B * square)
                ).astype(LOW)
        loader.wait(4)
        output[...] = (mid + mm(active[...], flat(wp)) + vec[7:8]).astype(LOW)

    return call(
        body, 10, [idx, inputs, vec, *returned, *attn[0], *attn[1], *ffn[0], *ffn[1]],
        [SMEM, VMEM, VMEM] + [ANY] * (SEATS + 4 * count),
        [((tokens, width), LOW, None)],
        [
            pltpu.VMEM((SEATS, 2, short, PAIR), LOW), pltpu.VMEM((count, rows, width), LOW),
            pltpu.VMEM((4, count, rows, width), LOW), pltpu.VMEM((count, 4, rows, width), LOW),
            pltpu.SemaphoreType.DMA((9 * count,)), pltpu.SemaphoreType.DMA((SEATS,)),
        ],
        [
            ((tokens, width), LOW, None), ((tokens, width), F32, None), ((tokens, width), LOW, None),
            ((tokens, 4 * width), LOW, None), ((tokens, 4 * width), LOW, None),
        ],
        keep,
    )


def read_returned(blocks, segment):
    pairs, singles = [], []
    for d in range(SEATS):
        pairs.append(jnp.concatenate([blocks[d, p, :segment].astype(F32) for p in range(2)], axis=0))
        singles.append(
            jnp.concatenate([unfold(blocks[d, p, segment:].astype(F32), d) for p in range(2)], axis=0)
        )
    return whole_rows(pairs, singles)


def feed_back_kernel(count, segment, grads, hopped, saved, attn, ffn, idx, keep):
    width = grads[0].shape[1]
    rows, tokens = width // count, 2 * segment
    short = segment + segment // 2
    given = [] if hopped is None else [hopped]

    def body(idx, first, second, middle, slope, active, normed, vec, *rest):
        arrived, rest = rest[: len(given)], rest[len(given) :]
        chunks, rest = rest[: 4 * count], rest[4 * count :]
        outs, rest = rest[:SEATS], rest[SEATS:]
        grad_middle, mine, theirs, sums, grad_out, blocks, wo, wf, wp, gh, sems, out_sems = rest
        loader = Loader(sems)
        loader.load(
            idx, count, chunks[2 * count : 3 * count], chunks[3 * count :],
            [[(b * rows, rows, wf.at[b], b) for b in range(4)], [(b * rows, rows, wp.at[:, b], 4) for b in range(4)]],
        )
        loader.load(idx, count, chunks[:count], chunks[count : 2 * count], [[], [(rows, rows, wo, 5)]])
        branch = jnp.concatenate([first[...], second[...]], axis=0).astype(F32)
        if given:
            branch = jnp.where(idx[count + 1] == 1, branch, arrived[0][...].astype(F32))
        wide, branch = branch, branch.astype(LOW)
        loader.wait(4)
        weight = flat(wp)
        back = jnp.zeros((tokens, width), F32)
        for b in range(4):
            span = slice(b * width, (b + 1) * width)
            ga = mm_nt(branch, weight[span])
            low = (ga * slope[:, span].astype(F32)).astype(LOW)
            gh[:, span] = low
            if keep:
                sums[3 + b : 4 + b] = jnp.sum(low.astype(F32), axis=0, keepdims=True)
            loader.wait(b)
            back += mm_nt(low, flat(wf.at[b]))
        hat, scale = centre(middle[...])
        total = wide + centre_back(back * vec[1:2], hat, scale)
        grad_middle[...] = total
        low = total.astype(LOW)
        grad_out[...] = low
        loader.wait(5)
        values = mm_nt(low, flat(wo))
        for d in range(SEATS):
            pair, single = tiles_of(values, d)
            for p in range(2):
                part = slice(p * segment, (p + 1) * segment)
                blocks[d, p, :segment] = pair[part].astype(LOW)
                blocks[d, p, segment:] = fold(single[part], d).astype(LOW)
        copies = to_seats(blocks, outs, idx, count, out_sems)
        if keep:
            sums[0:1] = jnp.sum(back * hat, axis=0, keepdims=True)
            sums[1:2] = jnp.sum(back, axis=0, keepdims=True)
            sums[2:3] = jnp.sum(low.astype(F32), axis=0, keepdims=True)
            sums[7:8] = jnp.sum(wide, axis=0, keepdims=True)

            @pl.when(idx[count] == 0)
            def _():
                mine[:, :width] = normed[...]
                mine[:, width:] = gh[...]
                theirs[:, :width] = branch
                theirs[:, width:] = active[...]

            @pl.when(idx[count] == 1)
            def _():
                mine[:, :width] = branch
                mine[:, width:] = active[...]
                theirs[:, :width] = normed[...]
                theirs[:, width:] = gh[...]

        wait_all(copies)

    return call(
        body, 14,
        [
            idx, *grads, saved.middle, saved.slope, saved.active, saved.normed_two, saved.vec,
            *given, *attn[0], *attn[1], *ffn[0], *ffn[1],
        ],
        [SMEM] + [VMEM] * (7 + len(given)) + [ANY] * (4 * count),
        [((2, short, PAIR), LOW, True)] * SEATS + [((tokens, width), F32, None)],
        [
            pltpu.VMEM((SEATS, 2, short, PAIR), LOW), pltpu.VMEM((count, rows, width), LOW),
            pltpu.VMEM((4, count, rows, width), LOW), pltpu.VMEM((count, 4, rows, width), LOW),
            pltpu.VMEM((tokens, 4 * width), LOW), pltpu.SemaphoreType.DMA((9 * count,)),
            pltpu.SemaphoreType.DMA((SEATS,)),
        ],
        [
            ((tokens, 5 * width), LOW, None), ((tokens, 5 * width), LOW, None), ((8, width), F32, None),
            ((tokens, width), LOW, None),
        ],
        keep,
    )


def project_back_kernel(count, segment, returned, grad_middle, grad_out, saved, attn, idx, keep):
    tokens, width = grad_middle.shape
    rows = width // count
    tall = block_rows(segment)
    kept = [grad_out, saved.normed, saved.attended_low] if keep else []

    def body(idx, grad_middle, x, vec, *rest):
        held, rest = rest[: len(kept)], rest[len(kept) :]
        back, rest = rest[:SEATS], rest[SEATS:]
        chunks, rest = rest[: 2 * count], rest[2 * count :]
        grad_low, grad_in, mine, theirs, sums, blocks, wq, wk, wv, sems, in_sems = rest
        copies = from_seats(back, blocks, idx, count, in_sems)
        loader = Loader(sems)
        loader.load(
            idx, count, chunks[:count], chunks[count:],
            [[(0, rows, wq, 0), (rows, rows, wk, 1)], [(0, rows, wv, 2)]],
        )
        hat, scale = centre(x[...].astype(F32))
        wait_all(copies)
        pairs, singles = [[], [], []], [[], [], []]
        for d in range(SEATS):
            for at in range(3):
                pairs[at].append(
                    jnp.concatenate(
                        [blocks[d, p, at * segment : (at + 1) * segment].astype(F32) for p in range(2)], axis=0
                    )
                )
            both = [split(blocks[d, p, 3 * segment : 4 * segment].astype(F32), d) for p in range(2)]
            for at in range(2):
                singles[at].append(jnp.concatenate([b[at] for b in both], axis=0))
            singles[2].append(
                jnp.concatenate([unfold(blocks[d, p, 4 * segment :].astype(F32), d) for p in range(2)], axis=0)
            )
        gq, gk, gv = [whole_rows(a, b).astype(LOW) for a, b in zip(pairs, singles)]
        loader.wait(0)
        total = mm_nt(gq, flat(wq))
        loader.wait(1)
        total += mm_nt(gk, flat(wk))
        loader.wait(2)
        total += mm_nt(gv, flat(wv))
        result = grad_middle[...] + centre_back(total * vec[0:1], hat, scale)
        grad_low[...] = result.astype(LOW)
        if not keep:
            return
        grad_in[...] = result
        sums[0:1] = jnp.sum(total * hat, axis=0, keepdims=True)
        sums[1:2] = jnp.sum(total, axis=0, keepdims=True)
        sums[2:3] = jnp.sum(gq.astype(F32), axis=0, keepdims=True)
        sums[3:4] = jnp.sum(gv.astype(F32), axis=0, keepdims=True)
        sums[4:8] = jnp.zeros((4, width), F32)
        grad_out, normed, attended = held

        def fill(first, second):
            first[:, :width] = normed[...]
            first[:, width : 2 * width] = gq
            first[:, 2 * width : 3 * width] = normed[...]
            first[:, 3 * width :] = gk
            second[:, :width] = normed[...]
            second[:, width : 2 * width] = gv
            second[:, 2 * width : 3 * width] = attended[...]
            second[:, 3 * width :] = grad_out[...]

        @pl.when(idx[count] == 0)
        def _():
            fill(mine, theirs)

        @pl.when(idx[count] == 1)
        def _():
            fill(theirs, mine)

    weight = pltpu.VMEM((count, rows, width), LOW)
    return call(
        body, 8, [idx, grad_middle, saved.inputs, saved.vec, *kept, *returned, *attn[0], *attn[1]],
        [SMEM] + [VMEM] * (3 + len(kept)) + [ANY] * (SEATS + 2 * count),
        [((tokens, width), LOW, None)],
        [
            pltpu.VMEM((SEATS, 2, tall, PAIR), LOW), weight, weight, weight,
            pltpu.SemaphoreType.DMA((3 * count,)), pltpu.SemaphoreType.DMA((SEATS,)),
        ],
        [
            ((tokens, width), F32, None), ((tokens, 4 * width), LOW, None),
            ((tokens, 4 * width), LOW, None), ((8, width), F32, None),
        ],
        keep,
    )


def send_out(scratch, outs, idx, count, blocks, rows, base, sems, start):
    for k in range(count):
        for b in range(blocks):
            if len(outs) == 1:
                piece, place = outs[0].at[k], k
            else:
                piece, place = outs[k], idx[k]
            copy = pltpu.make_async_copy(
                scratch.at[pl.ds(pl.multiple_of(b * base + place * rows, 16), rows)],
                piece.at[pl.ds(b * rows, rows)], sems.at[k * blocks + b],
            )
            copy.start() if start else copy.wait()


def ffn_terms_kernel(count, parts, idx):
    ties = []
    width = parts[0].shape[1] // 5
    rows = width // count

    shape = (4 * rows, width)
    pieces = [(shape, LOW, True)] * count

    def body(idx, *rest):
        given, rest = rest[: len(parts)], rest[len(parts) + len(ties) :]
        outs, (scratch, sems) = rest[: len(pieces)], rest[len(pieces) :]
        narrow = jnp.concatenate([part[:, :width] for part in given], axis=0)

        def wide(b):
            span = slice((1 + b) * width, (2 + b) * width)
            return jnp.concatenate([part[:, span] for part in given], axis=0)

        @pl.when(idx[count] == 0)
        def _():
            for b in range(4):
                scratch[b * width : (b + 1) * width] = mm_tn(narrow, wide(b)).astype(LOW)
            send_out(scratch, outs, idx, count, 4, rows, width, sems, True)
            send_out(scratch, outs, idx, count, 4, rows, width, sems, False)

        @pl.when(idx[count] == 1)
        def _():
            for b in range(4):
                scratch[b * width : (b + 1) * width] = mm_tn(wide(b), narrow).astype(LOW)
            send_out(scratch, outs, idx, count, 1, 4 * rows, 0, sems, True)
            send_out(scratch, outs, idx, count, 1, 4 * rows, 0, sems, False)

    return call(
        body, 8, [idx, *parts, *ties], [SMEM] + [VMEM] * len(parts) + [ANY] * len(ties),
        pieces,
        [pltpu.VMEM((4 * width, width), LOW), pltpu.SemaphoreType.DMA((4 * count,))],
    )


def attn_terms_kernel(count, parts, sums_one, sums_two, idx):
    ties = []
    width = parts[0].shape[1] // 4
    given = len(parts), len(sums_one)
    rows = width // count

    def body(idx, *rest):
        parts, rest = rest[: given[0]], rest[given[0] :]
        one = sum(ref[...] for ref in rest[: given[1]])
        two = sum(ref[...] for ref in rest[given[1] : 2 * given[1]])
        rest = rest[2 * given[1] + len(ties) :]
        outs, (scratch, notes, sems) = rest[:count], rest[count:]

        def both(b):
            span = slice(b * width, (b + 1) * width)
            return jnp.concatenate([part[:, span] for part in parts], axis=0)

        flatly = jnp.concatenate(
            [
                one[0:1], two[0:1], one[1:2], two[1:2], one[2:3], one[3:4], two[2:3], two[7:8],
                jnp.zeros((NOTE - 8, width), F32),
            ],
            axis=0,
        )
        lane = lax.broadcasted_iota(jnp.int32, (NOTE, width), 1)
        line = lax.broadcasted_iota(jnp.int32, (NOTE, width), 0)
        for s in range(count):
            note = pltpu.roll(flatly, width - s * rows, 1) if s else flatly
            start = 4 * rows * s
            hidden = two[3 + start // width : 4 + start // width]
            hidden = pltpu.roll(
                jnp.broadcast_to(hidden, (8, width)), (width - start % width) % width, 1
            )
            hidden = jnp.concatenate([hidden, hidden], axis=0)
            note = jnp.where(
                (line < 8) & (lane < rows), note,
                jnp.where((line == NOTE - 1) & (lane < 4 * rows), hidden, 0.0),
            )
            notes[s] = note.astype(LOW)
        for b in range(2):
            scratch[b * width : (b + 1) * width] = mm_tn(both(2 * b), both(2 * b + 1)).astype(LOW)
        for start in (True, False):
            send_out(scratch, outs, idx, count, 2, rows, width, sems, start)
            for k in range(count):
                copy = pltpu.make_async_copy(
                    notes.at[idx[k]], outs[k].at[pl.ds(2 * rows, NOTE)], sems.at[2 * count + k]
                )
                copy.start() if start else copy.wait()

    return call(
        body, 5, [idx, *parts, *sums_one, *sums_two, *ties],
        [SMEM] + [VMEM] * (given[0] + 2 * given[1]) + [ANY] * len(ties),
        [((2 * rows + NOTE, width), LOW, True)] * count,
        [
            pltpu.VMEM((2 * width, width), LOW), pltpu.VMEM((count, NOTE, width), LOW),
            pltpu.SemaphoreType.DMA((3 * count,)),
        ],
    )


def hold(values, *after):
    return lax.optimization_barrier((values, after))[0] if len(after) else values


class GatherRing:
    def __init__(self, chunk, count, rightward):
        self.right, self.left = ring_pairs(count)
        self.count, self.rightward, self.at = count, rightward, 0
        self.last = (chunk, chunk)
        self.own = {0: chunk}
        self.twin = {0: swap(chunk, REPLICA)}

    def keep(self, k, chunk):
        self.own[k], self.twin[k] = chunk, swap(chunk, REPLICA)

    def step(self, *after):
        self.at += 1
        near, far = hold(self.last, *after)
        if self.at < self.count // 2:
            near = lax.ppermute(near, SHARD, self.right)
            far = lax.ppermute(far, SHARD, self.left)
            self.keep(self.count - self.at, near)
            self.keep(self.at, far)
            self.last = (near, far)
        else:
            if self.rightward:
                last = lax.ppermute(near, SHARD, self.right)
            else:
                last = lax.ppermute(far, SHARD, self.left)
            self.keep(self.at, last)
            self.last = (last,)

    def lists(self):
        return [[side[k] for k in range(self.count)] for side in (self.own, self.twin)]


class ScatterRing:
    def __init__(self, pieces, count, rightward):
        self.right, self.left = ring_pairs(count)
        self.pieces, self.count, self.rightward = pieces, count, rightward
        self.at = count // 2
        self.last = None

    def step(self, *after):
        pieces, half = self.pieces, self.count // 2
        if self.at == half:
            far = hold(pieces[half], *after)
            if self.rightward:
                self.last = (lax.ppermute(far, SHARD, self.right), None)
            else:
                self.last = (None, lax.ppermute(far, SHARD, self.left))
        else:
            sides = []
            for piece, term in zip((pieces[self.at], pieces[self.count - self.at]), self.last):
                sides.append(piece if term is None else add_low(piece, term))
            first, second = hold(tuple(sides), *after)
            self.last = (
                lax.ppermute(first, SHARD, self.right), lax.ppermute(second, SHARD, self.left)
            )
        self.at -= 1

    def total(self):
        return self.pieces[0].astype(F32) + self.last[0].astype(F32) + self.last[1].astype(F32)


def fast_device(
    tokens, cotangent, group_order, norm_gains, norm_biases, w_qkv, qv_bias, w_out, out_bias,
    w_fc, fc_bias, w_proj, proj_bias,
):
    count = lax.axis_size(SHARD)
    section = lax.axis_index(SECTION)
    replica = lax.axis_index(REPLICA)
    shard = lax.axis_index(SHARD)
    segment, width = tokens.shape[1], tokens.shape[2]
    rows = w_qkv.shape[1]
    half = count // 2
    order = ring_order(count)
    position = jnp.asarray(np.argsort(np.array(order)), jnp.int32)[shard]
    around = lax.rem(position + jnp.arange(count, dtype=jnp.int32), count)
    seat = 2 * replica + lax.rem(shard, 2)
    others = seat ^ jnp.arange(SEATS, dtype=jnp.int32)
    idx = jnp.concatenate(
        [jnp.asarray(order, jnp.int32)[around], jnp.stack([replica, section]).astype(jnp.int32), others]
    )

    ways = [
        [
            (r * count + 2 * z + y, (z // 2) * count + 2 * (2 * r + (z + j) % 2) + y)
            for r in range(2) for z in range(half) for y in range(2)
        ]
        for j in range(2)
    ]
    odd = lax.rem(shard // 2, 2)

    def gather_in(x, j, *more):
        own = lax.dynamic_index_in_dim(x, lax.rem(odd + j, 2), 0, keepdims=False)
        own = jnp.concatenate([own, *more], axis=0) if more else own
        return lax.ppermute(own, (REPLICA, SHARD), ways[j])

    def give_back(x):
        parts = [
            lax.ppermute(
                x[j * segment : (j + 1) * segment], (REPLICA, SHARD), [(b, a) for a, b in ways[j]]
            )
            for j in range(2)
        ]
        return jnp.stack([jnp.where(odd == 0, *parts), jnp.where(odd == 0, *parts[::-1])])[None]

    def exchange(parts):
        diagonal = [(r * count + s, (1 - r) * count + (s ^ 1)) for r in range(2) for s in range(count)]
        return [
            parts[0],
            lax.ppermute(parts[1], SHARD, [(s, s ^ 1) for s in range(count)]),
            swap(parts[2], REPLICA),
            lax.ppermute(parts[3], (REPLICA, SHARD), diagonal),
        ]

    small = jnp.concatenate(
        [norm_gains[0], norm_biases[0], qv_bias[0], out_bias, fc_bias.reshape(4, rows), proj_bias],
        axis=0,
    )
    qkv = w_qkv[0]
    attn_own = jnp.concatenate(
        [
            jnp.where(replica == 0, qkv[:, :width], qkv[:, 2 * width :]),
            jnp.where(replica == 0, qkv[:, width : 2 * width], w_out[0]),
            note_rows(small, width),
        ],
        axis=0,
    )
    fc_blocks = jnp.concatenate([w_fc[0][:, b * width : (b + 1) * width] for b in range(4)], axis=0)
    ffn_own = jnp.where(replica == 0, fc_blocks, w_proj[0])

    attn_ring = GatherRing(attn_own, count, True)
    attn_ring.step()
    order_row = lax.dynamic_index_in_dim(group_order, odd, 0).astype(LOW)
    order_rows = jnp.pad(order_row, ((0, NOTE - 1), (0, width - count)))
    packed = [gather_in(tokens, 0, order_rows), gather_in(tokens, 1)]
    blocks_at = packed[0][segment, :count].astype(jnp.int32)
    pair = shard // 2
    slot = lax.rem(pair + jnp.arange(2, dtype=jnp.int32), 2)
    which = (4 * (others // 2) + others % 2)[:, None] + 2 * slot[None, :]
    at = jnp.sum(
        jnp.where(
            which.reshape(-1, 1) == jnp.arange(count, dtype=jnp.int32)[None, :], blocks_at[None, :], 0
        ),
        axis=1,
    )
    attn_ring.step()
    attn_ring.step()
    ffn_ring = GatherRing(hold(ffn_own, attn_ring.last), count, False)
    ffn_ring.step()
    attn_ring.step()
    attn = attn_ring.lists()

    def forward(hopped, keep, before):
        *sent, vec, inputs = project_kernel(count, segment, packed, hopped, attn, idx, keep)[: SEATS + 2 + keep]
        normed = None
        if keep:
            vec, inputs, normed = sent.pop(), vec, inputs
        sent = before[0](sent)
        arrived = exchange(sent)
        back = attend_kernel(count, segment, before[1](arrived), at, keep)
        back, kept = back[:SEATS], back[SEATS:]
        returned = exchange(before[2](back))
        fed = feed_kernel(
            count, segment, before[3](returned), inputs, vec, attn, ffn_ring.lists(), idx, keep
        )
        state = Bag(vec=vec, inputs=inputs, normed=normed, arrived=arrived, output=fed[0])
        if keep:
            state.attended, state.total = kept
            state.attended_low, state.middle, state.normed_two, state.slope, state.active = fed[1:]
        return state

    def ring_sent(sent):
        sent = hold(sent, ffn_ring.last)
        ffn_ring.step(sent[1])
        return sent

    def ring_arrived(arrived):
        return arrived

    def ring_back(back):
        ffn_ring.step(back[0])
        return back

    def ring_returned(returned):
        ffn_ring.step(returned[1])
        return returned

    def same(values):
        return values

    first = forward(None, False, [ring_sent, ring_arrived, ring_back, ring_returned])
    ffn = ffn_ring.lists()

    def hop(values, backward):
        return lax.ppermute(values, SECTION, [(1, 0)] if backward else [(0, 1)])

    upstream = [gather_in(hold(cotangent, first.output), j) for j in range(2)]
    state = forward(
        hop(first.output, False), True, [same, lambda arrived: hold(arrived, upstream), same, same]
    )
    acts = give_back(state.output)

    def backward(hopped, keep, ties, terms, between):
        out = feed_back_kernel(count, segment, upstream, hopped, state, attn, ffn, idx, keep)
        sent, grad_middle, kept = out[:SEATS], out[SEATS], out[SEATS + 1 :]
        arrived = exchange(sent)
        if keep:
            ties = ties + terms(kept)
        back = attend_back_kernel(
            count, segment, state.arrived, arrived, state.attended, state.total, at, ties
        )
        returned = exchange(between[0](back))
        low, *last = project_back_kernel(
            count, segment, between[1](returned), grad_middle, kept[3] if keep else None, state, attn,
            idx, keep,
        )
        return low, kept, last

    early, _, _ = backward(None, False, [acts], None, [same, same])
    rings = []

    def ffn_terms(kept):
        terms = ffn_terms_kernel(count, [kept[0], swap(kept[1], REPLICA)], idx)
        rings.append(ScatterRing(terms, count, False))
        rings[0].step()
        return [terms[0]]

    def ring_step(values):
        rings[0].step(values[1])
        return values

    low, kept, last = backward(hop(early, True), True, [], ffn_terms, [ring_step, ring_step])
    rings[0].step(low)
    terms = attn_terms_kernel(count, [last[1], swap(last[2], REPLICA)], [last[3]], [kept[2]], idx)
    rings.append(ScatterRing(terms, count, True))
    for _ in range(half):
        rings[1].step()
    in_grads = give_back(hold(last[0].astype(LOW), low)).astype(F32)

    def finished(ring):
        total = ring.total().astype(LOW)
        twin = swap(total, REPLICA)
        return (
            jnp.where(replica == 0, total, twin).astype(F32),
            jnp.where(replica == 0, twin, total).astype(F32),
        )

    ffn_total, attn_total = finished(rings[0]), finished(rings[1])
    fc_grad = jnp.concatenate([ffn_total[0][b * rows : (b + 1) * rows] for b in range(4)], axis=1)
    qkv_grad = jnp.concatenate(
        [attn_total[0][:rows], attn_total[0][rows : 2 * rows], attn_total[1][:rows]], axis=1
    )
    note = attn_total[0][2 * rows :] + attn_total[1][2 * rows :]
    vec = note[:8, :rows]
    return (
        acts, in_grads, vec[0:2][None], vec[2:4][None], qkv_grad[None], vec[4:6][None],
        attn_total[1][rows : 2 * rows][None], vec[6][None], fc_grad[None],
        note[NOTE - 1, : 4 * rows][None], ffn_total[1][None], vec[7][None],
    )


def on_each(tokens, *others):
    count = lax.axis_size(SHARD)
    tiles = (tokens.shape[2] // count) % 32 == 0 and tokens.shape[1] % 64 == 0
    seats = count == 2 * SEATS and tokens.shape[0] == 2 and HEADS == 3 * SEATS
    return (fast_device if tiles and seats else on_device)(tokens, *others)


def solution(mesh):
    in_specs = (
        P(REPLICA, SHARD, None),
        P(REPLICA, SHARD, None),
        P(REPLICA, None),
        P(SECTION, None, SHARD),
        P(SECTION, None, SHARD),
        P(SECTION, SHARD, None),
        P(SECTION, None, SHARD),
        P(SECTION, SHARD, None),
        P(SECTION, SHARD),
        P(SECTION, SHARD, None),
        P(SECTION, SHARD),
        P(SECTION, SHARD, None),
        P(SECTION, SHARD),
    )
    out_specs = (
        P(SECTION, REPLICA, SHARD, None),
        P(SECTION, REPLICA, SHARD, None),
        P(SECTION, None, SHARD),
        P(SECTION, None, SHARD),
        P(SECTION, SHARD, None),
        P(SECTION, None, SHARD),
        P(SECTION, SHARD, None),
        P(SECTION, SHARD),
        P(SECTION, SHARD, None),
        P(SECTION, SHARD),
        P(SECTION, SHARD, None),
        P(SECTION, SHARD),
    )
    return jax.shard_map(
        on_each, mesh=mesh, in_specs=in_specs, out_specs=out_specs, check_vma=False
    )
```

```python
import math
from types import SimpleNamespace as Bag

import jax
import jax.numpy as jnp
import numpy as np
from jax import lax
from jax.experimental import pallas as pl
from jax.experimental.pallas import tpu as pltpu
from jax.sharding import PartitionSpec as P

HEADS = 12
HEAD = 64
EPSILON = 1e-05
SCALING = 0.125
FLOOR = -1e30
SECTION, REPLICA, SHARD = "section", "replica", "shard"
LOW = jnp.bfloat16
F32 = jnp.float32


def ring_order(count):
    return list(range(0, count, 2)) + list(range(count - 1, 0, -2))


def ring_pairs(count):
    order = ring_order(count)
    right = [(order[i], order[(i + 1) % count]) for i in range(count)]
    return right, [(b, a) for a, b in right]


def ring_gather(chunk, count):
    right, left = ring_pairs(count)
    got = {0: chunk}
    from_left = from_right = chunk
    cut = chunk.shape[0] // 32 * 16
    for step in range(1, count // 2 + 1):
        if step == count // 2:
            got[step] = jnp.concatenate(
                [
                    lax.ppermute(from_left[:cut], SHARD, right),
                    lax.ppermute(from_right[cut:], SHARD, left),
                ],
                axis=0,
            )
        else:
            from_left = lax.ppermute(from_left, SHARD, right)
            from_right = lax.ppermute(from_right, SHARD, left)
            got[count - step] = from_left
            got[step] = from_right
    return [got[k] for k in range(count)]


def ring_scatter(piece, rows, count):
    right, left = ring_pairs(count)
    cut = rows // 32 * 16
    half = count // 2
    far = piece(half)
    to_right = lax.ppermute(far[:cut], SHARD, right)
    to_left = lax.ppermute(far[cut:], SHARD, left)
    for distance in range(half - 1, 0, -1):
        first, second = piece(distance), piece(count - distance)
        if distance == half - 1:
            first = jnp.concatenate([add_low(first[:cut], to_right), first[cut:]], axis=0)
            second = jnp.concatenate([second[:cut], add_low(second[cut:], to_left)], axis=0)
        else:
            first = add_low(first, to_right)
            second = add_low(second, to_left)
        to_right = lax.ppermute(first, SHARD, right)
        to_left = lax.ppermute(second, SHARD, left)
    return piece(0).astype(F32) + to_right.astype(F32) + to_left.astype(F32)


def add_low(a, b):
    return (a.astype(F32) + b.astype(F32)).astype(LOW)


def swap(x, axis):
    return lax.ppermute(x, axis, [(0, 1), (1, 0)])


def normalize(values, gain_row, offset):
    average = jnp.mean(values, axis=-1, keepdims=True)
    centred = values - average
    variance = jnp.mean(centred * centred, axis=-1, keepdims=True)
    return centred * lax.rsqrt(variance + EPSILON) * gain_row + offset


def gelu_tanh(values):
    return jax.nn.gelu(values, approximate=True)


def dot(a, b):
    return jnp.dot(a, b, preferred_element_type=F32)


def dot_t(a, b):
    return lax.dot_general(a, b, (((1,), (1,)), ((), ())), preferred_element_type=F32)


def dot_rows(a, b):
    return lax.dot_general(a, b, (((0,), (0,)), ((), ())), preferred_element_type=F32)


class Plan:
    def __init__(self, count, segment):
        self.count = count
        self.segment = segment
        self.splits = count // math.gcd(HEADS, count)
        self.units = HEADS * self.splits // count
        self.part = segment // self.splits
        self.first = [self.units * q // self.splits for q in range(count)]
        self.slots = max(
            (self.units * q + self.units - 1) // self.splits - self.first[q] + 1
            for q in range(count)
        )
        self.groups = [
            [r * count + h * (count // 2) + i for r in range(2) for i in range(count // 2)]
            for h in range(2)
        ]

    def exchange(self, blocks):
        return lax.all_to_all(
            blocks, (REPLICA, SHARD), 0, 0, tiled=True, axis_index_groups=self.groups
        )

    def pack_units(self, heads):
        parts = heads.reshape(self.splits, self.part, HEADS, HEAD)
        parts = parts.transpose(2, 0, 1, 3).reshape(
            self.count, self.units * self.part, HEAD
        )
        return self.fold(parts)

    def fold(self, parts):
        rows = parts.shape[1] // 2
        return jnp.concatenate([parts[:, :rows], parts[:, rows:]], axis=2)

    def unfold(self, folded):
        return jnp.concatenate([folded[..., :HEAD], folded[..., HEAD:]], axis=1)

    def unpack_units(self, folded):
        parts = self.unfold(folded).reshape(HEADS, self.splits, self.part, HEAD)
        return parts.transpose(1, 2, 0, 3).reshape(self.segment, HEADS * HEAD)

    def gather_units(self, folded):
        parts = self.unfold(folded).reshape(self.count, self.units, self.part, HEAD)
        return parts.transpose(1, 0, 2, 3).reshape(self.units, self.count * self.part, HEAD)

    def scatter_units(self, values):
        parts = values.reshape(self.units, self.count, self.part, HEAD).transpose(1, 0, 2, 3)
        return self.fold(parts.reshape(self.count, self.units * self.part, HEAD))

    def head_slots(self, rows):
        blocks = []
        for q in range(self.count):
            cols = []
            for slot in range(self.slots):
                head = min(self.first[q] + slot, HEADS - 1)
                cols.append(rows[:, head * HEAD : (head + 1) * HEAD])
            blocks.append(jnp.concatenate(cols, axis=1))
        return jnp.stack(blocks)

    def sum_slots(self, blocks):
        cols = []
        for head in range(HEADS):
            total = None
            for q in range(self.count):
                last = (self.units * (q + 1) - 1) // self.splits
                if self.first[q] <= head <= last:
                    slot = head - self.first[q]
                    term = blocks[q, :, slot * HEAD : (slot + 1) * HEAD].astype(F32)
                    total = term if total is None else total + term
            cols.append(total)
        return jnp.concatenate(cols, axis=1)


def over(a, b, dim_a, dim_b):
    return lax.dot_general(a, b, (((dim_a,), (dim_b,)), ((), ())), preferred_element_type=F32)


def over_units(a, b):
    return lax.dot_general(a, b, (((0, 1), (0, 1)), ((), ())), preferred_element_type=F32)


def widen(units, slot, slots):
    wide = jnp.concatenate([units] * slots, axis=2)
    lane_slot = jnp.arange(slots * HEAD, dtype=jnp.int32) // HEAD
    return jnp.where(lane_slot[None, None, :] == slot[:, None, None], wide, jnp.zeros_like(wide))


def narrow(wide, slot, slots):
    lane_slot = jnp.arange(slots * HEAD, dtype=jnp.int32) // HEAD
    wide = jnp.where(lane_slot[None, None, :] == slot[:, None, None], wide, jnp.zeros_like(wide))
    return sum(wide[:, :, s * HEAD : (s + 1) * HEAD] for s in range(slots))


def attend_forward(queries, keys, values, query_pos, key_pos):
    scores = over(queries, keys, 2, 1) * SCALING
    visible = key_pos[None, None, :] <= query_pos[:, :, None]
    scores = jnp.where(visible, scores, FLOOR)
    highest = jnp.max(scores, axis=-1, keepdims=True)
    terms = jnp.exp(scores - highest)
    total = jnp.sum(terms, axis=-1, keepdims=True)
    weights = (terms / total).astype(LOW)
    attended = over(weights, values, 2, 0)
    return attended, highest + jnp.log(total)


def attend_backward(queries, keys, values, query_pos, key_pos, log_total, grad, row_dots):
    scores = over(queries, keys, 2, 1) * SCALING
    visible = key_pos[None, None, :] <= query_pos[:, :, None]
    weights = jnp.where(visible, jnp.exp(scores - log_total), 0.0)
    grad_weights = over(grad, values, 2, 1)
    grad_scores = (weights * (grad_weights - row_dots)).astype(LOW)
    grad_queries = (
        over(grad_scores, keys, 2, 0) * SCALING
    )
    grad_keys = (
        over_units(grad_scores, queries) * SCALING
    )
    grad_values = over_units(weights.astype(LOW), grad)
    return grad_queries, grad_keys, grad_values


def layer_forward(inputs, weights, plan, place):
    normed = normalize(inputs, weights.gains[0], weights.offsets[0]).astype(LOW)
    queries = (dot(normed, weights.q) + weights.q_bias).astype(LOW)
    keys = dot(normed, weights.k).astype(LOW)
    values = (dot(normed, weights.v) + weights.v_bias).astype(LOW)
    segment = inputs.shape[0]
    width = plan.slots * HEAD
    sent = jnp.concatenate(
        [
            plan.head_slots(keys),
            plan.head_slots(values),
            plan.pack_units(queries.reshape(segment, HEADS, HEAD)).reshape(
                plan.count, -1, width
            ),
        ],
        axis=1,
    )
    arrived = plan.exchange(sent)
    length = plan.count * segment
    all_keys = arrived[:, :segment].reshape(length, width)
    all_values = arrived[:, segment : 2 * segment].reshape(length, width)
    units = plan.gather_units(arrived[:, 2 * segment :].reshape(plan.count, -1, 2 * HEAD))
    units = widen(units, place.slot, plan.slots)
    attended, log_total = attend_forward(
        units, all_keys, all_values, place.query_pos, place.key_pos
    )
    attended = narrow(attended, place.slot, plan.slots)
    returned = plan.exchange(plan.scatter_units(attended.astype(LOW)))
    attended_low = plan.unpack_units(returned)
    middle = inputs + dot(attended_low, weights.o) + weights.out_bias
    normed_two = normalize(middle, weights.gains[1], weights.offsets[1]).astype(LOW)
    hidden = dot(normed_two, weights.fc) + weights.fc_bias
    active = gelu_tanh(hidden).astype(LOW)
    output = middle + dot(active, weights.proj) + weights.proj_bias
    saved = Bag(
        inputs=inputs, normed=normed, units=units, keys=all_keys, values=all_values,
        attended=attended, log_total=log_total, attended_low=attended_low, middle=middle,
        normed_two=normed_two, hidden=hidden, active=active,
    )
    return output, saved


def layer_backward(arriving, saved, weights, plan, place):
    segment, model_width = arriving.shape
    grad_branch = arriving.astype(LOW)
    grad_active = dot_t(grad_branch, weights.proj)
    grad_hidden = jax.vjp(gelu_tanh, saved.hidden)[1](grad_active)[0].astype(LOW)
    grad_normed_two = dot_t(grad_hidden, weights.fc)
    grad_middle_norm, gain_two, offset_two = jax.vjp(
        normalize, saved.middle, weights.gains[1], weights.offsets[1]
    )[1](grad_normed_two)
    grads = Bag(
        proj=dot_rows(saved.active, grad_branch),
        proj_bias=jnp.sum(grad_branch.astype(F32), axis=0),
        fc=dot_rows(saved.normed_two, grad_hidden),
        fc_bias=jnp.sum(grad_hidden.astype(F32), axis=0),
    )
    grad_middle = arriving + grad_middle_norm
    grad_out = grad_middle.astype(LOW)
    grad_attended = dot_t(grad_out, weights.o).astype(LOW)
    arrived = plan.exchange(plan.pack_units(grad_attended.reshape(segment, HEADS, HEAD)))
    grad_units = plan.gather_units(arrived)
    row_dots = jnp.sum(grad_units.astype(F32) * saved.attended, axis=-1, keepdims=True)
    grad_queries, grad_keys, grad_values = attend_backward(
        saved.units, saved.keys, saved.values, place.query_pos, place.key_pos,
        saved.log_total, widen(grad_units, place.slot, plan.slots), row_dots,
    )
    grad_queries = narrow(grad_queries, place.slot, plan.slots).astype(LOW)
    width = plan.slots * HEAD
    sent = jnp.concatenate(
        [
            grad_keys.astype(LOW).reshape(plan.count, segment, width),
            grad_values.astype(LOW).reshape(plan.count, segment, width),
            plan.scatter_units(grad_queries).reshape(plan.count, -1, width),
        ],
        axis=1,
    )
    returned = plan.exchange(sent)
    grad_k = plan.sum_slots(returned[:, :segment]).astype(LOW)
    grad_v = plan.sum_slots(returned[:, segment : 2 * segment]).astype(LOW)
    grad_q = plan.unpack_units(returned[:, 2 * segment :].reshape(plan.count, -1, 2 * HEAD))
    grad_normed = (
        dot_t(grad_q, weights.q) + dot_t(grad_k, weights.k) + dot_t(grad_v, weights.v)
    )
    grad_input_norm, gain_one, offset_one = jax.vjp(
        normalize, saved.inputs, weights.gains[0], weights.offsets[0]
    )[1](grad_normed)
    grads = Bag(
        proj=grads.proj, proj_bias=grads.proj_bias, fc=grads.fc, fc_bias=grads.fc_bias,
        gains=jnp.stack([gain_one, gain_two]),
        offsets=jnp.stack([offset_one, offset_two]),
        q=dot_rows(saved.normed, grad_q),
        k=dot_rows(saved.normed, grad_k),
        v=dot_rows(saved.normed, grad_v),
        qv_bias=jnp.stack([jnp.sum(grad_q.astype(F32), axis=0), jnp.sum(grad_v.astype(F32), axis=0)]),
        o=dot_rows(saved.attended_low, grad_out),
        out_bias=jnp.sum(grad_out.astype(F32), axis=0),
    )
    return grad_middle + grad_input_norm, grads


def on_device(
    tokens, cotangent, group_order, norm_gains, norm_biases, w_qkv, qv_bias, w_out, out_bias,
    w_fc, fc_bias, w_proj, proj_bias,
):
    count = lax.axis_size(SHARD)
    section = lax.axis_index(SECTION)
    replica = lax.axis_index(REPLICA)
    shard = lax.axis_index(SHARD)
    segment, model_width = tokens.shape[1], tokens.shape[2]
    rows = w_qkv.shape[1]
    half = count // 2
    plan = Plan(count, segment)
    order = ring_order(count)
    position_of = np.argsort(np.array(order))
    position = jnp.asarray(position_of, jnp.int32)[shard]
    order_table = jnp.asarray(order, jnp.int32)

    def owner(offset):
        return order_table[lax.rem(position + offset, count)]

    home = shard // half
    keeps = home == replica
    crossing = []
    for s in range(half):
        crossing += [(count + s, s + half), (s + half, count + s)]

    def reshard(x):
        moved = lax.ppermute(x, (REPLICA, SHARD), crossing)
        return jnp.where(keeps, x, moved)

    def pick(x):
        return lax.dynamic_index_in_dim(x, section, 0, keepdims=False)

    order_row = pick(group_order).astype(LOW)
    order_row = jnp.broadcast_to(
        jnp.concatenate([order_row, jnp.zeros((model_width - count,), LOW)])[None], (16, model_width)
    )
    packed = reshard(jnp.concatenate([pick(tokens), order_row], axis=0))
    current = packed[:segment].astype(F32)
    blocks_at = packed[segment, :count].astype(jnp.int32)
    upstream = reshard(pick(cotangent))
    seat = replica * half + lax.rem(shard, half)
    key_pos = (
        blocks_at[:, None] * segment + jnp.arange(segment, dtype=jnp.int32)[None, :]
    )
    unit_ids = plan.units * seat + jnp.arange(plan.units, dtype=jnp.int32)
    unit_part = lax.rem(unit_ids, plan.splits)
    parts_pos = key_pos.reshape(count, plan.splits, plan.part)
    query_pos = jnp.stack(
        [
            lax.dynamic_index_in_dim(parts_pos, unit_part[u], 1, keepdims=False).reshape(-1)
            for u in range(plan.units)
        ]
    )
    place = Bag(
        slot=unit_ids // plan.splits - (plan.units * seat) // plan.splits,
        query_pos=query_pos,
        key_pos=key_pos.reshape(-1),
    )

    small = jnp.concatenate(
        [
            norm_gains[0], norm_biases[0], qv_bias[0], out_bias, fc_bias.reshape(4, rows), proj_bias,
        ],
        axis=0,
    ).reshape(-1)
    small_rows = -(-small.shape[0] // (16 * model_width)) * 16
    small = jnp.concatenate(
        [small, jnp.zeros((small_rows * model_width - small.shape[0],), LOW)]
    ).reshape(small_rows, model_width)
    qkv = w_qkv[0]
    attn_sets = (
        jnp.concatenate([qkv[:, :model_width], qkv[:, model_width : 2 * model_width], small], axis=0),
        jnp.concatenate([qkv[:, 2 * model_width :], w_out[0], small], axis=0),
    )
    fc_blocks = w_fc[0].reshape(rows, 4, model_width).transpose(1, 0, 2).reshape(4 * rows, model_width)
    ffn_sets = (fc_blocks, w_proj[0])

    def gathered(sets):
        own = jnp.where(replica == 0, sets[0], sets[1])
        other_layer = swap(own, SECTION)
        layers = []
        for layer in range(2):
            chunk = jnp.where(section == layer, own, other_layer)
            chunks = ring_gather(chunk, count)
            buffer = jnp.zeros((2, count) + chunk.shape, LOW)
            for offset in range(count):
                twin = swap(chunks[offset], REPLICA)
                at = owner(offset)
                buffer = lax.dynamic_update_slice(buffer, chunks[offset][None, None], (replica, at, 0, 0))
                buffer = lax.dynamic_update_slice(buffer, twin[None, None], (1 - replica, at, 0, 0))
            layers.append(buffer)
        return layers

    attn = gathered(attn_sets)
    ffn = gathered(ffn_sets)

    def block(buffer, which, at):
        return buffer[which, :, at * rows : (at + 1) * rows].reshape(count * rows, model_width)

    def unpacked(layer):
        a, f = attn[layer], ffn[layer]
        vec = a[0, :, 2 * rows :].reshape(count, -1)[:, : 12 * rows].reshape(count, 12, rows).astype(F32)

        def row(i):
            return vec[:, i].reshape(-1)

        return Bag(
            q=block(a, 0, 0), k=block(a, 0, 1), v=block(a, 1, 0), o=block(a, 1, 1),
            fc=jnp.concatenate([block(f, 0, i) for i in range(4)], axis=1),
            proj=f[1].reshape(count * 4 * rows, model_width),
            gains=(row(0), row(1)), offsets=(row(2), row(3)), q_bias=row(4), v_bias=row(5),
            out_bias=row(6), fc_bias=vec[:, 7:11].reshape(-1), proj_bias=row(11),
        )

    weights = [unpacked(0), unpacked(1)]
    outputs, states = [], []
    for layer in range(2):
        output, saved = layer_forward(current, weights[layer], plan, place)
        outputs.append(output.astype(LOW))
        states.append(saved)
        current = outputs[-1].astype(F32)
    grad_inputs, totals = [None, None], [None, None]
    arriving = upstream.astype(F32)

    def pieces(attn_rows, layer_grads, which):
        pass

    def blocks_of(grad, cols):
        return grad.astype(LOW).reshape(count, -1, cols)

    def scattered(sets):
        own = jnp.where(replica == 0, sets[0], sets[1])
        other = jnp.where(replica == 0, sets[1], sets[0])
        paired = add_low(own, swap(other, REPLICA))
        return ring_scatter(
            lambda k: lax.dynamic_index_in_dim(paired, owner(k), 0, keepdims=False),
            paired.shape[1], count,
        )

    scattered_attn, scattered_ffn = [None, None], [None, None]
    for layer in (1, 0):
        grad_input, grads = layer_backward(arriving, states[layer], weights[layer], plan, place)
        grad_inputs[layer] = grad_input
        arriving = grad_input.astype(LOW).astype(F32)
        vec = jnp.concatenate(
            [
                grads.gains, grads.offsets, grads.qv_bias, grads.out_bias[None],
            ], axis=0,
        ).reshape(7, count, rows).transpose(1, 0, 2)
        vec = jnp.concatenate(
            [vec, grads.fc_bias.reshape(count, 4, rows), grads.proj_bias.reshape(count, 1, rows)],
            axis=1,
        ).astype(LOW).reshape(count, 12 * rows)
        vec = jnp.concatenate(
            [vec, jnp.zeros((count, small_rows * model_width - 12 * rows), LOW)], axis=1
        ).reshape(count, small_rows, model_width)
        scattered_ffn[layer] = scattered(
            (
                jnp.concatenate(
                    [blocks_of(grads.fc[:, i * model_width : (i + 1) * model_width], model_width) for i in range(4)],
                    axis=1,
                ),
                blocks_of(grads.proj, model_width),
            )
        )
        scattered_attn[layer] = scattered(
            (
                jnp.concatenate([blocks_of(grads.q, model_width), blocks_of(grads.k, model_width), vec], axis=1),
                jnp.concatenate([blocks_of(grads.v, model_width), blocks_of(grads.o, model_width), vec], axis=1),
            )
        )

    def finished(parts):
        own = jnp.where(section == 0, parts[0], parts[1])
        other = jnp.where(section == 0, parts[1], parts[0]).astype(LOW)
        total = (own + swap(other, SECTION).astype(F32)).astype(LOW)
        twin = swap(total, REPLICA)
        return (
            jnp.where(replica == 0, total, twin).astype(F32),
            jnp.where(replica == 0, twin, total).astype(F32),
        )

    ffn_total = finished(scattered_ffn)
    attn_total = finished(scattered_attn)
    fc_grad = ffn_total[0].reshape(4, rows, model_width).transpose(1, 0, 2).reshape(rows, 4 * model_width)
    proj_grad = ffn_total[1]
    qkv_grad = jnp.concatenate(
        [attn_total[0][:rows], attn_total[0][rows : 2 * rows], attn_total[1][:rows]], axis=1
    )
    out_grad = attn_total[1][rows : 2 * rows]
    vec = attn_total[0][2 * rows :].reshape(-1)[: 12 * rows].reshape(12, rows)

    def by_owner(per_layer):
        low = [reshard(v.astype(LOW)) for v in per_layer]
        own = jnp.where(section == 0, low[0], low[1])
        other = jnp.where(section == 0, low[1], low[0])
        got = swap(other, SECTION)
        return jnp.stack([jnp.where(section == 0, own, got), jnp.where(section == 0, got, own)])[None]

    acts = by_owner(outputs)
    in_grads = by_owner(grad_inputs).astype(F32)
    return (
        acts,
        in_grads,
        vec[0:2][None],
        vec[2:4][None],
        qkv_grad[None],
        vec[4:6][None],
        out_grad[None],
        vec[6][None],
        fc_grad[None],
        vec[7:11].reshape(1, 4 * rows),
        proj_grad[None],
        vec[11][None],
    )


ANY = pl.BlockSpec(memory_space=pl.ANY)
VMEM = pl.BlockSpec(memory_space=pltpu.VMEM)
SMEM = pl.BlockSpec(memory_space=pltpu.SMEM)
PAIR = 2 * HEAD
VMEM_LIMIT = 24 * 2**20
MEMORY_RATE = 3.69e6


def mm(a, b):
    return lax.dot_general(a, b, (((1,), (0,)), ((), ())), preferred_element_type=F32)


def mm_nt(a, b):
    return lax.dot_general(a, b, (((1,), (1,)), ((), ())), preferred_element_type=F32)


def mm_tn(a, b):
    return lax.dot_general(a, b, (((0,), (0,)), ((), ())), preferred_element_type=F32)


def call(body, micros, operands, specs, outs, scratch, saves=(), keep=True):
    outs = list(outs) + (list(saves) if keep else [])
    spare = [] if keep else [pltpu.VMEM(shape, kind) for shape, kind, _ in saves]
    return pl.pallas_call(
        body,
        in_specs=specs,
        out_specs=[ANY if space is True else VMEM for _, _, space in outs],
        out_shape=[
            {None: jax.ShapeDtypeStruct, True: pltpu.HBM, False: pltpu.VMEM}[space](shape, kind)
            for shape, kind, space in outs
        ],
        scratch_shapes=spare + scratch,
        compiler_params=pltpu.CompilerParams(vmem_limit_bytes=VMEM_LIMIT),
        cost_estimate=pl.CostEstimate(
            flops=0, bytes_accessed=int(micros * MEMORY_RATE), transcendentals=0
        ),
    )(*operands)


SEATS = 4


def low_lanes(shape):
    return lax.broadcasted_iota(jnp.int32, shape, len(shape) - 1) % PAIR < HEAD


def turn(tile):
    return pltpu.roll(tile, HEAD, 1)


def tiles_of(values, seat):
    at = 3 * seat // 2
    pair, single = (at, at + 1) if seat % 2 == 0 else (at + 1, at)
    return [values[:, t * PAIR : (t + 1) * PAIR] for t in (pair, single)]


def join(first, second, seat):
    low = low_lanes(first.shape)
    if seat % 2 == 0:
        return jnp.where(low, first, turn(second))
    return jnp.where(low, turn(first), second)


def fold(tile, seat):
    half = tile.shape[0] // 2
    return join(tile[:half], tile[half:], seat)


def split(tile, seat):
    low = low_lanes(tile.shape)
    turned = turn(tile)
    if seat % 2 == 0:
        return jnp.where(low, tile, 0.0), jnp.where(low, turned, 0.0)
    return jnp.where(low, 0.0, turned), jnp.where(low, 0.0, tile)


def unfold(tile, seat):
    return jnp.concatenate(split(tile, seat), axis=0)


def whole_rows(pairs, singles):
    tiles = []
    for even in range(0, SEATS, 2):
        tiles += [pairs[even], singles[even] + singles[even + 1], pairs[even + 1]]
    return jnp.concatenate(tiles, axis=1)


def start_all(copies):
    for copy in copies:
        copy.start()
    return copies


def wait_all(copies):
    for copy in copies:
        copy.wait()


def to_seats(scratch, outs, idx, count, sems):
    return start_all(
        [
            pltpu.make_async_copy(scratch.at[idx[count + 2 + k]], outs[k], sems.at[k])
            for k in range(SEATS)
        ]
    )


def from_seats(ins, scratch, idx, count, sems):
    return start_all(
        [
            pltpu.make_async_copy(ins[k], scratch.at[idx[count + 2 + k]], sems.at[k])
            for k in range(SEATS)
        ]
    )


def in_order(refs, scratch, at, sems, outward):
    copies = []
    for k in range(SEATS):
        for p in range(2):
            ends = refs[k].at[p], scratch.at[at[2 * k + p]]
            if outward:
                ends = ends[::-1]
            copies.append(pltpu.make_async_copy(*ends, sems.at[2 * k + p]))
    return start_all(copies)


def block_rows(segment):
    return 4 * segment + segment // 2


class Loader:
    def __init__(self, sems):
        self.sems = sems
        self.used = 0
        self.waits = {}

    def load(self, idx, count, own, twin, targets):
        slots = {}
        for which in (0, 1):
            for at, (offset, rows, ref, key) in enumerate(targets[which]):
                for k in range(count):
                    slots[which, at, k] = self.used
                    self.waits.setdefault(key, []).append((ref, self.used))
                    self.used += 1
        for rep in (0, 1):
            @pl.when(idx[count] == rep)
            def _():
                for which in (0, 1):
                    chunks = own if which == rep else twin
                    for at, (offset, rows, ref, key) in enumerate(targets[which]):
                        for k in range(count):
                            if len(chunks) == 1:
                                chunk, place = chunks[0].at[k], k
                            else:
                                chunk, place = chunks[k], idx[k]
                            pltpu.make_async_copy(
                                chunk.at[pl.ds(offset, rows)], ref.at[place],
                                self.sems.at[slots[which, at, k]],
                            ).start()

    def wait(self, key):
        for ref, slot in self.waits[key]:
            pltpu.make_async_copy(ref.at[0], ref.at[0], self.sems.at[slot]).wait()


def flat(ref):
    return ref[...].reshape(-1, ref.shape[-1])


def centre(values):
    average = jnp.mean(values, axis=-1, keepdims=True)
    centred = values - average
    scale = lax.rsqrt(jnp.mean(centred * centred, axis=-1, keepdims=True) + EPSILON)
    return centred * scale, scale


def centre_back(grad, hat, scale):
    return scale * (
        grad
        - jnp.mean(grad, axis=-1, keepdims=True)
        - hat * jnp.mean(grad * hat, axis=-1, keepdims=True)
    )


GELU_A, GELU_B = math.sqrt(2 / math.pi), 0.044715


NOTE = 16


def note_rows(small, width):
    rows = small.shape[1]
    hidden = jnp.pad(small[7:11].reshape(1, 4 * rows), ((0, 0), (0, width - 4 * rows)))
    others = jnp.concatenate([small[:7], small[11:]], axis=0)
    others = jnp.pad(others, ((0, NOTE - 9), (0, width - rows)))
    return jnp.concatenate([others, hidden], axis=0)


def read_notes(notes, count, width):
    rows = width // count
    total = None
    hidden = []
    for s in range(count):
        note = notes[s].astype(F32)
        moved = pltpu.roll(note, s * rows, 1) if s else note
        total = moved if total is None else total + moved
        at = (4 * rows * s) % width
        hidden.append(pltpu.roll(note[8:], at, 1)[NOTE - 9 :] if at else note[8:][NOTE - 9 :])
    per = width // (4 * rows)
    lines = [sum(hidden[b * per + i] for i in range(per)) for b in range(4)]
    return [total[:8]] + lines


def flatten(rings):
    chunks = [chunk for lists in rings for chunks in lists for chunk in chunks]
    return [pltpu.with_memory_space_constraint(chunk, pltpu.HBM) for chunk in chunks]


def load_projections(loader, idx, count, rows, chunks, wq, wk, wv, notes):
    first = [(0, rows, wq, 0), (rows, NOTE, notes, 3)]
    loader.load(idx, count, chunks[:count], chunks[count : 2 * count], [first, [(0, rows, wv, 2)]])
    loader.load(idx, count, chunks[2 * count : 3 * count], chunks[3 * count :], [[(0, rows, wk, 1)], []])


def load_output(loader, idx, count, rows, chunks, wo):
    loader.load(idx, count, chunks[2 * count : 3 * count], chunks[3 * count : 4 * count], [[], [(0, rows, wo, 5)]])


def load_feed(loader, idx, count, rows, chunks, wf, wp):
    for pair in range(2):
        own, twin = [chunks[(2 * pair + i) * count : (2 * pair + i + 1) * count] for i in range(2)]
        loader.load(
            idx, count, own, twin,
            [
                [(i * rows, rows, wf.at[2 * pair + i], 2 * pair + i) for i in range(2)],
                [(i * rows, rows, wp.at[:, 2 * pair + i], 4) for i in range(2)],
            ],
        )


def project_kernel(count, segment, inputs, hopped, attn, idx):
    width = inputs[0].shape[1]
    rows = width // count
    given = [] if hopped is None else [hopped]
    tall = block_rows(segment)
    loading = hopped is None

    def body(idx, first, second, *rest):
        arrived, rest = rest[: len(given)], rest[len(given) :]
        if loading:
            chunks, rest = rest[: 4 * count], rest[4 * count :]
            outs, (chosen, wq, wk, wv, vec, blocks, normed, notes, sems, out_sems) = rest[:SEATS], rest[SEATS:]
            loader = Loader(sems)
            load_projections(loader, idx, count, rows, chunks, wq, wk, wv, notes)
        else:
            (wq, wk, wv, vec), rest = rest[:4], rest[4:]
            outs, (chosen, normed, blocks, out_sems) = rest[:SEATS], rest[SEATS:]
        values = jnp.concatenate([first[:segment], second[:segment]], axis=0).astype(F32)
        if given:
            values = jnp.where(idx[count + 1] == 0, values, arrived[0][...].astype(F32))
        chosen[...] = values.astype(LOW)
        hat, _ = centre(values)
        if loading:
            loader.wait(3)
            lines = read_notes([notes[s] for s in range(count)], count, width)
            vec[0:8] = lines[0]
            for b in range(4):
                vec[8 + b : 9 + b] = lines[1 + b]
        low = (hat * vec[0:1] + vec[2:3]).astype(LOW)
        normed[...] = low
        if loading:
            loader.wait(0)
        queries = mm(low, flat(wq)) + vec[4:5]
        if loading:
            loader.wait(1)
        keys = mm(low, flat(wk))
        if loading:
            loader.wait(2)
        values = mm(low, flat(wv)) + vec[5:6]
        for d in range(SEATS):
            (qp, qs), (kp, ks), (vp, vs) = [tiles_of(x, d) for x in (queries, keys, values)]
            both = join(qs, ks, d)
            for p in range(2):
                span = slice(p * segment, (p + 1) * segment)
                for at, tile in enumerate((qp, kp, vp, both)):
                    blocks[d, p, at * segment : (at + 1) * segment] = tile[span].astype(LOW)
                blocks[d, p, 4 * segment :] = fold(vs[span], d).astype(LOW)
        wait_all(to_seats(blocks, outs, idx, count, out_sems))

    weight = ((count, rows, width), LOW, False)
    tokens = ((2 * segment, width), LOW, None)
    stay = ((2 * segment, width), LOW, False)
    blocks = pltpu.VMEM((SEATS, 2, tall, PAIR), LOW)
    sent = [((2, tall, PAIR), LOW, True)] * SEATS
    if loading:
        out = call(
            body, 7, [idx, *inputs, *flatten(attn)], [SMEM, VMEM, VMEM] + [ANY] * (4 * count),
            sent + [tokens, weight, weight, weight, ((12, width), F32, None)],
            [
                blocks, pltpu.VMEM((2 * segment, width), LOW), pltpu.VMEM((count, NOTE, width), LOW),
                pltpu.SemaphoreType.DMA((4 * count,)), pltpu.SemaphoreType.DMA((SEATS,)),
            ],
        )
        return out[:SEATS], out[SEATS], None, out[SEATS + 1 :]
    out = call(
        body, 7, [idx, *inputs, *given, *attn], [SMEM] + [VMEM] * (2 + len(given) + 4),
        sent + [stay, stay], [blocks, pltpu.SemaphoreType.DMA((SEATS,))],
    )
    return out[:SEATS], out[SEATS], out[SEATS + 1], attn


def read_heads(blocks, segment):
    def joined(at):
        return jnp.concatenate(
            [blocks[i, at * segment : (at + 1) * segment] for i in range(blocks.shape[0])], axis=0
        )

    third = joined(3).astype(F32)
    low = low_lanes(third.shape)
    values = [unfold(blocks[i, 4 * segment :].astype(F32), 0) for i in range(blocks.shape[0])]
    return (
        (joined(0), joined(1), joined(2)),
        (
            jnp.where(low, third, 0.0).astype(LOW), turn(third).astype(LOW),
            jnp.concatenate(values, axis=0).astype(LOW),
        ),
    )


def stacked(rows):
    low = low_lanes(rows.shape)
    zero = jnp.zeros_like(rows)
    return jnp.concatenate([jnp.where(low, rows, zero), jnp.where(low, zero, rows)], axis=0)


def unstacked(rows):
    half = rows.shape[0] // 2
    return jnp.where(low_lanes((half, PAIR)), rows[:half], rows[half:])


def earlier(rows, step):
    row = lax.broadcasted_iota(jnp.int32, (rows, step), 0) % step
    return lax.broadcasted_iota(jnp.int32, (rows, step), 1) <= row


def attend_kernel(count, segment, arrived, at, keep):
    length, step = count * segment, 2 * segment
    tall = block_rows(segment)
    short = segment + segment // 2

    def body(at, *rest):
        ins, outs, rest = rest[:SEATS], rest[SEATS : 2 * SEATS], rest[2 * SEATS :]
        attended, total, blocks, backs, sems, out_sems = rest
        wait_all(in_order(ins, blocks, at, sems, False))
        heads = read_heads(blocks, segment)
        for i in range(length // step):
            span = slice(i * step, (i + 1) * step)
            logs = []
            for g, (queries, keys, values) in enumerate(heads):
                query = queries[span] * SCALING
                if g == 0:
                    query = stacked(query)
                mask = earlier(query.shape[0], step)
                near = jnp.where(mask, mm_nt(query, keys[span]), FLOOR)
                highest = jnp.max(near, axis=-1, keepdims=True)
                if i > 0:
                    far = mm_nt(query, keys[: i * step])
                    highest = jnp.maximum(highest, jnp.max(far, axis=-1, keepdims=True))
                    far = jnp.exp(far - highest)
                near = jnp.exp(near - highest)
                denominator = jnp.sum(near, axis=-1, keepdims=True)
                result = mm(near.astype(LOW), values[span])
                if i > 0:
                    denominator += jnp.sum(far, axis=-1, keepdims=True)
                    result += mm(far.astype(LOW), values[: i * step])
                result = result * (1.0 / denominator)
                log = highest + jnp.log(denominator)
                if g == 0:
                    result = unstacked(result)
                    logs += [log[:step], log[step:]]
                else:
                    logs.append(log)
                attended[g, span] = result
                for p in range(2):
                    tile = result[p * segment : (p + 1) * segment]
                    if g == 0:
                        backs[2 * i + p, :segment] = tile.astype(LOW)
                    else:
                        backs[2 * i + p, segment:] = fold(tile, 0).astype(LOW)
            lane = lax.broadcasted_iota(jnp.int32, (step, PAIR), 1)
            total[span] = jnp.where(lane == 0, logs[0], jnp.where(lane == 1, logs[1], logs[2]))
        wait_all(in_order(outs, backs, at, out_sems, True))

    return call(
        body, 9, [at, *arrived], [SMEM] + [ANY] * SEATS,
        [((2, short, PAIR), LOW, True)] * SEATS,
        [
            pltpu.VMEM((count, tall, PAIR), LOW), pltpu.VMEM((count, short, PAIR), LOW),
            pltpu.SemaphoreType.DMA((2 * SEATS,)), pltpu.SemaphoreType.DMA((2 * SEATS,)),
        ],
        [((2, length, PAIR), F32, False), ((length, PAIR), F32, False)], keep,
    )


def attend_back_kernel(count, segment, arrived, grads, attended, total, at, ties):
    length, step = count * segment, 2 * segment
    tall = block_rows(segment)
    short = segment + segment // 2

    def body(at, attended, total, *rest):
        ins, grad_ins, rest = rest[:SEATS], rest[SEATS : 2 * SEATS], rest[2 * SEATS + len(ties) :]
        outs, rest = rest[:SEATS], rest[SEATS:]
        blocks, grads, backs, of_keys, of_values, sems, grad_sems, out_sems = rest
        first = in_order(ins, blocks, at, sems, False)
        second = in_order(grad_ins, grads, at, grad_sems, False)
        wait_all(first)
        heads = read_heads(blocks, segment)
        wait_all(second)
        for i in reversed(range(length // step)):
            span = slice(i * step, (i + 1) * step)
            third = None
            for g, (queries, keys, values) in enumerate(heads):
                query = queries[span] * SCALING
                if g == 0:
                    grad = jnp.concatenate([grads[2 * i + p, :segment] for p in range(2)], axis=0)
                    dots = grad.astype(F32) * attended[0, span]
                    low = low_lanes(dots.shape)
                    dots = jnp.concatenate([jnp.where(low, dots, 0.0), jnp.where(low, 0.0, dots)], axis=0)
                    log = jnp.concatenate([total[span, 0:1], total[span, 1:2]], axis=0)
                    query, grad = stacked(query), stacked(grad)
                else:
                    grad = jnp.concatenate(
                        [unfold(grads[2 * i + p, segment:].astype(F32), 0) for p in range(2)], axis=0
                    )
                    dots = grad * attended[1, span]
                    grad = grad.astype(LOW)
                    log = total[span, 2:3]
                dots = jnp.sum(dots, axis=-1, keepdims=True)
                parts = [(span, True)] + ([(slice(0, i * step), False)] if i > 0 else [])
                of_queries = None
                for keyed, near in parts:
                    weights = jnp.exp(mm_nt(query, keys[keyed]) - log)
                    if near:
                        weights = jnp.where(earlier(query.shape[0], step), weights, 0.0)
                    grad_scores = (weights * (mm_nt(grad, values[keyed]) - dots)).astype(LOW)
                    term = mm(grad_scores, keys[keyed])
                    of_queries = term if of_queries is None else of_queries + term
                    key_term = mm_tn(grad_scores, query)
                    value_term = mm_tn(weights.astype(LOW), grad)
                    if i == length // step - 1:
                        of_keys[g, keyed] = key_term
                        of_values[g, keyed] = value_term
                    else:
                        of_keys[g, keyed] += key_term
                        of_values[g, keyed] += value_term
                of_queries = of_queries * SCALING
                if g == 0:
                    of_queries = unstacked(of_queries)
                    for p in range(2):
                        backs[2 * i + p, :segment] = of_queries[p * segment : (p + 1) * segment].astype(LOW)
                else:
                    third = of_queries
            low = low_lanes((segment, PAIR))
            for p in range(2):
                own = slice(i * step + p * segment, i * step + (p + 1) * segment)
                block = backs.at[2 * i + p]
                block[segment : 2 * segment] = of_keys[0, own].astype(LOW)
                block[2 * segment : 3 * segment] = of_values[0, own].astype(LOW)
                block[3 * segment : 4 * segment] = join(
                    third[p * segment : (p + 1) * segment], of_keys[1, own], 0
                ).astype(LOW)
                block[4 * segment :] = fold(of_values[1, own], 0).astype(LOW)
        wait_all(in_order(outs, backs, at, out_sems, True))

    return call(
        body, 14, [at, attended, total, *arrived, *grads, *ties],
        [SMEM, VMEM, VMEM] + [ANY] * (2 * SEATS + len(ties)),
        [((2, tall, PAIR), LOW, True)] * SEATS,
        [
            pltpu.VMEM((count, tall, PAIR), LOW), pltpu.VMEM((count, short, PAIR), LOW),
            pltpu.VMEM((count, tall, PAIR), LOW), pltpu.VMEM((2, length, PAIR), F32),
            pltpu.VMEM((2, length, PAIR), F32), pltpu.SemaphoreType.DMA((2 * SEATS,)),
            pltpu.SemaphoreType.DMA((2 * SEATS,)), pltpu.SemaphoreType.DMA((2 * SEATS,)),
        ],
    )


def feed_rows(mid, vec, wf, wp, active, slope, wait):
    width = mid.shape[1]
    hat, scale = centre(mid)
    low = (hat * vec[1:2] + vec[3:4]).astype(LOW)
    for b in range(4):
        wait(b)
        span = slice(b * width, (b + 1) * width)
        u = mm(low, flat(wf.at[b])) + vec[8 + b : 9 + b]
        square = u * u
        t = jnp.tanh(u * (GELU_A + GELU_A * GELU_B * square))
        half = 0.5 + 0.5 * t
        active[:, span] = (u * half).astype(LOW)
        if slope is not None:
            slope[:, span] = (
                half + u * (0.5 - 0.5 * t * t) * (GELU_A + 3.0 * GELU_A * GELU_B * square)
            ).astype(LOW)
    wait(4)
    return low, hat, scale, (mid + mm(active[...], flat(wp)) + vec[7:8]).astype(LOW)


def feed_kernel(count, segment, returned, inputs, vec, rings, idx):
    width = inputs.shape[1]
    rows, tokens = width // count, 2 * segment
    short = segment + segment // 2

    def body(idx, x, vec, *rest):
        back, chunks, rest = rest[:SEATS], rest[SEATS : SEATS + 8 * count], rest[SEATS + 8 * count :]
        output, wo, wf, wp, blocks, active, sems, in_sems = rest
        loader = Loader(sems)
        copies = from_seats(back, blocks, idx, count, in_sems)
        load_output(loader, idx, count, rows, chunks, wo)
        load_feed(loader, idx, count, rows, chunks[4 * count :], wf, wp)
        wait_all(copies)
        low = read_returned(blocks, segment).astype(LOW)
        loader.wait(5)
        mid = x[...].astype(F32) + mm(low, flat(wo)) + vec[6:7]
        output[...] = feed_rows(mid, vec, wf, wp, active, None, loader.wait)[3]

    return call(
        body, 10, [idx, inputs, vec, *returned, *flatten(rings)],
        [SMEM, VMEM, VMEM] + [ANY] * (SEATS + 8 * count),
        [
            ((tokens, width), LOW, None), ((count, rows, width), LOW, False),
            ((4, count, rows, width), LOW, False), ((count, 4, rows, width), LOW, False),
        ],
        [
            pltpu.VMEM((SEATS, 2, short, PAIR), LOW), pltpu.VMEM((tokens, 4 * width), LOW),
            pltpu.SemaphoreType.DMA((9 * count,)), pltpu.SemaphoreType.DMA((SEATS,)),
        ],
    )


def read_returned(blocks, segment):
    pairs, singles = [], []
    for d in range(SEATS):
        pairs.append(jnp.concatenate([blocks[d, p, :segment].astype(F32) for p in range(2)], axis=0))
        singles.append(
            jnp.concatenate([unfold(blocks[d, p, segment:].astype(F32), d) for p in range(2)], axis=0)
        )
    return whole_rows(pairs, singles)


def feed_back_rows(wide, hat, scale, slope, vec, wo, wf, wp, gh, sums, blocks, segment):
    width = wide.shape[1]
    branch = wide.astype(LOW)
    weight = flat(wp)
    back = jnp.zeros(wide.shape, F32)
    for b in range(4):
        span = slice(b * width, (b + 1) * width)
        ga = mm_nt(branch, weight[span])
        low = (ga * slope[:, span].astype(F32)).astype(LOW)
        if sums is not None:
            gh[:, span] = low
            sums[3 + b : 4 + b] = jnp.sum(low.astype(F32), axis=0, keepdims=True)
        back += mm_nt(low, flat(wf.at[b]))
    total = wide + centre_back(back * vec[1:2], hat, scale)
    low = total.astype(LOW)
    values = mm_nt(low, flat(wo))
    for d in range(SEATS):
        pair, single = tiles_of(values, d)
        for p in range(2):
            part = slice(p * segment, (p + 1) * segment)
            blocks[d, p, :segment] = pair[part].astype(LOW)
            blocks[d, p, segment:] = fold(single[part], d).astype(LOW)
    if sums is not None:
        sums[0:1] = jnp.sum(back * hat, axis=0, keepdims=True)
        sums[1:2] = jnp.sum(back, axis=0, keepdims=True)
        sums[2:3] = jnp.sum(low.astype(F32), axis=0, keepdims=True)
        sums[7:8] = jnp.sum(wide, axis=0, keepdims=True)
    return total, low


def turn_kernel(count, segment, returned, inputs, vec, weights, grads, idx):
    width = inputs.shape[1]
    tokens = 2 * segment
    short = segment + segment // 2

    def body(idx, x, vec, wo, wf, wp, first, second, *rest):
        back, outs, rest = rest[:SEATS], rest[SEATS : 2 * SEATS], rest[2 * SEATS :]
        output, attended, middle, normed, slope, active, grad_middle, blocks, in_sems, out_sems = rest
        wait_all(from_seats(back, blocks, idx, count, in_sems))
        low = read_returned(blocks, segment).astype(LOW)
        attended[...] = low
        mid = x[...].astype(F32) + mm(low, flat(wo)) + vec[6:7]
        middle[...] = mid
        normed[...], hat, scale, output[...] = feed_rows(
            mid, vec, wf, wp, active, slope, lambda key: None
        )
        wide = jnp.concatenate([first[...], second[...]], axis=0).astype(F32)
        grad_middle[...] = feed_back_rows(
            wide, hat, scale, slope, vec, wo, wf, wp, None, None, blocks, segment
        )[0]
        wait_all(to_seats(blocks, outs, idx, count, out_sems))

    rows = ((tokens, width), LOW, False)
    return call(
        body, 10, [idx, inputs, vec, *weights, *grads, *returned],
        [SMEM] + [VMEM] * 7 + [ANY] * SEATS,
        [((2, short, PAIR), LOW, True)] * SEATS
        + [
            ((tokens, width), LOW, None), rows, ((tokens, width), F32, False), rows,
            ((tokens, 4 * width), LOW, False), ((tokens, 4 * width), LOW, False),
            ((tokens, width), F32, False),
        ],
        [
            pltpu.VMEM((SEATS, 2, short, PAIR), LOW), pltpu.SemaphoreType.DMA((SEATS,)),
            pltpu.SemaphoreType.DMA((SEATS,)),
        ],
    )


def feed_back_kernel(count, segment, grads, hopped, saved, weights, idx):
    width = grads[0].shape[1]
    tokens = 2 * segment
    short = segment + segment // 2

    def body(idx, first, second, hopped, middle, slope, active, normed, vec, wo, wf, wp, *rest):
        outs, rest = rest[:SEATS], rest[SEATS:]
        grad_middle, mine, theirs, sums, grad_out, blocks, gh, out_sems = rest
        wide = jnp.concatenate([first[...], second[...]], axis=0).astype(F32)
        wide = jnp.where(idx[count + 1] == 1, wide, hopped[...].astype(F32))
        hat, scale = centre(middle[...])
        grad_middle[...], grad_out[...] = feed_back_rows(
            wide, hat, scale, slope, vec, wo, wf, wp, gh, sums, blocks, segment
        )
        copies = to_seats(blocks, outs, idx, count, out_sems)
        branch = wide.astype(LOW)

        @pl.when(idx[count] == 0)
        def _():
            mine[:, :width] = normed[...]
            mine[:, width:] = gh[...]
            theirs[:, :width] = branch
            theirs[:, width:] = active[...]

        @pl.when(idx[count] == 1)
        def _():
            mine[:, :width] = branch
            mine[:, width:] = active[...]
            theirs[:, :width] = normed[...]
            theirs[:, width:] = gh[...]

        wait_all(copies)

    return call(
        body, 14,
        [
            idx, *grads, hopped, saved.middle, saved.slope, saved.active, saved.normed_two, saved.vec,
            *weights,
        ],
        [SMEM] + [VMEM] * 11,
        [((2, short, PAIR), LOW, True)] * SEATS
        + [
            ((tokens, width), F32, None), ((tokens, 5 * width), LOW, None),
            ((tokens, 5 * width), LOW, None), ((8, width), F32, None), ((tokens, width), LOW, None),
        ],
        [
            pltpu.VMEM((SEATS, 2, short, PAIR), LOW), pltpu.VMEM((tokens, 4 * width), LOW),
            pltpu.SemaphoreType.DMA((SEATS,)),
        ],
    )


def project_back_kernel(count, segment, returned, grad_middle, grad_out, saved, weights, idx, keep):
    tokens, width = grad_middle.shape
    rows = width // count
    tall = block_rows(segment)
    kept = [grad_out, saved.normed, saved.attended_low] if keep else []

    def body(idx, grad_middle, x, vec, *rest):
        held, rest = rest[: len(kept)], rest[len(kept) :]
        back, rest = rest[:SEATS], rest[SEATS:]
        (wq, wk, wv), rest = rest[:3], rest[3:]
        grad_low, grad_in, mine, theirs, sums, blocks, in_sems = rest
        copies = from_seats(back, blocks, idx, count, in_sems)
        hat, scale = centre(x[...].astype(F32))
        wait_all(copies)
        pairs, singles = [[], [], []], [[], [], []]
        for d in range(SEATS):
            for at in range(3):
                pairs[at].append(
                    jnp.concatenate(
                        [blocks[d, p, at * segment : (at + 1) * segment].astype(F32) for p in range(2)], axis=0
                    )
                )
            both = [split(blocks[d, p, 3 * segment : 4 * segment].astype(F32), d) for p in range(2)]
            for at in range(2):
                singles[at].append(jnp.concatenate([b[at] for b in both], axis=0))
            singles[2].append(
                jnp.concatenate([unfold(blocks[d, p, 4 * segment :].astype(F32), d) for p in range(2)], axis=0)
            )
        gq, gk, gv = [whole_rows(a, b).astype(LOW) for a, b in zip(pairs, singles)]
        total = mm_nt(gq, flat(wq))
        total += mm_nt(gk, flat(wk))
        total += mm_nt(gv, flat(wv))
        result = grad_middle[...] + centre_back(total * vec[0:1], hat, scale)
        grad_low[...] = result.astype(LOW)
        if not keep:
            return
        grad_in[...] = result
        sums[0:1] = jnp.sum(total * hat, axis=0, keepdims=True)
        sums[1:2] = jnp.sum(total, axis=0, keepdims=True)
        sums[2:3] = jnp.sum(gq.astype(F32), axis=0, keepdims=True)
        sums[3:4] = jnp.sum(gv.astype(F32), axis=0, keepdims=True)
        sums[4:8] = jnp.zeros((4, width), F32)
        grad_out, normed, attended = held

        def fill(first, second):
            first[:, :width] = normed[...]
            first[:, width : 2 * width] = gq
            first[:, 2 * width : 3 * width] = normed[...]
            first[:, 3 * width :] = gk
            second[:, :width] = normed[...]
            second[:, width : 2 * width] = gv
            second[:, 2 * width : 3 * width] = attended[...]
            second[:, 3 * width :] = grad_out[...]

        @pl.when(idx[count] == 0)
        def _():
            fill(mine, theirs)

        @pl.when(idx[count] == 1)
        def _():
            fill(theirs, mine)

    return call(
        body, 8, [idx, grad_middle, saved.inputs, saved.vec, *kept, *returned, *weights],
        [SMEM] + [VMEM] * (3 + len(kept)) + [ANY] * SEATS + [VMEM] * 3,
        [((tokens, width), LOW, None)],
        [
            pltpu.VMEM((SEATS, 2, tall, PAIR), LOW), pltpu.SemaphoreType.DMA((SEATS,)),
        ],
        [
            ((tokens, width), F32, None), ((tokens, 4 * width), LOW, None),
            ((tokens, 4 * width), LOW, None), ((8, width), F32, None),
        ],
        keep,
    )


def send_out(scratch, pieces, idx, sems, start):
    for at, (out, to, rows, base, stride, k) in enumerate(pieces):
        source = pl.ds(pl.multiple_of(base + idx[k] * stride, 16), rows)
        copy = pltpu.make_async_copy(scratch.at[source], out.at[pl.ds(to, rows)], sems.at[at])
        copy.start() if start else copy.wait()


def ffn_terms_kernel(count, parts, idx):
    width = parts[0].shape[1] // 5
    rows = width // count

    def body(idx, *rest):
        given, rest = rest[: len(parts)], rest[len(parts) :]
        outs, (scratch, sems) = rest[: 2 * count], rest[2 * count :]
        narrow = jnp.concatenate([part[:, :width] for part in given], axis=0)

        def wide(b):
            span = slice((1 + b) * width, (2 + b) * width)
            return jnp.concatenate([part[:, span] for part in given], axis=0)

        def pieces(b):
            return [
                (outs[b // 2 * count + k], b % 2 * rows, rows, b * width, rows, k) for k in range(count)
            ]

        @pl.when(idx[count] == 0)
        def _():
            for b in range(4):
                scratch[b * width : (b + 1) * width] = mm_tn(narrow, wide(b)).astype(LOW)
                send_out(scratch, pieces(b), idx, sems.at[pl.ds(b * count, count)], True)
            for b in range(4):
                send_out(scratch, pieces(b), idx, sems.at[pl.ds(b * count, count)], False)

        @pl.when(idx[count] == 1)
        def _():
            for b in range(4):
                scratch[b * width : (b + 1) * width] = mm_tn(wide(b), narrow).astype(LOW)
            halves = [
                (outs[ring * count + k], 0, 2 * rows, 2 * rows * ring, 4 * rows, k)
                for ring in range(2) for k in range(count)
            ]
            send_out(scratch, halves, idx, sems, True)
            send_out(scratch, halves, idx, sems, False)

    outs = call(
        body, 8, [idx, *parts], [SMEM] + [VMEM] * len(parts),
        [((2 * rows, width), LOW, True)] * (2 * count),
        [pltpu.VMEM((4 * width, width), LOW), pltpu.SemaphoreType.DMA((4 * count,))],
    )
    return outs[:count], outs[count:]


def attn_terms_kernel(count, parts, sums_one, sums_two, idx):
    width = parts[0].shape[1] // 4
    rows = width // count

    def body(idx, *rest):
        parts_in, (one, two), rest = rest[: len(parts)], rest[len(parts) : len(parts) + 2], rest[len(parts) + 2 :]
        outs, (scratch, notes, sems, note_sems) = rest[: 2 * count], rest[2 * count :]

        def both(b):
            span = slice(b * width, (b + 1) * width)
            return jnp.concatenate([part[:, span] for part in parts_in], axis=0)

        def pieces(b):
            return [(outs[b * count + k], 0, rows, b * width, rows, k) for k in range(count)]

        flatly = jnp.concatenate(
            [
                one[0:1], two[0:1], one[1:2], two[1:2], one[2:3], one[3:4], two[2:3], two[7:8],
                jnp.zeros((NOTE - 8, width), F32),
            ],
            axis=0,
        )
        lane = lax.broadcasted_iota(jnp.int32, (NOTE, width), 1)
        line = lax.broadcasted_iota(jnp.int32, (NOTE, width), 0)
        for s in range(count):
            note = pltpu.roll(flatly, width - s * rows, 1) if s else flatly
            start = 4 * rows * s
            hidden = two[3 + start // width : 4 + start // width]
            hidden = pltpu.roll(
                jnp.broadcast_to(hidden, (8, width)), (width - start % width) % width, 1
            )
            hidden = jnp.concatenate([hidden, hidden], axis=0)
            note = jnp.where(
                (line < 8) & (lane < rows), note,
                jnp.where((line == NOTE - 1) & (lane < 4 * rows), hidden, 0.0),
            )
            notes[s] = note.astype(LOW)
        copies = start_all(
            [
                pltpu.make_async_copy(
                    notes.at[idx[k]], outs[k].at[pl.ds(rows, NOTE)], note_sems.at[k]
                )
                for k in range(count)
            ]
        )
        for b in range(2):
            scratch[b * width : (b + 1) * width] = mm_tn(both(2 * b), both(2 * b + 1)).astype(LOW)
            send_out(scratch, pieces(b), idx, sems.at[pl.ds(b * count, count)], True)
        for b in range(2):
            send_out(scratch, pieces(b), idx, sems.at[pl.ds(b * count, count)], False)
        wait_all(copies)

    outs = call(
        body, 5, [idx, *parts, sums_one, sums_two], [SMEM] + [VMEM] * (len(parts) + 2),
        [((rows + NOTE, width), LOW, True)] * count + [((rows, width), LOW, True)] * count,
        [
            pltpu.VMEM((2 * width, width), LOW), pltpu.VMEM((count, NOTE, width), LOW),
            pltpu.SemaphoreType.DMA((2 * count,)), pltpu.SemaphoreType.DMA((count,)),
        ],
    )
    return outs[:count], outs[count:]


class Rings:
    def __init__(self, rings):
        self.rings = rings

    def step(self, *after):
        for ring in self.rings:
            ring.step(*after)

    @property
    def last(self):
        return [v for ring in self.rings for v in ring.last if v is not None]


def hold(values, *after):
    return lax.optimization_barrier((values, after))[0] if len(after) else values


class GatherRing:
    def __init__(self, chunk, count, rightward):
        self.right, self.left = ring_pairs(count)
        self.count, self.rightward, self.at = count, rightward, 0
        self.last = (chunk, chunk)
        self.own = {0: chunk}
        self.twin = {0: swap(chunk, REPLICA)}

    def keep(self, k, chunk):
        self.own[k], self.twin[k] = chunk, swap(chunk, REPLICA)

    def step(self, *after):
        self.at += 1
        near, far = hold(self.last, *after)
        if self.at < self.count // 2:
            near = lax.ppermute(near, SHARD, self.right)
            far = lax.ppermute(far, SHARD, self.left)
            self.keep(self.count - self.at, near)
            self.keep(self.at, far)
            self.last = (near, far)
        else:
            if self.rightward:
                last = lax.ppermute(near, SHARD, self.right)
            else:
                last = lax.ppermute(far, SHARD, self.left)
            self.keep(self.at, last)
            self.last = (last,)

    def lists(self):
        return [[side[k] for k in range(self.count)] for side in (self.own, self.twin)]


class ScatterRing:
    def __init__(self, pieces, count, rightward):
        self.right, self.left = ring_pairs(count)
        self.pieces, self.count, self.rightward = pieces, count, rightward
        self.at = count // 2
        self.last = None

    def step(self, *after):
        pieces, half = self.pieces, self.count // 2
        if self.at == half:
            far = hold(pieces[half], *after)
            if self.rightward:
                self.last = (lax.ppermute(far, SHARD, self.right), None)
            else:
                self.last = (None, lax.ppermute(far, SHARD, self.left))
        else:
            sides = []
            for piece, term in zip((pieces[self.at], pieces[self.count - self.at]), self.last):
                sides.append(piece if term is None else add_low(piece, term))
            first, second = hold(tuple(sides), *after)
            self.last = (
                lax.ppermute(first, SHARD, self.right), lax.ppermute(second, SHARD, self.left)
            )
        self.at -= 1

    def total(self):
        return self.pieces[0].astype(F32) + self.last[0].astype(F32) + self.last[1].astype(F32)


def fast_device(
    tokens, cotangent, group_order, norm_gains, norm_biases, w_qkv, qv_bias, w_out, out_bias,
    w_fc, fc_bias, w_proj, proj_bias,
):
    count = lax.axis_size(SHARD)
    section = lax.axis_index(SECTION)
    replica = lax.axis_index(REPLICA)
    shard = lax.axis_index(SHARD)
    segment, width = tokens.shape[1], tokens.shape[2]
    rows = w_qkv.shape[1]
    half = count // 2
    order = ring_order(count)
    position = jnp.asarray(np.argsort(np.array(order)), jnp.int32)[shard]
    around = lax.rem(position + jnp.arange(count, dtype=jnp.int32), count)
    seat = 2 * replica + lax.rem(shard, 2)
    others = seat ^ jnp.arange(SEATS, dtype=jnp.int32)
    idx = jnp.concatenate(
        [jnp.asarray(order, jnp.int32)[around], jnp.stack([replica, section]).astype(jnp.int32), others]
    )

    ways = [
        [
            (r * count + 2 * z + y, (z // 2) * count + 2 * (2 * r + (z + j) % 2) + y)
            for r in range(2) for z in range(half) for y in range(2)
        ]
        for j in range(2)
    ]
    odd = lax.rem(shard // 2, 2)

    def gather_in(x, j, *more):
        own = lax.dynamic_index_in_dim(x, lax.rem(odd + j, 2), 0, keepdims=False)
        own = jnp.concatenate([own, *more], axis=0) if more else own
        return lax.ppermute(own, (REPLICA, SHARD), ways[j])

    def give_back(x):
        parts = [
            lax.ppermute(
                x[j * segment : (j + 1) * segment], (REPLICA, SHARD), [(b, a) for a, b in ways[j]]
            )
            for j in range(2)
        ]
        return jnp.stack([jnp.where(even, *parts), jnp.where(even, *parts[::-1])])[None]

    def exchange(parts):
        diagonal = [(r * count + s, (1 - r) * count + (s ^ 1)) for r in range(2) for s in range(count)]
        return [
            pltpu.with_memory_space_constraint(parts[0], pltpu.HBM),
            lax.ppermute(parts[1], SHARD, [(s, s ^ 1) for s in range(count)]),
            swap(parts[2], REPLICA),
            lax.ppermute(parts[3], (REPLICA, SHARD), diagonal),
        ]

    small = jnp.concatenate(
        [norm_gains[0], norm_biases[0], qv_bias[0], out_bias, fc_bias.reshape(4, rows), proj_bias],
        axis=0,
    )
    qkv = w_qkv[0]
    attn_own = [
        jnp.concatenate(
            [jnp.where(replica == 0, qkv[:, :width], qkv[:, 2 * width :]), note_rows(small, width)], axis=0
        ),
        jnp.where(replica == 0, qkv[:, width : 2 * width], w_out[0]),
    ]
    ffn_own = [
        jnp.where(
            replica == 0,
            jnp.concatenate([w_fc[0][:, b * width : (b + 1) * width] for b in (2 * i, 2 * i + 1)], axis=0),
            w_proj[0][2 * i * rows : 2 * (i + 1) * rows],
        )
        for i in range(2)
    ]

    attn_ring = Rings([GatherRing(own, count, i == 0) for i, own in enumerate(attn_own)])
    attn_ring.step()
    order_row = lax.dynamic_index_in_dim(group_order, odd, 0).astype(LOW)
    order_rows = jnp.pad(order_row, ((0, NOTE - 1), (0, width - count)))
    packed = [gather_in(tokens, 0, order_rows), gather_in(tokens, 1)]
    slot = lax.rem(shard // 2 + jnp.arange(2, dtype=jnp.int32), 2)
    which = ((4 * (others // 2) + others % 2)[:, None] + 2 * slot[None, :]).reshape(-1)
    chosen = (which[:, None] == jnp.arange(count, dtype=jnp.int32)[None, :]).astype(jnp.int32)
    packed, chosen, even = lax.optimization_barrier((packed, chosen, odd == 0))
    blocks_at = packed[0][segment, :count].astype(jnp.int32)
    at = jnp.sum(chosen * blocks_at[None, :], axis=1)
    attn_ring.step()
    attn_ring.step()
    ffn_ring = Rings(
        [GatherRing(hold(own, attn_ring.last), count, i == 0) for i, own in enumerate(ffn_own)]
    )
    attn_ring.step()
    attn_lists = [ring.lists() for ring in attn_ring.rings]
    ffn_ring.step()

    def forward(hopped, attn, before):
        sent, inputs, normed, attn = project_kernel(count, segment, packed, hopped, attn, idx)
        arrived = exchange(before[0](sent))
        back = attend_kernel(count, segment, before[1](arrived), at, hopped is not None)
        state = Bag(vec=attn[3], inputs=inputs, normed=normed, arrived=arrived)
        return state, attn, exchange(before[2](back[:SEATS])), back[SEATS:]

    def ring_sent(sent):
        sent = hold(sent, ffn_ring.last)
        ffn_ring.step()
        ffn_ring.step(sent[1])
        return sent

    def ring_arrived(arrived):
        return arrived

    def ring_back(back):
        ffn_ring.step(back[0])
        return back

    def same(values):
        return values

    first, attn, returned, _ = forward(None, attn_lists, [ring_sent, ring_arrived, ring_back])
    output, *ffn = feed_kernel(
        count, segment, returned, first.inputs, first.vec,
        attn_lists + [ring.lists() for ring in ffn_ring.rings], idx,
    )

    def hop(values, backward):
        return lax.ppermute(values, SECTION, [(1, 0)] if backward else [(0, 1)])

    upstream = [gather_in(hold(cotangent, output), j) for j in range(2)]
    state, attn, returned, kept = forward(
        hop(output, False), attn, [same, lambda arrived: hold(arrived, upstream), same]
    )
    state.attended, state.total = kept
    *sent, output, state.attended_low, state.middle, state.normed_two, state.slope, state.active, grad_middle = (
        turn_kernel(count, segment, returned, state.inputs, state.vec, ffn, upstream, idx)
    )
    acts = give_back(output)

    def backward(sent, grad_middle, grad_out, keep, ties, between):
        arrived = exchange(sent)
        ties = ties + between[0](arrived)
        back = attend_back_kernel(
            count, segment, state.arrived, arrived, state.attended, state.total, at, ties
        )
        returned = exchange(between[1](back))
        return project_back_kernel(
            count, segment, between[2](returned), grad_middle, grad_out, state, attn[:3], idx, keep
        )

    early = backward(
        sent, grad_middle, None, False, [],
        [lambda arrived: [], same, lambda returned: hold(returned, acts)],
    )
    rings = []
    *sent, grad_middle, mine, theirs, sums_two, grad_out = feed_back_kernel(
        count, segment, upstream, hop(early[0], True), state, ffn, idx
    )

    def ffn_terms(arrived):
        terms = ffn_terms_kernel(count, hold([mine, swap(theirs, REPLICA)], arrived), idx)
        rings.append(Rings([ScatterRing(t, count, i == 0) for i, t in enumerate(terms)]))
        rings[0].step()
        return [terms[0][0]]

    def ring_back(back):
        rings[0].step(back[1])
        return back

    def ring_returned(returned):
        returned = hold(returned, rings[0].last)
        rings[0].step(returned[1])
        return returned

    low, *last = backward(
        sent, grad_middle, grad_out, True, [], [ffn_terms, ring_back, ring_returned]
    )
    terms = attn_terms_kernel(count, [last[1], swap(last[2], REPLICA)], last[3], sums_two, idx)
    rings[0].step(terms[0][0])
    rings.append(Rings([ScatterRing(t, count, i == 0) for i, t in enumerate(terms)]))
    for _ in range(half):
        rings[1].step()
    in_grads = give_back(hold(last[0].astype(LOW), low)).astype(F32)

    def finished(ring):
        total = ring.total().astype(LOW)
        twin = swap(total, REPLICA)
        return (
            jnp.where(replica == 0, total, twin).astype(F32),
            jnp.where(replica == 0, twin, total).astype(F32),
        )

    feed_totals, totals = [[finished(ring) for ring in pair.rings] for pair in rings]
    fc_grad = jnp.concatenate(
        [half[0][b * rows : (b + 1) * rows] for half in feed_totals for b in range(2)], axis=1
    )
    proj_grad = jnp.concatenate([half[1] for half in feed_totals], axis=0)
    qkv_grad = jnp.concatenate([totals[0][0][:rows], totals[1][0], totals[0][1][:rows]], axis=1)
    note = totals[0][0][rows:] + totals[0][1][rows:]
    vec = note[:8, :rows]
    return (
        acts, in_grads, vec[0:2][None], vec[2:4][None], qkv_grad[None], vec[4:6][None],
        totals[1][1][None], vec[6][None], fc_grad[None], note[NOTE - 1, : 4 * rows][None],
        proj_grad[None], vec[7][None],
    )


def on_each(tokens, *others):
    count = lax.axis_size(SHARD)
    tiles = (tokens.shape[2] // count) % 32 == 0 and tokens.shape[1] % 64 == 0
    seats = count == 2 * SEATS and tokens.shape[0] == 2 and HEADS == 3 * SEATS
    return (fast_device if tiles and seats else on_device)(tokens, *others)


def solution(mesh):
    in_specs = (
        P(REPLICA, SHARD, None),
        P(REPLICA, SHARD, None),
        P(REPLICA, None),
        P(SECTION, None, SHARD),
        P(SECTION, None, SHARD),
        P(SECTION, SHARD, None),
        P(SECTION, None, SHARD),
        P(SECTION, SHARD, None),
        P(SECTION, SHARD),
        P(SECTION, SHARD, None),
        P(SECTION, SHARD),
        P(SECTION, SHARD, None),
        P(SECTION, SHARD),
    )
    out_specs = (
        P(SECTION, REPLICA, SHARD, None),
        P(SECTION, REPLICA, SHARD, None),
        P(SECTION, None, SHARD),
        P(SECTION, None, SHARD),
        P(SECTION, SHARD, None),
        P(SECTION, None, SHARD),
        P(SECTION, SHARD, None),
        P(SECTION, SHARD),
        P(SECTION, SHARD, None),
        P(SECTION, SHARD),
        P(SECTION, SHARD, None),
        P(SECTION, SHARD),
    )
    return jax.shard_map(
        on_each, mesh=mesh, in_specs=in_specs, out_specs=out_specs, check_vma=False
    )
```

```python
import functools
import math
from types import SimpleNamespace as Bag

import jax
import jax.numpy as jnp
import numpy as np
from jax import lax
from jax.experimental import pallas as pl
from jax.experimental.pallas import tpu as pltpu
from jax.sharding import PartitionSpec as P

HEADS = 12
HEAD = 64
EPSILON = 1e-05
SCALING = 0.125
FLOOR = -1e30
SECTION, REPLICA, SHARD = "section", "replica", "shard"
LOW = jnp.bfloat16
F32 = jnp.float32


def ring_order(count):
    return list(range(0, count, 2)) + list(range(count - 1, 0, -2))


def ring_pairs(count):
    order = ring_order(count)
    right = [(order[i], order[(i + 1) % count]) for i in range(count)]
    return right, [(b, a) for a, b in right]


def ring_gather(chunk, count):
    right, left = ring_pairs(count)
    got = {0: chunk}
    from_left = from_right = chunk
    cut = chunk.shape[0] // 32 * 16
    for step in range(1, count // 2 + 1):
        if step == count // 2:
            got[step] = jnp.concatenate(
                [
                    lax.ppermute(from_left[:cut], SHARD, right),
                    lax.ppermute(from_right[cut:], SHARD, left),
                ],
                axis=0,
            )
        else:
            from_left = lax.ppermute(from_left, SHARD, right)
            from_right = lax.ppermute(from_right, SHARD, left)
            got[count - step] = from_left
            got[step] = from_right
    return [got[k] for k in range(count)]


def ring_scatter(piece, rows, count):
    right, left = ring_pairs(count)
    cut = rows // 32 * 16
    half = count // 2
    far = piece(half)
    to_right = lax.ppermute(far[:cut], SHARD, right)
    to_left = lax.ppermute(far[cut:], SHARD, left)
    for distance in range(half - 1, 0, -1):
        first, second = piece(distance), piece(count - distance)
        if distance == half - 1:
            first = jnp.concatenate([add_low(first[:cut], to_right), first[cut:]], axis=0)
            second = jnp.concatenate([second[:cut], add_low(second[cut:], to_left)], axis=0)
        else:
            first = add_low(first, to_right)
            second = add_low(second, to_left)
        to_right = lax.ppermute(first, SHARD, right)
        to_left = lax.ppermute(second, SHARD, left)
    return piece(0).astype(F32) + to_right.astype(F32) + to_left.astype(F32)


def add_low(a, b):
    return (a.astype(F32) + b.astype(F32)).astype(LOW)


def swap(x, axis):
    return lax.ppermute(x, axis, [(0, 1), (1, 0)])


def normalize(values, gain_row, offset):
    average = jnp.mean(values, axis=-1, keepdims=True)
    centred = values - average
    variance = jnp.mean(centred * centred, axis=-1, keepdims=True)
    return centred * lax.rsqrt(variance + EPSILON) * gain_row + offset


def gelu_tanh(values):
    return jax.nn.gelu(values, approximate=True)


def dot(a, b):
    return jnp.dot(a, b, preferred_element_type=F32)


def dot_t(a, b):
    return lax.dot_general(a, b, (((1,), (1,)), ((), ())), preferred_element_type=F32)


def dot_rows(a, b):
    return lax.dot_general(a, b, (((0,), (0,)), ((), ())), preferred_element_type=F32)


class Plan:
    def __init__(self, count, segment):
        self.count = count
        self.segment = segment
        self.splits = count // math.gcd(HEADS, count)
        self.units = HEADS * self.splits // count
        self.part = segment // self.splits
        self.first = [self.units * q // self.splits for q in range(count)]
        self.slots = max(
            (self.units * q + self.units - 1) // self.splits - self.first[q] + 1
            for q in range(count)
        )
        self.groups = [
            [r * count + h * (count // 2) + i for r in range(2) for i in range(count // 2)]
            for h in range(2)
        ]

    def exchange(self, blocks):
        return lax.all_to_all(
            blocks, (REPLICA, SHARD), 0, 0, tiled=True, axis_index_groups=self.groups
        )

    def pack_units(self, heads):
        parts = heads.reshape(self.splits, self.part, HEADS, HEAD)
        parts = parts.transpose(2, 0, 1, 3).reshape(
            self.count, self.units * self.part, HEAD
        )
        return self.fold(parts)

    def fold(self, parts):
        rows = parts.shape[1] // 2
        return jnp.concatenate([parts[:, :rows], parts[:, rows:]], axis=2)

    def unfold(self, folded):
        return jnp.concatenate([folded[..., :HEAD], folded[..., HEAD:]], axis=1)

    def unpack_units(self, folded):
        parts = self.unfold(folded).reshape(HEADS, self.splits, self.part, HEAD)
        return parts.transpose(1, 2, 0, 3).reshape(self.segment, HEADS * HEAD)

    def gather_units(self, folded):
        parts = self.unfold(folded).reshape(self.count, self.units, self.part, HEAD)
        return parts.transpose(1, 0, 2, 3).reshape(self.units, self.count * self.part, HEAD)

    def scatter_units(self, values):
        parts = values.reshape(self.units, self.count, self.part, HEAD).transpose(1, 0, 2, 3)
        return self.fold(parts.reshape(self.count, self.units * self.part, HEAD))

    def head_slots(self, rows):
        blocks = []
        for q in range(self.count):
            cols = []
            for slot in range(self.slots):
                head = min(self.first[q] + slot, HEADS - 1)
                cols.append(rows[:, head * HEAD : (head + 1) * HEAD])
            blocks.append(jnp.concatenate(cols, axis=1))
        return jnp.stack(blocks)

    def sum_slots(self, blocks):
        cols = []
        for head in range(HEADS):
            total = None
            for q in range(self.count):
                last = (self.units * (q + 1) - 1) // self.splits
                if self.first[q] <= head <= last:
                    slot = head - self.first[q]
                    term = blocks[q, :, slot * HEAD : (slot + 1) * HEAD].astype(F32)
                    total = term if total is None else total + term
            cols.append(total)
        return jnp.concatenate(cols, axis=1)


def over(a, b, dim_a, dim_b):
    return lax.dot_general(a, b, (((dim_a,), (dim_b,)), ((), ())), preferred_element_type=F32)


def over_units(a, b):
    return lax.dot_general(a, b, (((0, 1), (0, 1)), ((), ())), preferred_element_type=F32)


def widen(units, slot, slots):
    wide = jnp.concatenate([units] * slots, axis=2)
    lane_slot = jnp.arange(slots * HEAD, dtype=jnp.int32) // HEAD
    return jnp.where(lane_slot[None, None, :] == slot[:, None, None], wide, jnp.zeros_like(wide))


def narrow(wide, slot, slots):
    lane_slot = jnp.arange(slots * HEAD, dtype=jnp.int32) // HEAD
    wide = jnp.where(lane_slot[None, None, :] == slot[:, None, None], wide, jnp.zeros_like(wide))
    return sum(wide[:, :, s * HEAD : (s + 1) * HEAD] for s in range(slots))


def attend_forward(queries, keys, values, query_pos, key_pos):
    scores = over(queries, keys, 2, 1) * SCALING
    visible = key_pos[None, None, :] <= query_pos[:, :, None]
    scores = jnp.where(visible, scores, FLOOR)
    highest = jnp.max(scores, axis=-1, keepdims=True)
    terms = jnp.exp(scores - highest)
    total = jnp.sum(terms, axis=-1, keepdims=True)
    weights = (terms / total).astype(LOW)
    attended = over(weights, values, 2, 0)
    return attended, highest + jnp.log(total)


def attend_backward(queries, keys, values, query_pos, key_pos, log_total, grad, row_dots):
    scores = over(queries, keys, 2, 1) * SCALING
    visible = key_pos[None, None, :] <= query_pos[:, :, None]
    weights = jnp.where(visible, jnp.exp(scores - log_total), 0.0)
    grad_weights = over(grad, values, 2, 1)
    grad_scores = (weights * (grad_weights - row_dots)).astype(LOW)
    grad_queries = (
        over(grad_scores, keys, 2, 0) * SCALING
    )
    grad_keys = (
        over_units(grad_scores, queries) * SCALING
    )
    grad_values = over_units(weights.astype(LOW), grad)
    return grad_queries, grad_keys, grad_values


def layer_forward(inputs, weights, plan, place):
    normed = normalize(inputs, weights.gains[0], weights.offsets[0]).astype(LOW)
    queries = (dot(normed, weights.q) + weights.q_bias).astype(LOW)
    keys = dot(normed, weights.k).astype(LOW)
    values = (dot(normed, weights.v) + weights.v_bias).astype(LOW)
    segment = inputs.shape[0]
    width = plan.slots * HEAD
    sent = jnp.concatenate(
        [
            plan.head_slots(keys),
            plan.head_slots(values),
            plan.pack_units(queries.reshape(segment, HEADS, HEAD)).reshape(
                plan.count, -1, width
            ),
        ],
        axis=1,
    )
    arrived = plan.exchange(sent)
    length = plan.count * segment
    all_keys = arrived[:, :segment].reshape(length, width)
    all_values = arrived[:, segment : 2 * segment].reshape(length, width)
    units = plan.gather_units(arrived[:, 2 * segment :].reshape(plan.count, -1, 2 * HEAD))
    units = widen(units, place.slot, plan.slots)
    attended, log_total = attend_forward(
        units, all_keys, all_values, place.query_pos, place.key_pos
    )
    attended = narrow(attended, place.slot, plan.slots)
    returned = plan.exchange(plan.scatter_units(attended.astype(LOW)))
    attended_low = plan.unpack_units(returned)
    middle = inputs + dot(attended_low, weights.o) + weights.out_bias
    normed_two = normalize(middle, weights.gains[1], weights.offsets[1]).astype(LOW)
    hidden = dot(normed_two, weights.fc) + weights.fc_bias
    active = gelu_tanh(hidden).astype(LOW)
    output = middle + dot(active, weights.proj) + weights.proj_bias
    saved = Bag(
        inputs=inputs, normed=normed, units=units, keys=all_keys, values=all_values,
        attended=attended, log_total=log_total, attended_low=attended_low, middle=middle,
        normed_two=normed_two, hidden=hidden, active=active,
    )
    return output, saved


def layer_backward(arriving, saved, weights, plan, place):
    segment, model_width = arriving.shape
    grad_branch = arriving.astype(LOW)
    grad_active = dot_t(grad_branch, weights.proj)
    grad_hidden = jax.vjp(gelu_tanh, saved.hidden)[1](grad_active)[0].astype(LOW)
    grad_normed_two = dot_t(grad_hidden, weights.fc)
    grad_middle_norm, gain_two, offset_two = jax.vjp(
        normalize, saved.middle, weights.gains[1], weights.offsets[1]
    )[1](grad_normed_two)
    grads = Bag(
        proj=dot_rows(saved.active, grad_branch),
        proj_bias=jnp.sum(grad_branch.astype(F32), axis=0),
        fc=dot_rows(saved.normed_two, grad_hidden),
        fc_bias=jnp.sum(grad_hidden.astype(F32), axis=0),
    )
    grad_middle = arriving + grad_middle_norm
    grad_out = grad_middle.astype(LOW)
    grad_attended = dot_t(grad_out, weights.o).astype(LOW)
    arrived = plan.exchange(plan.pack_units(grad_attended.reshape(segment, HEADS, HEAD)))
    grad_units = plan.gather_units(arrived)
    row_dots = jnp.sum(grad_units.astype(F32) * saved.attended, axis=-1, keepdims=True)
    grad_queries, grad_keys, grad_values = attend_backward(
        saved.units, saved.keys, saved.values, place.query_pos, place.key_pos,
        saved.log_total, widen(grad_units, place.slot, plan.slots), row_dots,
    )
    grad_queries = narrow(grad_queries, place.slot, plan.slots).astype(LOW)
    width = plan.slots * HEAD
    sent = jnp.concatenate(
        [
            grad_keys.astype(LOW).reshape(plan.count, segment, width),
            grad_values.astype(LOW).reshape(plan.count, segment, width),
            plan.scatter_units(grad_queries).reshape(plan.count, -1, width),
        ],
        axis=1,
    )
    returned = plan.exchange(sent)
    grad_k = plan.sum_slots(returned[:, :segment]).astype(LOW)
    grad_v = plan.sum_slots(returned[:, segment : 2 * segment]).astype(LOW)
    grad_q = plan.unpack_units(returned[:, 2 * segment :].reshape(plan.count, -1, 2 * HEAD))
    grad_normed = (
        dot_t(grad_q, weights.q) + dot_t(grad_k, weights.k) + dot_t(grad_v, weights.v)
    )
    grad_input_norm, gain_one, offset_one = jax.vjp(
        normalize, saved.inputs, weights.gains[0], weights.offsets[0]
    )[1](grad_normed)
    grads = Bag(
        proj=grads.proj, proj_bias=grads.proj_bias, fc=grads.fc, fc_bias=grads.fc_bias,
        gains=jnp.stack([gain_one, gain_two]),
        offsets=jnp.stack([offset_one, offset_two]),
        q=dot_rows(saved.normed, grad_q),
        k=dot_rows(saved.normed, grad_k),
        v=dot_rows(saved.normed, grad_v),
        qv_bias=jnp.stack([jnp.sum(grad_q.astype(F32), axis=0), jnp.sum(grad_v.astype(F32), axis=0)]),
        o=dot_rows(saved.attended_low, grad_out),
        out_bias=jnp.sum(grad_out.astype(F32), axis=0),
    )
    return grad_middle + grad_input_norm, grads


def on_device(
    tokens, cotangent, group_order, norm_gains, norm_biases, w_qkv, qv_bias, w_out, out_bias,
    w_fc, fc_bias, w_proj, proj_bias,
):
    count = lax.axis_size(SHARD)
    section = lax.axis_index(SECTION)
    replica = lax.axis_index(REPLICA)
    shard = lax.axis_index(SHARD)
    segment, model_width = tokens.shape[1], tokens.shape[2]
    rows = w_qkv.shape[1]
    half = count // 2
    plan = Plan(count, segment)
    order = ring_order(count)
    position_of = np.argsort(np.array(order))
    position = jnp.asarray(position_of, jnp.int32)[shard]
    order_table = jnp.asarray(order, jnp.int32)

    def owner(offset):
        return order_table[lax.rem(position + offset, count)]

    home = shard // half
    keeps = home == replica
    crossing = []
    for s in range(half):
        crossing += [(count + s, s + half), (s + half, count + s)]

    def reshard(x):
        moved = lax.ppermute(x, (REPLICA, SHARD), crossing)
        return jnp.where(keeps, x, moved)

    def pick(x):
        return lax.dynamic_index_in_dim(x, section, 0, keepdims=False)

    order_row = pick(group_order).astype(LOW)
    order_row = jnp.broadcast_to(
        jnp.concatenate([order_row, jnp.zeros((model_width - count,), LOW)])[None], (16, model_width)
    )
    packed = reshard(jnp.concatenate([pick(tokens), order_row], axis=0))
    current = packed[:segment].astype(F32)
    blocks_at = packed[segment, :count].astype(jnp.int32)
    upstream = reshard(pick(cotangent))
    seat = replica * half + lax.rem(shard, half)
    key_pos = (
        blocks_at[:, None] * segment + jnp.arange(segment, dtype=jnp.int32)[None, :]
    )
    unit_ids = plan.units * seat + jnp.arange(plan.units, dtype=jnp.int32)
    unit_part = lax.rem(unit_ids, plan.splits)
    parts_pos = key_pos.reshape(count, plan.splits, plan.part)
    query_pos = jnp.stack(
        [
            lax.dynamic_index_in_dim(parts_pos, unit_part[u], 1, keepdims=False).reshape(-1)
            for u in range(plan.units)
        ]
    )
    place = Bag(
        slot=unit_ids // plan.splits - (plan.units * seat) // plan.splits,
        query_pos=query_pos,
        key_pos=key_pos.reshape(-1),
    )

    small = jnp.concatenate(
        [
            norm_gains[0], norm_biases[0], qv_bias[0], out_bias, fc_bias.reshape(4, rows), proj_bias,
        ],
        axis=0,
    ).reshape(-1)
    small_rows = -(-small.shape[0] // (16 * model_width)) * 16
    small = jnp.concatenate(
        [small, jnp.zeros((small_rows * model_width - small.shape[0],), LOW)]
    ).reshape(small_rows, model_width)
    qkv = w_qkv[0]
    attn_sets = (
        jnp.concatenate([qkv[:, :model_width], qkv[:, model_width : 2 * model_width], small], axis=0),
        jnp.concatenate([qkv[:, 2 * model_width :], w_out[0], small], axis=0),
    )
    fc_blocks = w_fc[0].reshape(rows, 4, model_width).transpose(1, 0, 2).reshape(4 * rows, model_width)
    ffn_sets = (fc_blocks, w_proj[0])

    def gathered(sets):
        own = jnp.where(replica == 0, sets[0], sets[1])
        other_layer = swap(own, SECTION)
        layers = []
        for layer in range(2):
            chunk = jnp.where(section == layer, own, other_layer)
            chunks = ring_gather(chunk, count)
            buffer = jnp.zeros((2, count) + chunk.shape, LOW)
            for offset in range(count):
                twin = swap(chunks[offset], REPLICA)
                at = owner(offset)
                buffer = lax.dynamic_update_slice(buffer, chunks[offset][None, None], (replica, at, 0, 0))
                buffer = lax.dynamic_update_slice(buffer, twin[None, None], (1 - replica, at, 0, 0))
            layers.append(buffer)
        return layers

    attn = gathered(attn_sets)
    ffn = gathered(ffn_sets)

    def block(buffer, which, at):
        return buffer[which, :, at * rows : (at + 1) * rows].reshape(count * rows, model_width)

    def unpacked(layer):
        a, f = attn[layer], ffn[layer]
        vec = a[0, :, 2 * rows :].reshape(count, -1)[:, : 12 * rows].reshape(count, 12, rows).astype(F32)

        def row(i):
            return vec[:, i].reshape(-1)

        return Bag(
            q=block(a, 0, 0), k=block(a, 0, 1), v=block(a, 1, 0), o=block(a, 1, 1),
            fc=jnp.concatenate([block(f, 0, i) for i in range(4)], axis=1),
            proj=f[1].reshape(count * 4 * rows, model_width),
            gains=(row(0), row(1)), offsets=(row(2), row(3)), q_bias=row(4), v_bias=row(5),
            out_bias=row(6), fc_bias=vec[:, 7:11].reshape(-1), proj_bias=row(11),
        )

    weights = [unpacked(0), unpacked(1)]
    outputs, states = [], []
    for layer in range(2):
        output, saved = layer_forward(current, weights[layer], plan, place)
        outputs.append(output.astype(LOW))
        states.append(saved)
        current = outputs[-1].astype(F32)
    grad_inputs, totals = [None, None], [None, None]
    arriving = upstream.astype(F32)

    def pieces(attn_rows, layer_grads, which):
        pass

    def blocks_of(grad, cols):
        return grad.astype(LOW).reshape(count, -1, cols)

    def scattered(sets):
        own = jnp.where(replica == 0, sets[0], sets[1])
        other = jnp.where(replica == 0, sets[1], sets[0])
        paired = add_low(own, swap(other, REPLICA))
        return ring_scatter(
            lambda k: lax.dynamic_index_in_dim(paired, owner(k), 0, keepdims=False),
            paired.shape[1], count,
        )

    scattered_attn, scattered_ffn = [None, None], [None, None]
    for layer in (1, 0):
        grad_input, grads = layer_backward(arriving, states[layer], weights[layer], plan, place)
        grad_inputs[layer] = grad_input
        arriving = grad_input.astype(LOW).astype(F32)
        vec = jnp.concatenate(
            [
                grads.gains, grads.offsets, grads.qv_bias, grads.out_bias[None],
            ], axis=0,
        ).reshape(7, count, rows).transpose(1, 0, 2)
        vec = jnp.concatenate(
            [vec, grads.fc_bias.reshape(count, 4, rows), grads.proj_bias.reshape(count, 1, rows)],
            axis=1,
        ).astype(LOW).reshape(count, 12 * rows)
        vec = jnp.concatenate(
            [vec, jnp.zeros((count, small_rows * model_width - 12 * rows), LOW)], axis=1
        ).reshape(count, small_rows, model_width)
        scattered_ffn[layer] = scattered(
            (
                jnp.concatenate(
                    [blocks_of(grads.fc[:, i * model_width : (i + 1) * model_width], model_width) for i in range(4)],
                    axis=1,
                ),
                blocks_of(grads.proj, model_width),
            )
        )
        scattered_attn[layer] = scattered(
            (
                jnp.concatenate([blocks_of(grads.q, model_width), blocks_of(grads.k, model_width), vec], axis=1),
                jnp.concatenate([blocks_of(grads.v, model_width), blocks_of(grads.o, model_width), vec], axis=1),
            )
        )

    def finished(parts):
        own = jnp.where(section == 0, parts[0], parts[1])
        other = jnp.where(section == 0, parts[1], parts[0]).astype(LOW)
        total = (own + swap(other, SECTION).astype(F32)).astype(LOW)
        twin = swap(total, REPLICA)
        return (
            jnp.where(replica == 0, total, twin).astype(F32),
            jnp.where(replica == 0, twin, total).astype(F32),
        )

    ffn_total = finished(scattered_ffn)
    attn_total = finished(scattered_attn)
    fc_grad = ffn_total[0].reshape(4, rows, model_width).transpose(1, 0, 2).reshape(rows, 4 * model_width)
    proj_grad = ffn_total[1]
    qkv_grad = jnp.concatenate(
        [attn_total[0][:rows], attn_total[0][rows : 2 * rows], attn_total[1][:rows]], axis=1
    )
    out_grad = attn_total[1][rows : 2 * rows]
    vec = attn_total[0][2 * rows :].reshape(-1)[: 12 * rows].reshape(12, rows)

    def by_owner(per_layer):
        low = [reshard(v.astype(LOW)) for v in per_layer]
        own = jnp.where(section == 0, low[0], low[1])
        other = jnp.where(section == 0, low[1], low[0])
        got = swap(other, SECTION)
        return jnp.stack([jnp.where(section == 0, own, got), jnp.where(section == 0, got, own)])[None]

    acts = by_owner(outputs)
    in_grads = by_owner(grad_inputs).astype(F32)
    return (
        acts,
        in_grads,
        vec[0:2][None],
        vec[2:4][None],
        qkv_grad[None],
        vec[4:6][None],
        out_grad[None],
        vec[6][None],
        fc_grad[None],
        vec[7:11].reshape(1, 4 * rows),
        proj_grad[None],
        vec[11][None],
    )


ANY = pl.BlockSpec(memory_space=pl.ANY)
VMEM = pl.BlockSpec(memory_space=pltpu.VMEM)
SMEM = pl.BlockSpec(memory_space=pltpu.SMEM)
PAIR = 2 * HEAD
VMEM_LIMIT = 24 * 2**20
MEMORY_RATE = 3.69e6


def mm(a, b):
    return lax.dot_general(a, b, (((1,), (0,)), ((), ())), preferred_element_type=F32)


def mm_nt(a, b):
    return lax.dot_general(a, b, (((1,), (1,)), ((), ())), preferred_element_type=F32)


def mm_tn(a, b):
    return lax.dot_general(a, b, (((0,), (0,)), ((), ())), preferred_element_type=F32)


def call(body, micros, operands, specs, outs, scratch, saves=(), keep=True):
    outs = list(outs) + (list(saves) if keep else [])
    spare = [] if keep else [pltpu.VMEM(shape, kind) for shape, kind, _ in saves]
    return pl.pallas_call(
        body,
        in_specs=specs,
        out_specs=[ANY if space is True else VMEM for _, _, space in outs],
        out_shape=[
            {None: jax.ShapeDtypeStruct, True: pltpu.HBM, False: pltpu.VMEM}[space](shape, kind)
            for shape, kind, space in outs
        ],
        scratch_shapes=spare + scratch,
        compiler_params=pltpu.CompilerParams(vmem_limit_bytes=VMEM_LIMIT),
        cost_estimate=pl.CostEstimate(
            flops=0, bytes_accessed=int(micros * MEMORY_RATE), transcendentals=0
        ),
    )(*operands)


SEATS = 4


def low_lanes(shape):
    return lax.broadcasted_iota(jnp.int32, shape, len(shape) - 1) % PAIR < HEAD


def turn(tile):
    return pltpu.roll(tile, HEAD, 1)


def tiles_of(values, seat):
    at = 3 * seat // 2
    pair, single = (at, at + 1) if seat % 2 == 0 else (at + 1, at)
    return [values[:, t * PAIR : (t + 1) * PAIR] for t in (pair, single)]


def join(first, second, seat):
    low = low_lanes(first.shape)
    if seat % 2 == 0:
        return jnp.where(low, first, turn(second))
    return jnp.where(low, turn(first), second)


def fold(tile, seat):
    half = tile.shape[0] // 2
    return join(tile[:half], tile[half:], seat)


def split(tile, seat):
    low = low_lanes(tile.shape)
    turned = turn(tile)
    if seat % 2 == 0:
        return jnp.where(low, tile, 0.0), jnp.where(low, turned, 0.0)
    return jnp.where(low, 0.0, turned), jnp.where(low, 0.0, tile)


def unfold(tile, seat):
    return jnp.concatenate(split(tile, seat), axis=0)


def whole_rows(pairs, singles):
    tiles = []
    for even in range(0, SEATS, 2):
        tiles += [pairs[even], singles[even] + singles[even + 1], pairs[even + 1]]
    return jnp.concatenate(tiles, axis=1)


def start_all(copies):
    for copy in copies:
        copy.start()
    return copies


def wait_all(copies):
    for copy in copies:
        copy.wait()


def to_seats(scratch, outs, idx, count, sems):
    return start_all(
        [
            pltpu.make_async_copy(scratch.at[idx[count + 2 + k]], outs[k], sems.at[k])
            for k in range(SEATS)
        ]
    )


def from_seats(ins, scratch, idx, count, sems):
    return start_all(
        [
            pltpu.make_async_copy(ins[k], scratch.at[idx[count + 2 + k]], sems.at[k])
            for k in range(SEATS)
        ]
    )


def in_order(refs, scratch, at, sems, outward):
    copies = []
    for k in range(SEATS):
        for p in range(2):
            ends = refs[k].at[p], scratch.at[at[2 * k + p]]
            if outward:
                ends = ends[::-1]
            copies.append(pltpu.make_async_copy(*ends, sems.at[2 * k + p]))
    return start_all(copies)


def block_rows(segment):
    return 4 * segment + segment // 2


class Loader:
    def __init__(self, sems):
        self.sems = sems
        self.used = 0
        self.waits = {}

    def load(self, idx, count, own, twin, targets):
        slots = {}
        for which in (0, 1):
            for at, (offset, rows, ref, key) in enumerate(targets[which]):
                for k in range(count):
                    slots[which, at, k] = self.used
                    self.waits.setdefault(key, []).append((ref, self.used))
                    self.used += 1
        for rep in (0, 1):
            @pl.when(idx[count] == rep)
            def _():
                for which in (0, 1):
                    chunks = own if which == rep else twin
                    for at, (offset, rows, ref, key) in enumerate(targets[which]):
                        for k in range(count):
                            if len(chunks) == 1:
                                chunk, place = chunks[0].at[k], k
                            else:
                                chunk, place = chunks[k], idx[k]
                            pltpu.make_async_copy(
                                chunk.at[pl.ds(offset, rows)], ref.at[place],
                                self.sems.at[slots[which, at, k]],
                            ).start()

    def wait(self, key):
        for ref, slot in self.waits[key]:
            pltpu.make_async_copy(ref.at[0], ref.at[0], self.sems.at[slot]).wait()


def flat(ref):
    return ref[...].reshape(-1, ref.shape[-1])


def centre(values):
    average = jnp.mean(values, axis=-1, keepdims=True)
    centred = values - average
    scale = lax.rsqrt(jnp.mean(centred * centred, axis=-1, keepdims=True) + EPSILON)
    return centred * scale, scale


def centre_back(grad, hat, scale):
    return scale * (
        grad
        - jnp.mean(grad, axis=-1, keepdims=True)
        - hat * jnp.mean(grad * hat, axis=-1, keepdims=True)
    )


GELU_A, GELU_B = math.sqrt(2 / math.pi), 0.044715


NOTE = 16


def note_rows(small, width):
    rows = small.shape[1]
    hidden = jnp.pad(small[7:11].reshape(1, 4 * rows), ((0, 0), (0, width - 4 * rows)))
    others = jnp.concatenate([small[:7], small[11:]], axis=0)
    others = jnp.pad(others, ((0, NOTE - 9), (0, width - rows)))
    return jnp.concatenate([others, hidden], axis=0)


def read_notes(notes, count, width):
    rows = width // count
    total = None
    hidden = []
    for s in range(count):
        note = notes[s].astype(F32)
        moved = pltpu.roll(note, s * rows, 1) if s else note
        total = moved if total is None else total + moved
        at = (4 * rows * s) % width
        hidden.append(pltpu.roll(note[8:], at, 1)[NOTE - 9 :] if at else note[8:][NOTE - 9 :])
    per = width // (4 * rows)
    lines = [sum(hidden[b * per + i] for i in range(per)) for b in range(4)]
    return [total[:8]] + lines


def flatten(rings):
    chunks = [chunk for lists in rings for chunks in lists for chunk in chunks]
    return [pltpu.with_memory_space_constraint(chunk, pltpu.HBM) for chunk in chunks]


def load_projections(loader, idx, count, rows, chunks, wq, wk, wv, notes):
    first = [(0, rows, wq, 0), (rows, NOTE, notes, 3)]
    loader.load(idx, count, chunks[:count], chunks[count : 2 * count], [first, [(0, rows, wv, 2)]])
    loader.load(idx, count, chunks[2 * count : 3 * count], chunks[3 * count :], [[(0, rows, wk, 1)], []])


def load_output(loader, idx, count, rows, chunks, wo):
    loader.load(idx, count, chunks[2 * count : 3 * count], chunks[3 * count : 4 * count], [[], [(0, rows, wo, 5)]])


def load_feed(loader, idx, count, rows, chunks, wf, wp):
    for pair in range(2):
        own, twin = [chunks[(2 * pair + i) * count : (2 * pair + i + 1) * count] for i in range(2)]
        loader.load(
            idx, count, own, twin,
            [
                [(i * rows, rows, wf.at[2 * pair + i], 2 * pair + i) for i in range(2)],
                [(i * rows, rows, wp.at[:, 2 * pair + i], 4) for i in range(2)],
            ],
        )


def project_kernel(count, segment, inputs, hopped, attn, idx):
    width = inputs[0].shape[1]
    rows = width // count
    given = [] if hopped is None else [hopped]
    tall = block_rows(segment)
    loading = hopped is None

    def body(idx, first, second, *rest):
        arrived, rest = rest[: len(given)], rest[len(given) :]
        if loading:
            chunks, rest = rest[: 4 * count], rest[4 * count :]
            outs, (chosen, wq, wk, wv, vec, blocks, normed, notes, sems, out_sems) = rest[:SEATS], rest[SEATS:]
            loader = Loader(sems)
            load_projections(loader, idx, count, rows, chunks, wq, wk, wv, notes)
        else:
            (wq, wk, wv, vec), rest = rest[:4], rest[4:]
            outs, (chosen, normed, blocks, out_sems) = rest[:SEATS], rest[SEATS:]
        values = jnp.concatenate([first[:segment], second[:segment]], axis=0).astype(F32)
        if given:
            values = jnp.where(idx[count + 1] == 0, values, arrived[0][...].astype(F32))
        chosen[...] = values.astype(LOW)
        hat, _ = centre(values)
        if loading:
            loader.wait(3)
            lines = read_notes([notes[s] for s in range(count)], count, width)
            vec[0:8] = lines[0]
            for b in range(4):
                vec[8 + b : 9 + b] = lines[1 + b]
        low = (hat * vec[0:1] + vec[2:3]).astype(LOW)
        normed[...] = low
        if loading:
            loader.wait(0)
        queries = mm(low, flat(wq)) + vec[4:5]
        if loading:
            loader.wait(1)
        keys = mm(low, flat(wk))
        if loading:
            loader.wait(2)
        values = mm(low, flat(wv)) + vec[5:6]
        for d in range(SEATS):
            (qp, qs), (kp, ks), (vp, vs) = [tiles_of(x, d) for x in (queries, keys, values)]
            both = join(qs, ks, d)
            for p in range(2):
                span = slice(p * segment, (p + 1) * segment)
                for at, tile in enumerate((qp, kp, vp, both)):
                    blocks[d, p, at * segment : (at + 1) * segment] = tile[span].astype(LOW)
                blocks[d, p, 4 * segment :] = fold(vs[span], d).astype(LOW)
        wait_all(to_seats(blocks, outs, idx, count, out_sems))

    weight = ((count, rows, width), LOW, False)
    tokens = ((2 * segment, width), LOW, None)
    stay = ((2 * segment, width), LOW, False)
    blocks = pltpu.VMEM((SEATS, 2, tall, PAIR), LOW)
    sent = [((2, tall, PAIR), LOW, True)] * SEATS
    if loading:
        out = call(
            body, 7, [idx, *inputs, *flatten(attn)], [SMEM, VMEM, VMEM] + [ANY] * (4 * count),
            sent + [tokens, weight, weight, weight, ((12, width), F32, None)],
            [
                blocks, pltpu.VMEM((2 * segment, width), LOW), pltpu.VMEM((count, NOTE, width), LOW),
                pltpu.SemaphoreType.DMA((4 * count,)), pltpu.SemaphoreType.DMA((SEATS,)),
            ],
        )
        return out[:SEATS], out[SEATS], None, out[SEATS + 1 :]
    out = call(
        body, 7, [idx, *inputs, *given, *attn], [SMEM] + [VMEM] * (2 + len(given) + 4),
        sent + [stay, stay], [blocks, pltpu.SemaphoreType.DMA((SEATS,))],
    )
    return out[:SEATS], out[SEATS], out[SEATS + 1], attn


def read_heads(blocks, segment):
    def joined(at):
        return jnp.concatenate(
            [blocks[i, at * segment : (at + 1) * segment] for i in range(blocks.shape[0])], axis=0
        )

    third = joined(3).astype(F32)
    low = low_lanes(third.shape)
    values = [unfold(blocks[i, 4 * segment :].astype(F32), 0) for i in range(blocks.shape[0])]
    return (
        (joined(0), joined(1), joined(2)),
        (
            jnp.where(low, third, 0.0).astype(LOW), turn(third).astype(LOW),
            jnp.concatenate(values, axis=0).astype(LOW),
        ),
    )


def stacked(rows):
    low = low_lanes(rows.shape)
    zero = jnp.zeros_like(rows)
    return jnp.concatenate([jnp.where(low, rows, zero), jnp.where(low, zero, rows)], axis=0)


def unstacked(rows):
    half = rows.shape[0] // 2
    return jnp.where(low_lanes((half, PAIR)), rows[:half], rows[half:])


def earlier(rows, step):
    row = lax.broadcasted_iota(jnp.int32, (rows, step), 0) % step
    return lax.broadcasted_iota(jnp.int32, (rows, step), 1) <= row


def attend_kernel(count, segment, arrived, at, keep):
    length, step = count * segment, 2 * segment
    tall = block_rows(segment)
    short = segment + segment // 2

    def body(at, *rest):
        ins, outs, rest = rest[:SEATS], rest[SEATS : 2 * SEATS], rest[2 * SEATS :]
        attended, total, blocks, backs, sems, out_sems = rest
        wait_all(in_order(ins, blocks, at, sems, False))
        heads = read_heads(blocks, segment)
        for i in range(length // step):
            span = slice(i * step, (i + 1) * step)
            logs = []
            for g, (queries, keys, values) in enumerate(heads):
                query = queries[span] * SCALING
                if g == 0:
                    query = stacked(query)
                mask = earlier(query.shape[0], step)
                near = jnp.where(mask, mm_nt(query, keys[span]), FLOOR)
                highest = jnp.max(near, axis=-1, keepdims=True)
                if i > 0:
                    far = mm_nt(query, keys[: i * step])
                    highest = jnp.maximum(highest, jnp.max(far, axis=-1, keepdims=True))
                    far = jnp.exp(far - highest)
                near = jnp.exp(near - highest)
                denominator = jnp.sum(near, axis=-1, keepdims=True)
                result = mm(near.astype(LOW), values[span])
                if i > 0:
                    denominator += jnp.sum(far, axis=-1, keepdims=True)
                    result += mm(far.astype(LOW), values[: i * step])
                result = result * (1.0 / denominator)
                log = highest + jnp.log(denominator)
                if g == 0:
                    result = unstacked(result)
                    logs += [log[:step], log[step:]]
                else:
                    logs.append(log)
                attended[g, span] = result
                for p in range(2):
                    tile = result[p * segment : (p + 1) * segment]
                    if g == 0:
                        backs[2 * i + p, :segment] = tile.astype(LOW)
                    else:
                        backs[2 * i + p, segment:] = fold(tile, 0).astype(LOW)
            lane = lax.broadcasted_iota(jnp.int32, (step, PAIR), 1)
            total[span] = jnp.where(lane == 0, logs[0], jnp.where(lane == 1, logs[1], logs[2]))
        wait_all(in_order(outs, backs, at, out_sems, True))

    return call(
        body, 9, [at, *arrived], [SMEM] + [ANY] * SEATS,
        [((2, short, PAIR), LOW, True)] * SEATS,
        [
            pltpu.VMEM((count, tall, PAIR), LOW), pltpu.VMEM((count, short, PAIR), LOW),
            pltpu.SemaphoreType.DMA((2 * SEATS,)), pltpu.SemaphoreType.DMA((2 * SEATS,)),
        ],
        [((2, length, PAIR), F32, False), ((length, PAIR), F32, False)], keep,
    )


def attend_back_kernel(count, segment, arrived, grads, attended, total, at, ties):
    length, step = count * segment, 2 * segment
    tall = block_rows(segment)
    short = segment + segment // 2

    def body(at, attended, total, *rest):
        ins, grad_ins, rest = rest[:SEATS], rest[SEATS : 2 * SEATS], rest[2 * SEATS + len(ties) :]
        outs, rest = rest[:SEATS], rest[SEATS:]
        blocks, grads, backs, of_keys, of_values, sems, grad_sems, out_sems = rest
        first = in_order(ins, blocks, at, sems, False)
        second = in_order(grad_ins, grads, at, grad_sems, False)
        wait_all(first)
        heads = read_heads(blocks, segment)
        wait_all(second)
        for i in reversed(range(length // step)):
            span = slice(i * step, (i + 1) * step)
            third = None
            for g, (queries, keys, values) in enumerate(heads):
                query = queries[span] * SCALING
                if g == 0:
                    grad = jnp.concatenate([grads[2 * i + p, :segment] for p in range(2)], axis=0)
                    dots = grad.astype(F32) * attended[0, span]
                    low = low_lanes(dots.shape)
                    dots = jnp.concatenate([jnp.where(low, dots, 0.0), jnp.where(low, 0.0, dots)], axis=0)
                    log = jnp.concatenate([total[span, 0:1], total[span, 1:2]], axis=0)
                    query, grad = stacked(query), stacked(grad)
                else:
                    grad = jnp.concatenate(
                        [unfold(grads[2 * i + p, segment:].astype(F32), 0) for p in range(2)], axis=0
                    )
                    dots = grad * attended[1, span]
                    grad = grad.astype(LOW)
                    log = total[span, 2:3]
                dots = jnp.sum(dots, axis=-1, keepdims=True)
                parts = [(span, True)] + ([(slice(0, i * step), False)] if i > 0 else [])
                of_queries = None
                for keyed, near in parts:
                    weights = jnp.exp(mm_nt(query, keys[keyed]) - log)
                    if near:
                        weights = jnp.where(earlier(query.shape[0], step), weights, 0.0)
                    grad_scores = (weights * (mm_nt(grad, values[keyed]) - dots)).astype(LOW)
                    term = mm(grad_scores, keys[keyed])
                    of_queries = term if of_queries is None else of_queries + term
                    key_term = mm_tn(grad_scores, query)
                    value_term = mm_tn(weights.astype(LOW), grad)
                    if i == length // step - 1:
                        of_keys[g, keyed] = key_term
                        of_values[g, keyed] = value_term
                    else:
                        of_keys[g, keyed] += key_term
                        of_values[g, keyed] += value_term
                of_queries = of_queries * SCALING
                if g == 0:
                    of_queries = unstacked(of_queries)
                    for p in range(2):
                        backs[2 * i + p, :segment] = of_queries[p * segment : (p + 1) * segment].astype(LOW)
                else:
                    third = of_queries
            low = low_lanes((segment, PAIR))
            for p in range(2):
                own = slice(i * step + p * segment, i * step + (p + 1) * segment)
                block = backs.at[2 * i + p]
                block[segment : 2 * segment] = of_keys[0, own].astype(LOW)
                block[2 * segment : 3 * segment] = of_values[0, own].astype(LOW)
                block[3 * segment : 4 * segment] = join(
                    third[p * segment : (p + 1) * segment], of_keys[1, own], 0
                ).astype(LOW)
                block[4 * segment :] = fold(of_values[1, own], 0).astype(LOW)
        wait_all(in_order(outs, backs, at, out_sems, True))

    return call(
        body, 14, [at, attended, total, *arrived, *grads, *ties],
        [SMEM, VMEM, VMEM] + [ANY] * (2 * SEATS + len(ties)),
        [((2, tall, PAIR), LOW, True)] * SEATS,
        [
            pltpu.VMEM((count, tall, PAIR), LOW), pltpu.VMEM((count, short, PAIR), LOW),
            pltpu.VMEM((count, tall, PAIR), LOW), pltpu.VMEM((2, length, PAIR), F32),
            pltpu.VMEM((2, length, PAIR), F32), pltpu.SemaphoreType.DMA((2 * SEATS,)),
            pltpu.SemaphoreType.DMA((2 * SEATS,)), pltpu.SemaphoreType.DMA((2 * SEATS,)),
        ],
    )


def feed_rows(mid, vec, wf, wp, active, slope, wait):
    width = mid.shape[1]
    hat, scale = centre(mid)
    low = (hat * vec[1:2] + vec[3:4]).astype(LOW)
    for b in range(4):
        wait(b)
        span = slice(b * width, (b + 1) * width)
        u = mm(low, flat(wf.at[b])) + vec[8 + b : 9 + b]
        square = u * u
        t = jnp.tanh(u * (GELU_A + GELU_A * GELU_B * square))
        half = 0.5 + 0.5 * t
        active[:, span] = (u * half).astype(LOW)
        if slope is not None:
            slope[:, span] = (
                half + u * (0.5 - 0.5 * t * t) * (GELU_A + 3.0 * GELU_A * GELU_B * square)
            ).astype(LOW)
    wait(4)
    return low, hat, scale, (mid + mm(active[...], flat(wp)) + vec[7:8]).astype(LOW)


def feed_kernel(count, segment, returned, inputs, vec, rings, idx):
    width = inputs.shape[1]
    rows, tokens = width // count, 2 * segment
    short = segment + segment // 2

    def body(idx, x, vec, *rest):
        back, chunks, rest = rest[:SEATS], rest[SEATS : SEATS + 8 * count], rest[SEATS + 8 * count :]
        output, wo, wf, wp, blocks, active, sems, in_sems = rest
        loader = Loader(sems)
        copies = from_seats(back, blocks, idx, count, in_sems)
        load_output(loader, idx, count, rows, chunks, wo)
        load_feed(loader, idx, count, rows, chunks[4 * count :], wf, wp)
        wait_all(copies)
        low = read_returned(blocks, segment).astype(LOW)
        loader.wait(5)
        mid = x[...].astype(F32) + mm(low, flat(wo)) + vec[6:7]
        output[...] = feed_rows(mid, vec, wf, wp, active, None, loader.wait)[3]

    return call(
        body, 10, [idx, inputs, vec, *returned, *flatten(rings)],
        [SMEM, VMEM, VMEM] + [ANY] * (SEATS + 8 * count),
        [
            ((tokens, width), LOW, None), ((count, rows, width), LOW, False),
            ((4, count, rows, width), LOW, False), ((count, 4, rows, width), LOW, False),
        ],
        [
            pltpu.VMEM((SEATS, 2, short, PAIR), LOW), pltpu.VMEM((tokens, 4 * width), LOW),
            pltpu.SemaphoreType.DMA((9 * count,)), pltpu.SemaphoreType.DMA((SEATS,)),
        ],
    )


def read_returned(blocks, segment):
    pairs, singles = [], []
    for d in range(SEATS):
        pairs.append(jnp.concatenate([blocks[d, p, :segment].astype(F32) for p in range(2)], axis=0))
        singles.append(
            jnp.concatenate([unfold(blocks[d, p, segment:].astype(F32), d) for p in range(2)], axis=0)
        )
    return whole_rows(pairs, singles)


def feed_back_rows(wide, hat, scale, slope, vec, wo, wf, wp, gh, sums, blocks, segment):
    width = wide.shape[1]
    branch = wide.astype(LOW)
    weight = flat(wp)
    back = jnp.zeros(wide.shape, F32)
    for b in range(4):
        span = slice(b * width, (b + 1) * width)
        ga = mm_nt(branch, weight[span])
        low = (ga * slope[:, span].astype(F32)).astype(LOW)
        if sums is not None:
            gh[:, span] = low
            sums[3 + b : 4 + b] = jnp.sum(low.astype(F32), axis=0, keepdims=True)
        back += mm_nt(low, flat(wf.at[b]))
    total = wide + centre_back(back * vec[1:2], hat, scale)
    low = total.astype(LOW)
    values = mm_nt(low, flat(wo))
    for d in range(SEATS):
        pair, single = tiles_of(values, d)
        for p in range(2):
            part = slice(p * segment, (p + 1) * segment)
            blocks[d, p, :segment] = pair[part].astype(LOW)
            blocks[d, p, segment:] = fold(single[part], d).astype(LOW)
    if sums is not None:
        sums[0:1] = jnp.sum(back * hat, axis=0, keepdims=True)
        sums[1:2] = jnp.sum(back, axis=0, keepdims=True)
        sums[2:3] = jnp.sum(low.astype(F32), axis=0, keepdims=True)
        sums[7:8] = jnp.sum(wide, axis=0, keepdims=True)
    return total, low


def turn_kernel(count, segment, returned, inputs, vec, weights, grads, idx):
    width = inputs.shape[1]
    tokens = 2 * segment
    short = segment + segment // 2

    def body(idx, x, vec, wo, wf, wp, first, second, *rest):
        back, outs, rest = rest[:SEATS], rest[SEATS : 2 * SEATS], rest[2 * SEATS :]
        output, attended, middle, normed, slope, active, grad_middle, blocks, in_sems, out_sems = rest
        wait_all(from_seats(back, blocks, idx, count, in_sems))
        low = read_returned(blocks, segment).astype(LOW)
        attended[...] = low
        mid = x[...].astype(F32) + mm(low, flat(wo)) + vec[6:7]
        middle[...] = mid
        normed[...], hat, scale, output[...] = feed_rows(
            mid, vec, wf, wp, active, slope, lambda key: None
        )
        wide = jnp.concatenate([first[...], second[...]], axis=0).astype(F32)
        grad_middle[...] = feed_back_rows(
            wide, hat, scale, slope, vec, wo, wf, wp, None, None, blocks, segment
        )[0]
        wait_all(to_seats(blocks, outs, idx, count, out_sems))

    rows = ((tokens, width), LOW, False)
    return call(
        body, 10, [idx, inputs, vec, *weights, *grads, *returned],
        [SMEM] + [VMEM] * 7 + [ANY] * SEATS,
        [((2, short, PAIR), LOW, True)] * SEATS
        + [
            ((tokens, width), LOW, None), rows, ((tokens, width), F32, False), rows,
            ((tokens, 4 * width), LOW, False), ((tokens, 4 * width), LOW, False),
            ((tokens, width), F32, False),
        ],
        [
            pltpu.VMEM((SEATS, 2, short, PAIR), LOW), pltpu.SemaphoreType.DMA((SEATS,)),
            pltpu.SemaphoreType.DMA((SEATS,)),
        ],
    )


def feed_back_kernel(count, segment, grads, hopped, saved, weights, idx):
    width = grads[0].shape[1]
    tokens = 2 * segment
    short = segment + segment // 2

    def body(idx, first, second, hopped, middle, slope, vec, wo, wf, wp, *rest):
        outs, rest = rest[:SEATS], rest[SEATS:]
        grad_middle, mine, theirs, sums, grad_out, blocks, gh, out_sems = rest
        wide = jnp.concatenate([first[...], second[...]], axis=0).astype(F32)
        wide = jnp.where(idx[count + 1] == 1, wide, hopped[...].astype(F32))
        hat, scale = centre(middle[...])
        grad_middle[...], grad_out[...] = feed_back_rows(
            wide, hat, scale, slope, vec, wo, wf, wp, gh, sums, blocks, segment
        )
        copies = to_seats(blocks, outs, idx, count, out_sems)
        branch = wide.astype(LOW)

        def part(values, core):
            half = values.shape[1] // 2
            return values[:, core * half : (core + 1) * half]

        def fill(rep):
            for ref, core in ((mine, rep), (theirs, 1 - rep)):
                ref[:, : 2 * width] = part(gh, core)
                ref[:, 2 * width :] = part(branch, core)

        for rep in range(2):
            pl.when(idx[count] == rep)(functools.partial(fill, rep))

        wait_all(copies)

    return call(
        body, 14,
        [
            idx, *grads, hopped, saved.middle, saved.slope, saved.vec,
            *weights,
        ],
        [SMEM] + [VMEM] * 9,
        [((2, short, PAIR), LOW, True)] * SEATS
        + [
            ((tokens, width), F32, None), ((tokens, 5 * width // 2), LOW, None),
            ((tokens, 5 * width // 2), LOW, None), ((8, width), F32, None), ((tokens, width), LOW, None),
        ],
        [
            pltpu.VMEM((SEATS, 2, short, PAIR), LOW), pltpu.VMEM((tokens, 4 * width), LOW),
            pltpu.SemaphoreType.DMA((SEATS,)),
        ],
    )


def project_back_kernel(count, segment, returned, grad_middle, grad_out, saved, weights, idx, keep):
    tokens, width = grad_middle.shape
    rows = width // count
    tall = block_rows(segment)
    kept = [grad_out] if keep else []

    def body(idx, grad_middle, x, vec, *rest):
        held, rest = rest[: len(kept)], rest[len(kept) :]
        back, rest = rest[:SEATS], rest[SEATS:]
        (wq, wk, wv), rest = rest[:3], rest[3:]
        grad_low, grad_in, mine, theirs, sums, blocks, in_sems = rest
        copies = from_seats(back, blocks, idx, count, in_sems)
        hat, scale = centre(x[...].astype(F32))
        wait_all(copies)
        pairs, singles = [[], [], []], [[], [], []]
        for d in range(SEATS):
            for at in range(3):
                pairs[at].append(
                    jnp.concatenate(
                        [blocks[d, p, at * segment : (at + 1) * segment].astype(F32) for p in range(2)], axis=0
                    )
                )
            both = [split(blocks[d, p, 3 * segment : 4 * segment].astype(F32), d) for p in range(2)]
            for at in range(2):
                singles[at].append(jnp.concatenate([b[at] for b in both], axis=0))
            singles[2].append(
                jnp.concatenate([unfold(blocks[d, p, 4 * segment :].astype(F32), d) for p in range(2)], axis=0)
            )
        gq, gk, gv = [whole_rows(a, b).astype(LOW) for a, b in zip(pairs, singles)]
        total = mm_nt(gq, flat(wq))
        total += mm_nt(gk, flat(wk))
        total += mm_nt(gv, flat(wv))
        result = grad_middle[...] + centre_back(total * vec[0:1], hat, scale)
        grad_low[...] = result.astype(LOW)
        if not keep:
            return
        grad_in[...] = result
        sums[0:1] = jnp.sum(total * hat, axis=0, keepdims=True)
        sums[1:2] = jnp.sum(total, axis=0, keepdims=True)
        sums[2:3] = jnp.sum(gq.astype(F32), axis=0, keepdims=True)
        sums[3:4] = jnp.sum(gv.astype(F32), axis=0, keepdims=True)
        sums[4:8] = jnp.zeros((4, width), F32)
        (grad_out,) = held

        def fill(first, second):
            first[:, :width] = gq
            first[:, width:] = gk
            second[:, :width] = gv
            second[:, width:] = grad_out[...]

        @pl.when(idx[count] == 0)
        def _():
            fill(mine, theirs)

        @pl.when(idx[count] == 1)
        def _():
            fill(theirs, mine)

    return call(
        body, 8, [idx, grad_middle, saved.inputs, saved.vec, *kept, *returned, *weights],
        [SMEM] + [VMEM] * (3 + len(kept)) + [ANY] * SEATS + [VMEM] * 3,
        [((tokens, width), LOW, None)],
        [
            pltpu.VMEM((SEATS, 2, tall, PAIR), LOW), pltpu.SemaphoreType.DMA((SEATS,)),
        ],
        [
            ((tokens, width), F32, None), ((tokens, 2 * width), LOW, None),
            ((tokens, 2 * width), LOW, None), ((8, width), F32, None),
        ],
        keep,
    )


def send_out(scratch, pieces, idx, sems, start):
    for at, (out, to, rows, base, stride, k) in enumerate(pieces):
        source = pl.ds(pl.multiple_of(base + idx[k] * stride, 16), rows)
        copy = pltpu.make_async_copy(scratch.at[source], out.at[pl.ds(to, rows)], sems.at[at])
        copy.start() if start else copy.wait()


def rows_of(refs, span=slice(None)):
    return jnp.concatenate([ref[:, span] for ref in refs], axis=0)


def ffn_terms_kernel(count, normed, active, late, idx):
    width = normed[0].shape[1]
    rows, half = width // count, width // 2

    def body(idx, *rest):
        normed, active, late, rest = rest[:2], rest[2:4], rest[4:6], rest[6:]
        outs, (inward, outward, sems) = rest[: 2 * count], rest[2 * count :]
        narrow = rows_of(normed)
        pieces = []
        for b in range(2):
            inward[b * width : (b + 1) * width] = mm_tn(
                narrow, rows_of(late, slice(b * width, (b + 1) * width))
            ).astype(LOW)
            pieces.append([(outs[k], b * rows, rows, b * width, rows, k) for k in range(count)])
            send_out(inward, pieces[b], idx, sems.at[pl.ds(b * count, count)], True)
        branch = rows_of(late, slice(2 * width, 2 * width + half))
        for b in range(4):
            span = slice(b * width, (b + 1) * width)
            outward[span] = mm_tn(rows_of(active, span), branch).astype(LOW)
        pieces.append([(outs[count + k], 0, 4 * rows, 0, 4 * rows, k) for k in range(count)])
        send_out(outward, pieces[2], idx, sems.at[pl.ds(2 * count, count)], True)
        for b, scratch in enumerate((inward, inward, outward)):
            send_out(scratch, pieces[b], idx, sems.at[pl.ds(b * count, count)], False)

    outs = call(
        body, 5, [idx, *normed, *active, *late], [SMEM] + [VMEM] * 6,
        [((2 * rows, width), LOW, True)] * count + [((4 * rows, half), LOW, True)] * count,
        [
            pltpu.VMEM((2 * width, width), LOW), pltpu.VMEM((4 * width, half), LOW),
            pltpu.SemaphoreType.DMA((3 * count,)),
        ],
    )
    return outs[:count], outs[count:]


def attn_terms_kernel(count, normed, attended, late, sums_one, sums_two, idx):
    width = normed[0].shape[1]
    rows = width // count

    def body(idx, *rest):
        normed, attended, late, (one, two), rest = rest[:2], rest[2:4], rest[4:6], rest[6:8], rest[8:]
        outs, (scratch, notes, sems, note_sems) = rest[: 2 * count], rest[2 * count :]

        def pieces(b):
            return [(outs[b * count + k], 0, rows, b * width, rows, k) for k in range(count)]

        flatly = jnp.concatenate(
            [
                one[0:1], two[0:1], one[1:2], two[1:2], one[2:3], one[3:4], two[2:3], two[7:8],
                jnp.zeros((NOTE - 8, width), F32),
            ],
            axis=0,
        )
        lane = lax.broadcasted_iota(jnp.int32, (NOTE, width), 1)
        line = lax.broadcasted_iota(jnp.int32, (NOTE, width), 0)
        for s in range(count):
            note = pltpu.roll(flatly, width - s * rows, 1) if s else flatly
            start = 4 * rows * s
            hidden = two[3 + start // width : 4 + start // width]
            hidden = pltpu.roll(
                jnp.broadcast_to(hidden, (8, width)), (width - start % width) % width, 1
            )
            hidden = jnp.concatenate([hidden, hidden], axis=0)
            note = jnp.where(
                (line < 8) & (lane < rows), note,
                jnp.where((line == NOTE - 1) & (lane < 4 * rows), hidden, 0.0),
            )
            notes[s] = note.astype(LOW)
        copies = start_all(
            [
                pltpu.make_async_copy(
                    notes.at[idx[k]], outs[k].at[pl.ds(rows, NOTE)], note_sems.at[k]
                )
                for k in range(count)
            ]
        )
        for b in range(2):
            grads = rows_of(late, slice(b * width, (b + 1) * width))
            if b == 0:
                scratch[:width] = mm_tn(rows_of(normed), grads).astype(LOW)
            else:

                @pl.when(idx[count] == 0)
                def _():
                    scratch[width:] = mm_tn(rows_of(normed), grads).astype(LOW)

                @pl.when(idx[count] == 1)
                def _():
                    scratch[width:] = mm_tn(rows_of(attended), grads).astype(LOW)

            send_out(scratch, pieces(b), idx, sems.at[pl.ds(b * count, count)], True)
        for b in range(2):
            send_out(scratch, pieces(b), idx, sems.at[pl.ds(b * count, count)], False)
        wait_all(copies)

    outs = call(
        body, 5, [idx, *normed, *attended, *late, sums_one, sums_two], [SMEM] + [VMEM] * 8,
        [((rows + NOTE, width), LOW, True)] * count + [((rows, width), LOW, True)] * count,
        [
            pltpu.VMEM((2 * width, width), LOW), pltpu.VMEM((count, NOTE, width), LOW),
            pltpu.SemaphoreType.DMA((2 * count,)), pltpu.SemaphoreType.DMA((count,)),
        ],
    )
    return outs[:count], outs[count:]


class Rings:
    def __init__(self, rings):
        self.rings = rings

    def step(self, *after):
        for ring in self.rings:
            ring.step(*after)

    @property
    def last(self):
        return [v for ring in self.rings for v in ring.last if v is not None]


def hold(values, *after):
    return lax.optimization_barrier((values, after))[0] if len(after) else values


class GatherRing:
    def __init__(self, chunk, count, rightward):
        self.right, self.left = ring_pairs(count)
        self.count, self.rightward, self.at = count, rightward, 0
        self.last = (chunk, chunk)
        self.own = {0: chunk}
        self.twin = {}

    def pass_on(self, values):
        places = [self.count - self.at, self.at][: len(values)]
        if len(values) == 1:
            places = [self.at]
        for k, value in zip(places, values):
            self.twin[k] = swap(value, REPLICA)

    def step(self, *after):
        values = hold(self.last, *after)
        near, far = values
        if self.at > 0:
            self.pass_on(values)
        if self.at == 1:
            self.twin[0] = swap(hold(self.own[0], values), REPLICA)
        self.at += 1
        if self.at < self.count // 2:
            near = lax.ppermute(near, SHARD, self.right)
            far = lax.ppermute(far, SHARD, self.left)
            self.own[self.count - self.at], self.own[self.at] = near, far
            self.last = (near, far)
        else:
            if self.rightward:
                last = lax.ppermute(near, SHARD, self.right)
            else:
                last = lax.ppermute(far, SHARD, self.left)
            self.own[self.at] = last
            self.last = (last,)

    def lists(self):
        if self.at not in self.twin:
            self.pass_on(self.last)
        return [[side[k] for k in range(self.count)] for side in (self.own, self.twin)]


class ScatterRing:
    def __init__(self, pieces, count, rightward):
        self.right, self.left = ring_pairs(count)
        self.pieces, self.count, self.rightward = pieces, count, rightward
        self.at = count // 2
        self.last = None

    def step(self, *after):
        pieces, half = self.pieces, self.count // 2
        if self.at == half:
            far = hold(pieces[half], *after)
            if self.rightward:
                self.last = (lax.ppermute(far, SHARD, self.right), None)
            else:
                self.last = (None, lax.ppermute(far, SHARD, self.left))
        else:
            last = hold([v for v in self.last if v is not None], *after)
            sides = []
            for piece, term in zip((pieces[self.at], pieces[self.count - self.at]), self.last):
                sides.append(piece if term is None else add_low(piece, last.pop(0)))
            if len(after) > 0 and None in self.last:
                sides = hold(sides, *after)
            self.last = (
                lax.ppermute(sides[0], SHARD, self.right), lax.ppermute(sides[1], SHARD, self.left)
            )
        self.at -= 1

    def total(self):
        return self.pieces[0].astype(F32) + self.last[0].astype(F32) + self.last[1].astype(F32)


def fast_device(
    tokens, cotangent, group_order, norm_gains, norm_biases, w_qkv, qv_bias, w_out, out_bias,
    w_fc, fc_bias, w_proj, proj_bias,
):
    count = lax.axis_size(SHARD)
    section = lax.axis_index(SECTION)
    replica = lax.axis_index(REPLICA)
    shard = lax.axis_index(SHARD)
    segment, width = tokens.shape[1], tokens.shape[2]
    rows = w_qkv.shape[1]
    half = count // 2
    order = ring_order(count)
    position = jnp.asarray(np.argsort(np.array(order)), jnp.int32)[shard]
    around = lax.rem(position + jnp.arange(count, dtype=jnp.int32), count)
    seat = 2 * replica + lax.rem(shard, 2)
    others = seat ^ jnp.arange(SEATS, dtype=jnp.int32)
    idx = jnp.concatenate(
        [jnp.asarray(order, jnp.int32)[around], jnp.stack([replica, section]).astype(jnp.int32), others]
    )

    ways = [
        [
            (r * count + 2 * z + y, (z // 2) * count + 2 * (2 * r + (z + j) % 2) + y)
            for r in range(2) for z in range(half) for y in range(2)
        ]
        for j in range(2)
    ]
    odd = lax.rem(shard // 2, 2)

    def gather_in(x, j, *more):
        own = lax.dynamic_index_in_dim(x, lax.rem(odd + j, 2), 0, keepdims=False)
        own = jnp.concatenate([own, *more], axis=0) if more else own
        return lax.ppermute(own, (REPLICA, SHARD), ways[j])

    def give_back(x):
        return [
            lax.ppermute(
                x[j * segment : (j + 1) * segment], (REPLICA, SHARD), [(b, a) for a, b in ways[j]]
            )
            for j in range(2)
        ]

    def by_sequence(parts):
        return jnp.stack([jnp.where(even, *parts), jnp.where(even, *parts[::-1])])[None]

    def exchange(parts):
        diagonal = [(r * count + s, (1 - r) * count + (s ^ 1)) for r in range(2) for s in range(count)]
        return [
            pltpu.with_memory_space_constraint(parts[0], pltpu.HBM),
            lax.ppermute(parts[1], SHARD, [(s, s ^ 1) for s in range(count)]),
            swap(parts[2], REPLICA),
            lax.ppermute(parts[3], (REPLICA, SHARD), diagonal),
        ]

    small = jnp.concatenate(
        [norm_gains[0], norm_biases[0], qv_bias[0], out_bias, fc_bias.reshape(4, rows), proj_bias],
        axis=0,
    )
    qkv = w_qkv[0]
    attn_own = [
        jnp.concatenate(
            [jnp.where(replica == 0, qkv[:, :width], qkv[:, 2 * width :]), note_rows(small, width)], axis=0
        ),
        jnp.where(replica == 0, qkv[:, width : 2 * width], w_out[0]),
    ]
    ffn_own = [
        jnp.where(
            replica == 0,
            jnp.concatenate([w_fc[0][:, b * width : (b + 1) * width] for b in (2 * i, 2 * i + 1)], axis=0),
            w_proj[0][2 * i * rows : 2 * (i + 1) * rows],
        )
        for i in range(2)
    ]

    attn_ring = Rings([GatherRing(own, count, i == 0) for i, own in enumerate(attn_own)])
    attn_ring.step()
    order_row = lax.dynamic_index_in_dim(group_order, odd, 0).astype(LOW)
    order_rows = jnp.pad(order_row, ((0, NOTE - 1), (0, width - count)))
    tokens = hold(tokens, attn_ring.last)
    packed = [gather_in(tokens, 0, order_rows), gather_in(tokens, 1)]
    slot = lax.rem(shard // 2 + jnp.arange(2, dtype=jnp.int32), 2)
    which = ((4 * (others // 2) + others % 2)[:, None] + 2 * slot[None, :]).reshape(-1)
    chosen = (which[:, None] == jnp.arange(count, dtype=jnp.int32)[None, :]).astype(jnp.int32)
    packed, chosen, even = lax.optimization_barrier((packed, chosen, odd == 0))
    blocks_at = packed[0][segment, :count].astype(jnp.int32)
    at = jnp.sum(chosen * blocks_at[None, :], axis=1)
    attn_ring.step()
    attn_ring.step()
    ffn_ring = Rings(
        [GatherRing(hold(own, attn_ring.last), count, i == 0) for i, own in enumerate(ffn_own)]
    )
    ffn_ring.step()
    attn_ring.step()
    attn_lists = [ring.lists() for ring in attn_ring.rings]

    def forward(hopped, attn, before):
        sent, inputs, normed, attn = project_kernel(count, segment, packed, hopped, attn, idx)
        arrived = exchange(before[0](sent))
        back = attend_kernel(count, segment, before[1](arrived), at, hopped is not None)
        state = Bag(vec=attn[3], inputs=inputs, normed=normed, arrived=arrived)
        return state, attn, exchange(before[2](back[:SEATS])), back[SEATS:]

    def ring_sent(sent):
        ffn_ring.step(sent[1])
        return sent

    def ring_arrived(arrived):
        ffn_ring.step(arrived[1])
        return arrived

    def ring_back(back):
        ffn_ring.step(back[1])
        return back

    def same(values):
        return values

    first, attn, returned, _ = forward(None, attn_lists, [ring_sent, ring_arrived, ring_back])
    output, *ffn = feed_kernel(
        count, segment, returned, first.inputs, first.vec,
        attn_lists + [ring.lists() for ring in ffn_ring.rings], idx,
    )

    def hop(values, backward):
        return lax.ppermute(values, SECTION, [(1, 0)] if backward else [(0, 1)])

    upstream = [gather_in(hold(cotangent, output), j) for j in range(2)]
    state, attn, returned, kept = forward(
        hop(output, False), attn, [same, lambda arrived: hold(arrived, upstream), same]
    )
    state.attended, state.total = kept
    *sent, output, state.attended_low, state.middle, state.normed_two, state.slope, state.active, grad_middle = (
        turn_kernel(count, segment, returned, state.inputs, state.vec, ffn, upstream, idx)
    )
    kept_rows = state.normed_two, state.active, state.normed, state.attended_low
    pairs, acts = [], []

    def aside(back):
        pairs.extend([own, swap(hold(own, back[0]), REPLICA)] for own in kept_rows)
        acts.extend(give_back(hold(output, back[0])))
        return back

    def backward(sent, grad_middle, grad_out, keep, ties, between):
        arrived = exchange(sent)
        ties = ties + between[0](arrived)
        back = attend_back_kernel(
            count, segment, state.arrived, arrived, state.attended, state.total, at, ties
        )
        returned = exchange(between[1](back))
        return project_back_kernel(
            count, segment, between[2](returned), grad_middle, grad_out, state, attn[:3], idx, keep
        )

    early = backward(
        sent, grad_middle, None, False, [],
        [lambda arrived: [], aside, same],
    )
    hopped, acts, pairs = lax.optimization_barrier((hop(early[0], True), acts, pairs))
    acts = by_sequence(acts)
    rings = []
    *sent, grad_middle, mine, theirs, sums_two, grad_out = feed_back_kernel(
        count, segment, upstream, hopped, state, ffn, idx
    )

    def ffn_terms(arrived):
        terms = ffn_terms_kernel(
            count, pairs[0], pairs[1], hold([mine, swap(theirs, REPLICA)], arrived), idx
        )
        rings.append(Rings([ScatterRing(t, count, i == 0) for i, t in enumerate(terms)]))
        rings[0].step()
        return [terms[0][0]]

    def ring_back(back):
        back = hold(back, rings[0].last)
        rings[0].step(back[0])
        return back

    low, *last = backward(sent, grad_middle, grad_out, True, [], [ffn_terms, ring_back, same])
    terms = attn_terms_kernel(
        count, pairs[2], pairs[3], [last[1], swap(last[2], REPLICA)], last[3], sums_two, idx
    )
    rings.append(Rings([ScatterRing(t, count, i == 0) for i, t in enumerate(terms)]))
    rings[0].step(terms[0][0])
    rings[1].step()
    rings[1].step()
    rings[0].step()
    in_grads = give_back(hold(last[0].astype(LOW), rings[1].last))
    rings[1].step()
    rings[1].step()
    in_grads = by_sequence(hold(in_grads, rings[1].last)).astype(F32)

    def finished(ring):
        total = ring.total().astype(LOW)
        twin = swap(total, REPLICA)
        return (
            jnp.where(replica == 0, total, twin).astype(F32),
            jnp.where(replica == 0, twin, total).astype(F32),
        )

    feed_totals, totals = [[finished(ring) for ring in pair.rings] for pair in rings]
    fc_grad = jnp.concatenate(
        [part[b * rows : (b + 1) * rows] for part in feed_totals[0] for b in range(2)], axis=1
    )
    proj_grad = jnp.concatenate(feed_totals[1], axis=1)
    qkv_grad = jnp.concatenate([totals[0][0][:rows], totals[1][0], totals[0][1][:rows]], axis=1)
    note = totals[0][0][rows:] + totals[0][1][rows:]
    vec = note[:8, :rows]
    return (
        acts, in_grads, vec[0:2][None], vec[2:4][None], qkv_grad[None], vec[4:6][None],
        totals[1][1][None], vec[6][None], fc_grad[None], note[NOTE - 1, : 4 * rows][None],
        proj_grad[None], vec[7][None],
    )


def on_each(tokens, *others):
    count = lax.axis_size(SHARD)
    tiles = (tokens.shape[2] // count) % 32 == 0 and tokens.shape[1] % 64 == 0
    seats = count == 2 * SEATS and tokens.shape[0] == 2 and HEADS == 3 * SEATS
    return (fast_device if tiles and seats else on_device)(tokens, *others)


def solution(mesh):
    in_specs = (
        P(REPLICA, SHARD, None),
        P(REPLICA, SHARD, None),
        P(REPLICA, None),
        P(SECTION, None, SHARD),
        P(SECTION, None, SHARD),
        P(SECTION, SHARD, None),
        P(SECTION, None, SHARD),
        P(SECTION, SHARD, None),
        P(SECTION, SHARD),
        P(SECTION, SHARD, None),
        P(SECTION, SHARD),
        P(SECTION, SHARD, None),
        P(SECTION, SHARD),
    )
    out_specs = (
        P(SECTION, REPLICA, SHARD, None),
        P(SECTION, REPLICA, SHARD, None),
        P(SECTION, None, SHARD),
        P(SECTION, None, SHARD),
        P(SECTION, SHARD, None),
        P(SECTION, None, SHARD),
        P(SECTION, SHARD, None),
        P(SECTION, SHARD),
        P(SECTION, SHARD, None),
        P(SECTION, SHARD),
        P(SECTION, SHARD, None),
        P(SECTION, SHARD),
    )
    return jax.shard_map(
        on_each, mesh=mesh, in_specs=in_specs, out_specs=out_specs, check_vma=False
    )
```

```python
import functools
import math
from types import SimpleNamespace as Bag

import jax
import jax.numpy as jnp
import numpy as np
from jax import lax
from jax.experimental import pallas as pl
from jax.experimental.pallas import tpu as pltpu
from jax.sharding import PartitionSpec as P

HEADS = 12
HEAD = 64
EPSILON = 1e-05
SCALING = 0.125
FLOOR = -1e30
SECTION, REPLICA, SHARD = "section", "replica", "shard"
LOW = jnp.bfloat16
F32 = jnp.float32


def ring_order(count):
    return list(range(0, count, 2)) + list(range(count - 1, 0, -2))


def ring_pairs(count):
    order = ring_order(count)
    right = [(order[i], order[(i + 1) % count]) for i in range(count)]
    return right, [(b, a) for a, b in right]


def ring_gather(chunk, count):
    right, left = ring_pairs(count)
    got = {0: chunk}
    from_left = from_right = chunk
    cut = chunk.shape[0] // 32 * 16
    for step in range(1, count // 2 + 1):
        if step == count // 2:
            got[step] = jnp.concatenate(
                [
                    lax.ppermute(from_left[:cut], SHARD, right),
                    lax.ppermute(from_right[cut:], SHARD, left),
                ],
                axis=0,
            )
        else:
            from_left = lax.ppermute(from_left, SHARD, right)
            from_right = lax.ppermute(from_right, SHARD, left)
            got[count - step] = from_left
            got[step] = from_right
    return [got[k] for k in range(count)]


def ring_scatter(piece, rows, count):
    right, left = ring_pairs(count)
    cut = rows // 32 * 16
    half = count // 2
    far = piece(half)
    to_right = lax.ppermute(far[:cut], SHARD, right)
    to_left = lax.ppermute(far[cut:], SHARD, left)
    for distance in range(half - 1, 0, -1):
        first, second = piece(distance), piece(count - distance)
        if distance == half - 1:
            first = jnp.concatenate([add_low(first[:cut], to_right), first[cut:]], axis=0)
            second = jnp.concatenate([second[:cut], add_low(second[cut:], to_left)], axis=0)
        else:
            first = add_low(first, to_right)
            second = add_low(second, to_left)
        to_right = lax.ppermute(first, SHARD, right)
        to_left = lax.ppermute(second, SHARD, left)
    return piece(0).astype(F32) + to_right.astype(F32) + to_left.astype(F32)


def add_low(a, b):
    return (a.astype(F32) + b.astype(F32)).astype(LOW)


def swap(x, axis):
    return lax.ppermute(x, axis, [(0, 1), (1, 0)])


def normalize(values, gain_row, offset):
    average = jnp.mean(values, axis=-1, keepdims=True)
    centred = values - average
    variance = jnp.mean(centred * centred, axis=-1, keepdims=True)
    return centred * lax.rsqrt(variance + EPSILON) * gain_row + offset


def gelu_tanh(values):
    return jax.nn.gelu(values, approximate=True)


def dot(a, b):
    return jnp.dot(a, b, preferred_element_type=F32)


def dot_t(a, b):
    return lax.dot_general(a, b, (((1,), (1,)), ((), ())), preferred_element_type=F32)


def dot_rows(a, b):
    return lax.dot_general(a, b, (((0,), (0,)), ((), ())), preferred_element_type=F32)


class Plan:
    def __init__(self, count, segment):
        self.count = count
        self.segment = segment
        self.splits = count // math.gcd(HEADS, count)
        self.units = HEADS * self.splits // count
        self.part = segment // self.splits
        self.first = [self.units * q // self.splits for q in range(count)]
        self.slots = max(
            (self.units * q + self.units - 1) // self.splits - self.first[q] + 1
            for q in range(count)
        )
        self.groups = [
            [r * count + h * (count // 2) + i for r in range(2) for i in range(count // 2)]
            for h in range(2)
        ]

    def exchange(self, blocks):
        return lax.all_to_all(
            blocks, (REPLICA, SHARD), 0, 0, tiled=True, axis_index_groups=self.groups
        )

    def pack_units(self, heads):
        parts = heads.reshape(self.splits, self.part, HEADS, HEAD)
        parts = parts.transpose(2, 0, 1, 3).reshape(
            self.count, self.units * self.part, HEAD
        )
        return self.fold(parts)

    def fold(self, parts):
        rows = parts.shape[1] // 2
        return jnp.concatenate([parts[:, :rows], parts[:, rows:]], axis=2)

    def unfold(self, folded):
        return jnp.concatenate([folded[..., :HEAD], folded[..., HEAD:]], axis=1)

    def unpack_units(self, folded):
        parts = self.unfold(folded).reshape(HEADS, self.splits, self.part, HEAD)
        return parts.transpose(1, 2, 0, 3).reshape(self.segment, HEADS * HEAD)

    def gather_units(self, folded):
        parts = self.unfold(folded).reshape(self.count, self.units, self.part, HEAD)
        return parts.transpose(1, 0, 2, 3).reshape(self.units, self.count * self.part, HEAD)

    def scatter_units(self, values):
        parts = values.reshape(self.units, self.count, self.part, HEAD).transpose(1, 0, 2, 3)
        return self.fold(parts.reshape(self.count, self.units * self.part, HEAD))

    def head_slots(self, rows):
        blocks = []
        for q in range(self.count):
            cols = []
            for slot in range(self.slots):
                head = min(self.first[q] + slot, HEADS - 1)
                cols.append(rows[:, head * HEAD : (head + 1) * HEAD])
            blocks.append(jnp.concatenate(cols, axis=1))
        return jnp.stack(blocks)

    def sum_slots(self, blocks):
        cols = []
        for head in range(HEADS):
            total = None
            for q in range(self.count):
                last = (self.units * (q + 1) - 1) // self.splits
                if self.first[q] <= head <= last:
                    slot = head - self.first[q]
                    term = blocks[q, :, slot * HEAD : (slot + 1) * HEAD].astype(F32)
                    total = term if total is None else total + term
            cols.append(total)
        return jnp.concatenate(cols, axis=1)


def over(a, b, dim_a, dim_b):
    return lax.dot_general(a, b, (((dim_a,), (dim_b,)), ((), ())), preferred_element_type=F32)


def over_units(a, b):
    return lax.dot_general(a, b, (((0, 1), (0, 1)), ((), ())), preferred_element_type=F32)


def widen(units, slot, slots):
    wide = jnp.concatenate([units] * slots, axis=2)
    lane_slot = jnp.arange(slots * HEAD, dtype=jnp.int32) // HEAD
    return jnp.where(lane_slot[None, None, :] == slot[:, None, None], wide, jnp.zeros_like(wide))


def narrow(wide, slot, slots):
    lane_slot = jnp.arange(slots * HEAD, dtype=jnp.int32) // HEAD
    wide = jnp.where(lane_slot[None, None, :] == slot[:, None, None], wide, jnp.zeros_like(wide))
    return sum(wide[:, :, s * HEAD : (s + 1) * HEAD] for s in range(slots))


def attend_forward(queries, keys, values, query_pos, key_pos):
    scores = over(queries, keys, 2, 1) * SCALING
    visible = key_pos[None, None, :] <= query_pos[:, :, None]
    scores = jnp.where(visible, scores, FLOOR)
    highest = jnp.max(scores, axis=-1, keepdims=True)
    terms = jnp.exp(scores - highest)
    total = jnp.sum(terms, axis=-1, keepdims=True)
    weights = (terms / total).astype(LOW)
    attended = over(weights, values, 2, 0)
    return attended, highest + jnp.log(total)


def attend_backward(queries, keys, values, query_pos, key_pos, log_total, grad, row_dots):
    scores = over(queries, keys, 2, 1) * SCALING
    visible = key_pos[None, None, :] <= query_pos[:, :, None]
    weights = jnp.where(visible, jnp.exp(scores - log_total), 0.0)
    grad_weights = over(grad, values, 2, 1)
    grad_scores = (weights * (grad_weights - row_dots)).astype(LOW)
    grad_queries = (
        over(grad_scores, keys, 2, 0) * SCALING
    )
    grad_keys = (
        over_units(grad_scores, queries) * SCALING
    )
    grad_values = over_units(weights.astype(LOW), grad)
    return grad_queries, grad_keys, grad_values


def layer_forward(inputs, weights, plan, place):
    normed = normalize(inputs, weights.gains[0], weights.offsets[0]).astype(LOW)
    queries = (dot(normed, weights.q) + weights.q_bias).astype(LOW)
    keys = dot(normed, weights.k).astype(LOW)
    values = (dot(normed, weights.v) + weights.v_bias).astype(LOW)
    segment = inputs.shape[0]
    width = plan.slots * HEAD
    sent = jnp.concatenate(
        [
            plan.head_slots(keys),
            plan.head_slots(values),
            plan.pack_units(queries.reshape(segment, HEADS, HEAD)).reshape(
                plan.count, -1, width
            ),
        ],
        axis=1,
    )
    arrived = plan.exchange(sent)
    length = plan.count * segment
    all_keys = arrived[:, :segment].reshape(length, width)
    all_values = arrived[:, segment : 2 * segment].reshape(length, width)
    units = plan.gather_units(arrived[:, 2 * segment :].reshape(plan.count, -1, 2 * HEAD))
    units = widen(units, place.slot, plan.slots)
    attended, log_total = attend_forward(
        units, all_keys, all_values, place.query_pos, place.key_pos
    )
    attended = narrow(attended, place.slot, plan.slots)
    returned = plan.exchange(plan.scatter_units(attended.astype(LOW)))
    attended_low = plan.unpack_units(returned)
    middle = inputs + dot(attended_low, weights.o) + weights.out_bias
    normed_two = normalize(middle, weights.gains[1], weights.offsets[1]).astype(LOW)
    hidden = dot(normed_two, weights.fc) + weights.fc_bias
    active = gelu_tanh(hidden).astype(LOW)
    output = middle + dot(active, weights.proj) + weights.proj_bias
    saved = Bag(
        inputs=inputs, normed=normed, units=units, keys=all_keys, values=all_values,
        attended=attended, log_total=log_total, attended_low=attended_low, middle=middle,
        normed_two=normed_two, hidden=hidden, active=active,
    )
    return output, saved


def layer_backward(arriving, saved, weights, plan, place):
    segment, model_width = arriving.shape
    grad_branch = arriving.astype(LOW)
    grad_active = dot_t(grad_branch, weights.proj)
    grad_hidden = jax.vjp(gelu_tanh, saved.hidden)[1](grad_active)[0].astype(LOW)
    grad_normed_two = dot_t(grad_hidden, weights.fc)
    grad_middle_norm, gain_two, offset_two = jax.vjp(
        normalize, saved.middle, weights.gains[1], weights.offsets[1]
    )[1](grad_normed_two)
    grads = Bag(
        proj=dot_rows(saved.active, grad_branch),
        proj_bias=jnp.sum(grad_branch.astype(F32), axis=0),
        fc=dot_rows(saved.normed_two, grad_hidden),
        fc_bias=jnp.sum(grad_hidden.astype(F32), axis=0),
    )
    grad_middle = arriving + grad_middle_norm
    grad_out = grad_middle.astype(LOW)
    grad_attended = dot_t(grad_out, weights.o).astype(LOW)
    arrived = plan.exchange(plan.pack_units(grad_attended.reshape(segment, HEADS, HEAD)))
    grad_units = plan.gather_units(arrived)
    row_dots = jnp.sum(grad_units.astype(F32) * saved.attended, axis=-1, keepdims=True)
    grad_queries, grad_keys, grad_values = attend_backward(
        saved.units, saved.keys, saved.values, place.query_pos, place.key_pos,
        saved.log_total, widen(grad_units, place.slot, plan.slots), row_dots,
    )
    grad_queries = narrow(grad_queries, place.slot, plan.slots).astype(LOW)
    width = plan.slots * HEAD
    sent = jnp.concatenate(
        [
            grad_keys.astype(LOW).reshape(plan.count, segment, width),
            grad_values.astype(LOW).reshape(plan.count, segment, width),
            plan.scatter_units(grad_queries).reshape(plan.count, -1, width),
        ],
        axis=1,
    )
    returned = plan.exchange(sent)
    grad_k = plan.sum_slots(returned[:, :segment]).astype(LOW)
    grad_v = plan.sum_slots(returned[:, segment : 2 * segment]).astype(LOW)
    grad_q = plan.unpack_units(returned[:, 2 * segment :].reshape(plan.count, -1, 2 * HEAD))
    grad_normed = (
        dot_t(grad_q, weights.q) + dot_t(grad_k, weights.k) + dot_t(grad_v, weights.v)
    )
    grad_input_norm, gain_one, offset_one = jax.vjp(
        normalize, saved.inputs, weights.gains[0], weights.offsets[0]
    )[1](grad_normed)
    grads = Bag(
        proj=grads.proj, proj_bias=grads.proj_bias, fc=grads.fc, fc_bias=grads.fc_bias,
        gains=jnp.stack([gain_one, gain_two]),
        offsets=jnp.stack([offset_one, offset_two]),
        q=dot_rows(saved.normed, grad_q),
        k=dot_rows(saved.normed, grad_k),
        v=dot_rows(saved.normed, grad_v),
        qv_bias=jnp.stack([jnp.sum(grad_q.astype(F32), axis=0), jnp.sum(grad_v.astype(F32), axis=0)]),
        o=dot_rows(saved.attended_low, grad_out),
        out_bias=jnp.sum(grad_out.astype(F32), axis=0),
    )
    return grad_middle + grad_input_norm, grads


def on_device(
    tokens, cotangent, group_order, norm_gains, norm_biases, w_qkv, qv_bias, w_out, out_bias,
    w_fc, fc_bias, w_proj, proj_bias,
):
    count = lax.axis_size(SHARD)
    section = lax.axis_index(SECTION)
    replica = lax.axis_index(REPLICA)
    shard = lax.axis_index(SHARD)
    segment, model_width = tokens.shape[1], tokens.shape[2]
    rows = w_qkv.shape[1]
    half = count // 2
    plan = Plan(count, segment)
    order = ring_order(count)
    position_of = np.argsort(np.array(order))
    position = jnp.asarray(position_of, jnp.int32)[shard]
    order_table = jnp.asarray(order, jnp.int32)

    def owner(offset):
        return order_table[lax.rem(position + offset, count)]

    home = shard // half
    keeps = home == replica
    crossing = []
    for s in range(half):
        crossing += [(count + s, s + half), (s + half, count + s)]

    def reshard(x):
        moved = lax.ppermute(x, (REPLICA, SHARD), crossing)
        return jnp.where(keeps, x, moved)

    def pick(x):
        return lax.dynamic_index_in_dim(x, section, 0, keepdims=False)

    order_row = pick(group_order).astype(LOW)
    order_row = jnp.broadcast_to(
        jnp.concatenate([order_row, jnp.zeros((model_width - count,), LOW)])[None], (16, model_width)
    )
    packed = reshard(jnp.concatenate([pick(tokens), order_row], axis=0))
    current = packed[:segment].astype(F32)
    blocks_at = packed[segment, :count].astype(jnp.int32)
    upstream = reshard(pick(cotangent))
    seat = replica * half + lax.rem(shard, half)
    key_pos = (
        blocks_at[:, None] * segment + jnp.arange(segment, dtype=jnp.int32)[None, :]
    )
    unit_ids = plan.units * seat + jnp.arange(plan.units, dtype=jnp.int32)
    unit_part = lax.rem(unit_ids, plan.splits)
    parts_pos = key_pos.reshape(count, plan.splits, plan.part)
    query_pos = jnp.stack(
        [
            lax.dynamic_index_in_dim(parts_pos, unit_part[u], 1, keepdims=False).reshape(-1)
            for u in range(plan.units)
        ]
    )
    place = Bag(
        slot=unit_ids // plan.splits - (plan.units * seat) // plan.splits,
        query_pos=query_pos,
        key_pos=key_pos.reshape(-1),
    )

    small = jnp.concatenate(
        [
            norm_gains[0], norm_biases[0], qv_bias[0], out_bias, fc_bias.reshape(4, rows), proj_bias,
        ],
        axis=0,
    ).reshape(-1)
    small_rows = -(-small.shape[0] // (16 * model_width)) * 16
    small = jnp.concatenate(
        [small, jnp.zeros((small_rows * model_width - small.shape[0],), LOW)]
    ).reshape(small_rows, model_width)
    qkv = w_qkv[0]
    attn_sets = (
        jnp.concatenate([qkv[:, :model_width], qkv[:, model_width : 2 * model_width], small], axis=0),
        jnp.concatenate([qkv[:, 2 * model_width :], w_out[0], small], axis=0),
    )
    fc_blocks = w_fc[0].reshape(rows, 4, model_width).transpose(1, 0, 2).reshape(4 * rows, model_width)
    ffn_sets = (fc_blocks, w_proj[0])

    def gathered(sets):
        own = jnp.where(replica == 0, sets[0], sets[1])
        other_layer = swap(own, SECTION)
        layers = []
        for layer in range(2):
            chunk = jnp.where(section == layer, own, other_layer)
            chunks = ring_gather(chunk, count)
            buffer = jnp.zeros((2, count) + chunk.shape, LOW)
            for offset in range(count):
                twin = swap(chunks[offset], REPLICA)
                at = owner(offset)
                buffer = lax.dynamic_update_slice(buffer, chunks[offset][None, None], (replica, at, 0, 0))
                buffer = lax.dynamic_update_slice(buffer, twin[None, None], (1 - replica, at, 0, 0))
            layers.append(buffer)
        return layers

    attn = gathered(attn_sets)
    ffn = gathered(ffn_sets)

    def block(buffer, which, at):
        return buffer[which, :, at * rows : (at + 1) * rows].reshape(count * rows, model_width)

    def unpacked(layer):
        a, f = attn[layer], ffn[layer]
        vec = a[0, :, 2 * rows :].reshape(count, -1)[:, : 12 * rows].reshape(count, 12, rows).astype(F32)

        def row(i):
            return vec[:, i].reshape(-1)

        return Bag(
            q=block(a, 0, 0), k=block(a, 0, 1), v=block(a, 1, 0), o=block(a, 1, 1),
            fc=jnp.concatenate([block(f, 0, i) for i in range(4)], axis=1),
            proj=f[1].reshape(count * 4 * rows, model_width),
            gains=(row(0), row(1)), offsets=(row(2), row(3)), q_bias=row(4), v_bias=row(5),
            out_bias=row(6), fc_bias=vec[:, 7:11].reshape(-1), proj_bias=row(11),
        )

    weights = [unpacked(0), unpacked(1)]
    outputs, states = [], []
    for layer in range(2):
        output, saved = layer_forward(current, weights[layer], plan, place)
        outputs.append(output.astype(LOW))
        states.append(saved)
        current = outputs[-1].astype(F32)
    grad_inputs, totals = [None, None], [None, None]
    arriving = upstream.astype(F32)

    def pieces(attn_rows, layer_grads, which):
        pass

    def blocks_of(grad, cols):
        return grad.astype(LOW).reshape(count, -1, cols)

    def scattered(sets):
        own = jnp.where(replica == 0, sets[0], sets[1])
        other = jnp.where(replica == 0, sets[1], sets[0])
        paired = add_low(own, swap(other, REPLICA))
        return ring_scatter(
            lambda k: lax.dynamic_index_in_dim(paired, owner(k), 0, keepdims=False),
            paired.shape[1], count,
        )

    scattered_attn, scattered_ffn = [None, None], [None, None]
    for layer in (1, 0):
        grad_input, grads = layer_backward(arriving, states[layer], weights[layer], plan, place)
        grad_inputs[layer] = grad_input
        arriving = grad_input.astype(LOW).astype(F32)
        vec = jnp.concatenate(
            [
                grads.gains, grads.offsets, grads.qv_bias, grads.out_bias[None],
            ], axis=0,
        ).reshape(7, count, rows).transpose(1, 0, 2)
        vec = jnp.concatenate(
            [vec, grads.fc_bias.reshape(count, 4, rows), grads.proj_bias.reshape(count, 1, rows)],
            axis=1,
        ).astype(LOW).reshape(count, 12 * rows)
        vec = jnp.concatenate(
            [vec, jnp.zeros((count, small_rows * model_width - 12 * rows), LOW)], axis=1
        ).reshape(count, small_rows, model_width)
        scattered_ffn[layer] = scattered(
            (
                jnp.concatenate(
                    [blocks_of(grads.fc[:, i * model_width : (i + 1) * model_width], model_width) for i in range(4)],
                    axis=1,
                ),
                blocks_of(grads.proj, model_width),
            )
        )
        scattered_attn[layer] = scattered(
            (
                jnp.concatenate([blocks_of(grads.q, model_width), blocks_of(grads.k, model_width), vec], axis=1),
                jnp.concatenate([blocks_of(grads.v, model_width), blocks_of(grads.o, model_width), vec], axis=1),
            )
        )

    def finished(parts):
        own = jnp.where(section == 0, parts[0], parts[1])
        other = jnp.where(section == 0, parts[1], parts[0]).astype(LOW)
        total = (own + swap(other, SECTION).astype(F32)).astype(LOW)
        twin = swap(total, REPLICA)
        return (
            jnp.where(replica == 0, total, twin).astype(F32),
            jnp.where(replica == 0, twin, total).astype(F32),
        )

    ffn_total = finished(scattered_ffn)
    attn_total = finished(scattered_attn)
    fc_grad = ffn_total[0].reshape(4, rows, model_width).transpose(1, 0, 2).reshape(rows, 4 * model_width)
    proj_grad = ffn_total[1]
    qkv_grad = jnp.concatenate(
        [attn_total[0][:rows], attn_total[0][rows : 2 * rows], attn_total[1][:rows]], axis=1
    )
    out_grad = attn_total[1][rows : 2 * rows]
    vec = attn_total[0][2 * rows :].reshape(-1)[: 12 * rows].reshape(12, rows)

    def by_owner(per_layer):
        low = [reshard(v.astype(LOW)) for v in per_layer]
        own = jnp.where(section == 0, low[0], low[1])
        other = jnp.where(section == 0, low[1], low[0])
        got = swap(other, SECTION)
        return jnp.stack([jnp.where(section == 0, own, got), jnp.where(section == 0, got, own)])[None]

    acts = by_owner(outputs)
    in_grads = by_owner(grad_inputs).astype(F32)
    return (
        acts,
        in_grads,
        vec[0:2][None],
        vec[2:4][None],
        qkv_grad[None],
        vec[4:6][None],
        out_grad[None],
        vec[6][None],
        fc_grad[None],
        vec[7:11].reshape(1, 4 * rows),
        proj_grad[None],
        vec[11][None],
    )


ANY = pl.BlockSpec(memory_space=pl.ANY)
VMEM = pl.BlockSpec(memory_space=pltpu.VMEM)
SMEM = pl.BlockSpec(memory_space=pltpu.SMEM)
PAIR = 2 * HEAD
VMEM_LIMIT = 24 * 2**20
MEMORY_RATE = 3.69e6


def mm(a, b):
    return lax.dot_general(a, b, (((1,), (0,)), ((), ())), preferred_element_type=F32)


def mm_nt(a, b):
    return lax.dot_general(a, b, (((1,), (1,)), ((), ())), preferred_element_type=F32)


def mm_tn(a, b):
    return lax.dot_general(a, b, (((0,), (0,)), ((), ())), preferred_element_type=F32)


def call(body, micros, operands, specs, outs, scratch, saves=(), keep=True):
    outs = list(outs) + (list(saves) if keep else [])
    spare = [] if keep else [pltpu.VMEM(shape, kind) for shape, kind, _ in saves]
    return pl.pallas_call(
        body,
        in_specs=specs,
        out_specs=[ANY if space is True else VMEM for _, _, space in outs],
        out_shape=[
            {None: jax.ShapeDtypeStruct, True: pltpu.HBM, False: pltpu.VMEM}[space](shape, kind)
            for shape, kind, space in outs
        ],
        scratch_shapes=spare + scratch,
        compiler_params=pltpu.CompilerParams(vmem_limit_bytes=VMEM_LIMIT),
        cost_estimate=pl.CostEstimate(
            flops=0, bytes_accessed=int(micros * MEMORY_RATE), transcendentals=0
        ),
    )(*operands)


SEATS = 4


def low_lanes(shape):
    return lax.broadcasted_iota(jnp.int32, shape, len(shape) - 1) % PAIR < HEAD


def turn(tile):
    return pltpu.roll(tile, HEAD, 1)


def tiles_of(values, seat):
    at = 3 * seat // 2
    pair, single = (at, at + 1) if seat % 2 == 0 else (at + 1, at)
    return [values[:, t * PAIR : (t + 1) * PAIR] for t in (pair, single)]


def join(first, second, seat):
    low = low_lanes(first.shape)
    if seat % 2 == 0:
        return jnp.where(low, first, turn(second))
    return jnp.where(low, turn(first), second)


def fold(tile, seat):
    half = tile.shape[0] // 2
    return join(tile[:half], tile[half:], seat)


def split(tile, seat):
    low = low_lanes(tile.shape)
    turned = turn(tile)
    if seat % 2 == 0:
        return jnp.where(low, tile, 0.0), jnp.where(low, turned, 0.0)
    return jnp.where(low, 0.0, turned), jnp.where(low, 0.0, tile)


def unfold(tile, seat):
    return jnp.concatenate(split(tile, seat), axis=0)


def whole_rows(pairs, singles):
    tiles = []
    for even in range(0, SEATS, 2):
        tiles += [pairs[even], singles[even] + singles[even + 1], pairs[even + 1]]
    return jnp.concatenate(tiles, axis=1)


def start_all(copies):
    for copy in copies:
        copy.start()
    return copies


def wait_all(copies):
    for copy in copies:
        copy.wait()


def to_seats(scratch, outs, idx, count, sems):
    return start_all(
        [
            pltpu.make_async_copy(scratch.at[idx[count + 2 + k]], outs[k], sems.at[k])
            for k in range(SEATS)
        ]
    )


def from_seats(ins, scratch, idx, count, sems):
    return start_all(
        [
            pltpu.make_async_copy(ins[k], scratch.at[idx[count + 2 + k]], sems.at[k])
            for k in range(SEATS)
        ]
    )


def in_order(refs, scratch, at, sems, outward):
    copies = []
    for k in range(SEATS):
        for p in range(2):
            ends = refs[k].at[p], scratch.at[at[2 * k + p]]
            if outward:
                ends = ends[::-1]
            copies.append(pltpu.make_async_copy(*ends, sems.at[2 * k + p]))
    return start_all(copies)


def block_rows(segment):
    return 4 * segment + segment // 2


class Loader:
    def __init__(self, sems):
        self.sems = sems
        self.used = 0
        self.waits = {}

    def load(self, idx, count, own, twin, targets):
        slots = {}
        for which in (0, 1):
            for at, (offset, rows, ref, key) in enumerate(targets[which]):
                for k in range(count):
                    slots[which, at, k] = self.used
                    self.waits.setdefault(key, []).append((ref, self.used))
                    self.used += 1
        for rep in (0, 1):
            @pl.when(idx[count] == rep)
            def _():
                for which in (0, 1):
                    chunks = own if which == rep else twin
                    for at, (offset, rows, ref, key) in enumerate(targets[which]):
                        for k in range(count):
                            if len(chunks) == 1:
                                chunk, place = chunks[0].at[k], k
                            else:
                                chunk, place = chunks[k], idx[k]
                            pltpu.make_async_copy(
                                chunk.at[pl.ds(offset, rows)], ref.at[place],
                                self.sems.at[slots[which, at, k]],
                            ).start()

    def wait(self, key):
        for ref, slot in self.waits[key]:
            pltpu.make_async_copy(ref.at[0], ref.at[0], self.sems.at[slot]).wait()


def flat(ref):
    return ref[...].reshape(-1, ref.shape[-1])


def centre(values):
    average = jnp.mean(values, axis=-1, keepdims=True)
    centred = values - average
    scale = lax.rsqrt(jnp.mean(centred * centred, axis=-1, keepdims=True) + EPSILON)
    return centred * scale, scale


def centre_back(grad, hat, scale):
    return scale * (
        grad
        - jnp.mean(grad, axis=-1, keepdims=True)
        - hat * jnp.mean(grad * hat, axis=-1, keepdims=True)
    )


GELU_A, GELU_B = math.sqrt(2 / math.pi), 0.044715


NOTE = 16


def note_rows(small, width):
    rows = small.shape[1]
    hidden = jnp.pad(small[7:11].reshape(1, 4 * rows), ((0, 0), (0, width - 4 * rows)))
    others = jnp.concatenate([small[:7], small[11:]], axis=0)
    others = jnp.pad(others, ((0, NOTE - 9), (0, width - rows)))
    return jnp.concatenate([others, hidden], axis=0)


def read_notes(notes, count, width):
    rows = width // count
    total = None
    hidden = []
    for s in range(count):
        note = notes[s].astype(F32)
        moved = pltpu.roll(note, s * rows, 1) if s else note
        total = moved if total is None else total + moved
        at = (4 * rows * s) % width
        hidden.append(pltpu.roll(note[8:], at, 1)[NOTE - 9 :] if at else note[8:][NOTE - 9 :])
    per = width // (4 * rows)
    lines = [sum(hidden[b * per + i] for i in range(per)) for b in range(4)]
    return [total[:8]] + lines


def flatten(rings):
    chunks = [chunk for lists in rings for chunks in lists for chunk in chunks]
    return [pltpu.with_memory_space_constraint(chunk, pltpu.HBM) for chunk in chunks]


def load_projections(loader, idx, count, rows, chunks, wq, wk, wv, notes):
    first = [(0, rows, wq, 0), (rows, NOTE, notes, 3)]
    loader.load(idx, count, chunks[:count], chunks[count : 2 * count], [first, [(0, rows, wv, 2)]])
    loader.load(idx, count, chunks[2 * count : 3 * count], chunks[3 * count :], [[(0, rows, wk, 1)], []])


def load_output(loader, idx, count, rows, chunks, wo):
    loader.load(idx, count, chunks[2 * count : 3 * count], chunks[3 * count : 4 * count], [[], [(0, rows, wo, 5)]])


def load_feed(loader, idx, count, rows, chunks, wf, wp):
    for pair in range(2):
        own, twin = [chunks[(2 * pair + i) * count : (2 * pair + i + 1) * count] for i in range(2)]
        loader.load(
            idx, count, own, twin,
            [
                [(i * rows, rows, wf.at[2 * pair + i], 2 * pair + i) for i in range(2)],
                [(i * rows, rows, wp.at[:, 2 * pair + i], 4) for i in range(2)],
            ],
        )


def project_kernel(count, segment, inputs, hopped, attn, idx):
    width = inputs[0].shape[1]
    rows = width // count
    given = [] if hopped is None else [hopped]
    tall = block_rows(segment)
    loading = hopped is None

    def body(idx, first, second, *rest):
        arrived, rest = rest[: len(given)], rest[len(given) :]
        if loading:
            chunks, rest = rest[: 4 * count], rest[4 * count :]
            outs, (chosen, wq, wk, wv, vec, blocks, normed, notes, sems, out_sems) = rest[:SEATS], rest[SEATS:]
            loader = Loader(sems)
            load_projections(loader, idx, count, rows, chunks, wq, wk, wv, notes)
        else:
            (wq, wk, wv, vec), rest = rest[:4], rest[4:]
            outs, (chosen, normed, blocks, out_sems) = rest[:SEATS], rest[SEATS:]
        values = jnp.concatenate([first[:segment], second[:segment]], axis=0).astype(F32)
        if given:
            values = jnp.where(idx[count + 1] == 0, values, arrived[0][...].astype(F32))
        chosen[...] = values.astype(LOW)
        hat, _ = centre(values)
        if loading:
            loader.wait(3)
            lines = read_notes([notes[s] for s in range(count)], count, width)
            vec[0:8] = lines[0]
            for b in range(4):
                vec[8 + b : 9 + b] = lines[1 + b]
        low = (hat * vec[0:1] + vec[2:3]).astype(LOW)
        normed[...] = low
        if loading:
            loader.wait(0)
        queries = mm(low, flat(wq)) + vec[4:5]
        if loading:
            loader.wait(1)
        keys = mm(low, flat(wk))
        if loading:
            loader.wait(2)
        values = mm(low, flat(wv)) + vec[5:6]
        for d in range(SEATS):
            (qp, qs), (kp, ks), (vp, vs) = [tiles_of(x, d) for x in (queries, keys, values)]
            both = join(qs, ks, d)
            for p in range(2):
                span = slice(p * segment, (p + 1) * segment)
                for at, tile in enumerate((qp, kp, vp, both)):
                    blocks[d, p, at * segment : (at + 1) * segment] = tile[span].astype(LOW)
                blocks[d, p, 4 * segment :] = fold(vs[span], d).astype(LOW)
        wait_all(to_seats(blocks, outs, idx, count, out_sems))

    weight = ((count, rows, width), LOW, False)
    tokens = ((2 * segment, width), LOW, None)
    stay = ((2 * segment, width), LOW, False)
    blocks = pltpu.VMEM((SEATS, 2, tall, PAIR), LOW)
    sent = [((2, tall, PAIR), LOW, True)] * SEATS
    if loading:
        out = call(
            body, 7, [idx, *inputs, *flatten(attn)], [SMEM, VMEM, VMEM] + [ANY] * (4 * count),
            sent + [tokens, weight, weight, weight, ((12, width), F32, None)],
            [
                blocks, pltpu.VMEM((2 * segment, width), LOW), pltpu.VMEM((count, NOTE, width), LOW),
                pltpu.SemaphoreType.DMA((4 * count,)), pltpu.SemaphoreType.DMA((SEATS,)),
            ],
        )
        return out[:SEATS], out[SEATS], None, out[SEATS + 1 :]
    out = call(
        body, 7, [idx, *inputs, *given, *attn], [SMEM] + [VMEM] * (2 + len(given) + 4),
        sent + [stay, stay], [blocks, pltpu.SemaphoreType.DMA((SEATS,))],
    )
    return out[:SEATS], out[SEATS], out[SEATS + 1], attn


def read_heads(blocks, segment):
    def joined(at):
        return jnp.concatenate(
            [blocks[i, at * segment : (at + 1) * segment] for i in range(blocks.shape[0])], axis=0
        )

    third = joined(3).astype(F32)
    low = low_lanes(third.shape)
    values = [unfold(blocks[i, 4 * segment :].astype(F32), 0) for i in range(blocks.shape[0])]
    return (
        (joined(0), joined(1), joined(2)),
        (
            jnp.where(low, third, 0.0).astype(LOW), turn(third).astype(LOW),
            jnp.concatenate(values, axis=0).astype(LOW),
        ),
    )


def stacked(rows):
    low = low_lanes(rows.shape)
    zero = jnp.zeros_like(rows)
    return jnp.concatenate([jnp.where(low, rows, zero), jnp.where(low, zero, rows)], axis=0)


def unstacked(rows):
    half = rows.shape[0] // 2
    return jnp.where(low_lanes((half, PAIR)), rows[:half], rows[half:])


def earlier(rows, step):
    row = lax.broadcasted_iota(jnp.int32, (rows, step), 0) % step
    return lax.broadcasted_iota(jnp.int32, (rows, step), 1) <= row


def attend_kernel(count, segment, arrived, at, keep):
    length, step = count * segment, 2 * segment
    tall = block_rows(segment)
    short = segment + segment // 2

    def body(at, *rest):
        ins, outs, rest = rest[:SEATS], rest[SEATS : 2 * SEATS], rest[2 * SEATS :]
        attended, total, blocks, backs, sems, out_sems = rest
        wait_all(in_order(ins, blocks, at, sems, False))
        heads = read_heads(blocks, segment)
        for i in range(length // step):
            span = slice(i * step, (i + 1) * step)
            logs = []
            for g, (queries, keys, values) in enumerate(heads):
                query = queries[span] * SCALING
                if g == 0:
                    query = stacked(query)
                mask = earlier(query.shape[0], step)
                near = jnp.where(mask, mm_nt(query, keys[span]), FLOOR)
                highest = jnp.max(near, axis=-1, keepdims=True)
                if i > 0:
                    far = mm_nt(query, keys[: i * step])
                    highest = jnp.maximum(highest, jnp.max(far, axis=-1, keepdims=True))
                    far = jnp.exp(far - highest)
                near = jnp.exp(near - highest)
                denominator = jnp.sum(near, axis=-1, keepdims=True)
                result = mm(near.astype(LOW), values[span])
                if i > 0:
                    denominator += jnp.sum(far, axis=-1, keepdims=True)
                    result += mm(far.astype(LOW), values[: i * step])
                result = result * (1.0 / denominator)
                log = highest + jnp.log(denominator)
                if g == 0:
                    result = unstacked(result)
                    logs += [log[:step], log[step:]]
                else:
                    logs.append(log)
                attended[g, span] = result
                for p in range(2):
                    tile = result[p * segment : (p + 1) * segment]
                    if g == 0:
                        backs[2 * i + p, :segment] = tile.astype(LOW)
                    else:
                        backs[2 * i + p, segment:] = fold(tile, 0).astype(LOW)
            lane = lax.broadcasted_iota(jnp.int32, (step, PAIR), 1)
            total[span] = jnp.where(lane == 0, logs[0], jnp.where(lane == 1, logs[1], logs[2]))
        wait_all(in_order(outs, backs, at, out_sems, True))

    return call(
        body, 9, [at, *arrived], [SMEM] + [ANY] * SEATS,
        [((2, short, PAIR), LOW, True)] * SEATS,
        [
            pltpu.VMEM((count, tall, PAIR), LOW), pltpu.VMEM((count, short, PAIR), LOW),
            pltpu.SemaphoreType.DMA((2 * SEATS,)), pltpu.SemaphoreType.DMA((2 * SEATS,)),
        ],
        [((2, length, PAIR), F32, False), ((length, PAIR), F32, False)], keep,
    )


def attend_back_kernel(count, segment, arrived, grads, attended, total, at, ties):
    length, step = count * segment, 2 * segment
    tall = block_rows(segment)
    short = segment + segment // 2

    def body(at, attended, total, *rest):
        ins, grad_ins, rest = rest[:SEATS], rest[SEATS : 2 * SEATS], rest[2 * SEATS + len(ties) :]
        outs, rest = rest[:SEATS], rest[SEATS:]
        blocks, grads, backs, of_keys, of_values, sems, grad_sems, out_sems = rest
        first = in_order(ins, blocks, at, sems, False)
        second = in_order(grad_ins, grads, at, grad_sems, False)
        wait_all(first)
        heads = read_heads(blocks, segment)
        wait_all(second)
        for i in reversed(range(length // step)):
            span = slice(i * step, (i + 1) * step)
            third = None
            for g, (queries, keys, values) in enumerate(heads):
                query = queries[span] * SCALING
                if g == 0:
                    grad = jnp.concatenate([grads[2 * i + p, :segment] for p in range(2)], axis=0)
                    dots = grad.astype(F32) * attended[0, span]
                    low = low_lanes(dots.shape)
                    dots = jnp.concatenate([jnp.where(low, dots, 0.0), jnp.where(low, 0.0, dots)], axis=0)
                    log = jnp.concatenate([total[span, 0:1], total[span, 1:2]], axis=0)
                    query, grad = stacked(query), stacked(grad)
                else:
                    grad = jnp.concatenate(
                        [unfold(grads[2 * i + p, segment:].astype(F32), 0) for p in range(2)], axis=0
                    )
                    dots = grad * attended[1, span]
                    grad = grad.astype(LOW)
                    log = total[span, 2:3]
                dots = jnp.sum(dots, axis=-1, keepdims=True)
                parts = [(span, True)] + ([(slice(0, i * step), False)] if i > 0 else [])
                of_queries = None
                for keyed, near in parts:
                    weights = jnp.exp(mm_nt(query, keys[keyed]) - log)
                    if near:
                        weights = jnp.where(earlier(query.shape[0], step), weights, 0.0)
                    grad_scores = (weights * (mm_nt(grad, values[keyed]) - dots)).astype(LOW)
                    term = mm(grad_scores, keys[keyed])
                    of_queries = term if of_queries is None else of_queries + term
                    key_term = mm_tn(grad_scores, query)
                    value_term = mm_tn(weights.astype(LOW), grad)
                    if i == length // step - 1:
                        of_keys[g, keyed] = key_term
                        of_values[g, keyed] = value_term
                    else:
                        of_keys[g, keyed] += key_term
                        of_values[g, keyed] += value_term
                of_queries = of_queries * SCALING
                if g == 0:
                    of_queries = unstacked(of_queries)
                    for p in range(2):
                        backs[2 * i + p, :segment] = of_queries[p * segment : (p + 1) * segment].astype(LOW)
                else:
                    third = of_queries
            low = low_lanes((segment, PAIR))
            for p in range(2):
                own = slice(i * step + p * segment, i * step + (p + 1) * segment)
                block = backs.at[2 * i + p]
                block[segment : 2 * segment] = of_keys[0, own].astype(LOW)
                block[2 * segment : 3 * segment] = of_values[0, own].astype(LOW)
                block[3 * segment : 4 * segment] = join(
                    third[p * segment : (p + 1) * segment], of_keys[1, own], 0
                ).astype(LOW)
                block[4 * segment :] = fold(of_values[1, own], 0).astype(LOW)
        wait_all(in_order(outs, backs, at, out_sems, True))

    return call(
        body, 14, [at, attended, total, *arrived, *grads, *ties],
        [SMEM, VMEM, VMEM] + [ANY] * (2 * SEATS + len(ties)),
        [((2, tall, PAIR), LOW, True)] * SEATS,
        [
            pltpu.VMEM((count, tall, PAIR), LOW), pltpu.VMEM((count, short, PAIR), LOW),
            pltpu.VMEM((count, tall, PAIR), LOW), pltpu.VMEM((2, length, PAIR), F32),
            pltpu.VMEM((2, length, PAIR), F32), pltpu.SemaphoreType.DMA((2 * SEATS,)),
            pltpu.SemaphoreType.DMA((2 * SEATS,)), pltpu.SemaphoreType.DMA((2 * SEATS,)),
        ],
    )


def feed_rows(mid, vec, wf, wp, active, slope, wait):
    width = mid.shape[1]
    hat, scale = centre(mid)
    low = (hat * vec[1:2] + vec[3:4]).astype(LOW)
    for b in range(4):
        wait(b)
        span = slice(b * width, (b + 1) * width)
        u = mm(low, flat(wf.at[b])) + vec[8 + b : 9 + b]
        square = u * u
        t = jnp.tanh(u * (GELU_A + GELU_A * GELU_B * square))
        half = 0.5 + 0.5 * t
        active[:, span] = (u * half).astype(LOW)
        if slope is not None:
            slope[:, span] = (
                half + u * (0.5 - 0.5 * t * t) * (GELU_A + 3.0 * GELU_A * GELU_B * square)
            ).astype(LOW)
    wait(4)
    return low, hat, scale, (mid + mm(active[...], flat(wp)) + vec[7:8]).astype(LOW)


def feed_kernel(count, segment, returned, inputs, vec, rings, idx):
    width = inputs.shape[1]
    rows, tokens = width // count, 2 * segment
    short = segment + segment // 2

    def body(idx, x, vec, *rest):
        back, chunks, rest = rest[:SEATS], rest[SEATS : SEATS + 8 * count], rest[SEATS + 8 * count :]
        output, wo, wf, wp, blocks, active, sems, in_sems = rest
        loader = Loader(sems)
        copies = from_seats(back, blocks, idx, count, in_sems)
        load_output(loader, idx, count, rows, chunks, wo)
        load_feed(loader, idx, count, rows, chunks[4 * count :], wf, wp)
        wait_all(copies)
        low = read_returned(blocks, segment).astype(LOW)
        loader.wait(5)
        mid = x[...].astype(F32) + mm(low, flat(wo)) + vec[6:7]
        output[...] = feed_rows(mid, vec, wf, wp, active, None, loader.wait)[3]

    return call(
        body, 10, [idx, inputs, vec, *returned, *flatten(rings)],
        [SMEM, VMEM, VMEM] + [ANY] * (SEATS + 8 * count),
        [
            ((tokens, width), LOW, None), ((count, rows, width), LOW, False),
            ((4, count, rows, width), LOW, False), ((count, 4, rows, width), LOW, False),
        ],
        [
            pltpu.VMEM((SEATS, 2, short, PAIR), LOW), pltpu.VMEM((tokens, 4 * width), LOW),
            pltpu.SemaphoreType.DMA((9 * count,)), pltpu.SemaphoreType.DMA((SEATS,)),
        ],
    )


def read_returned(blocks, segment):
    pairs, singles = [], []
    for d in range(SEATS):
        pairs.append(jnp.concatenate([blocks[d, p, :segment].astype(F32) for p in range(2)], axis=0))
        singles.append(
            jnp.concatenate([unfold(blocks[d, p, segment:].astype(F32), d) for p in range(2)], axis=0)
        )
    return whole_rows(pairs, singles)


def feed_back_rows(wide, hat, scale, slope, vec, wo, wf, wp, gh, sums, blocks, segment):
    width = wide.shape[1]
    branch = wide.astype(LOW)
    weight = flat(wp)
    back = jnp.zeros(wide.shape, F32)
    for b in range(4):
        span = slice(b * width, (b + 1) * width)
        ga = mm_nt(branch, weight[span])
        low = (ga * slope[:, span].astype(F32)).astype(LOW)
        if sums is not None:
            gh[:, span] = low
            sums[3 + b : 4 + b] = jnp.sum(low.astype(F32), axis=0, keepdims=True)
        back += mm_nt(low, flat(wf.at[b]))
    total = wide + centre_back(back * vec[1:2], hat, scale)
    low = total.astype(LOW)
    values = mm_nt(low, flat(wo))
    for d in range(SEATS):
        pair, single = tiles_of(values, d)
        for p in range(2):
            part = slice(p * segment, (p + 1) * segment)
            blocks[d, p, :segment] = pair[part].astype(LOW)
            blocks[d, p, segment:] = fold(single[part], d).astype(LOW)
    if sums is not None:
        sums[0:1] = jnp.sum(back * hat, axis=0, keepdims=True)
        sums[1:2] = jnp.sum(back, axis=0, keepdims=True)
        sums[2:3] = jnp.sum(low.astype(F32), axis=0, keepdims=True)
        sums[7:8] = jnp.sum(wide, axis=0, keepdims=True)
    return total, low


def turn_kernel(count, segment, returned, inputs, vec, weights, grads, idx):
    width = inputs.shape[1]
    tokens = 2 * segment
    short = segment + segment // 2

    def body(idx, x, vec, wo, wf, wp, first, second, *rest):
        back, outs, rest = rest[:SEATS], rest[SEATS : 2 * SEATS], rest[2 * SEATS :]
        output, attended, middle, normed, slope, active, grad_middle, blocks, in_sems, out_sems = rest
        wait_all(from_seats(back, blocks, idx, count, in_sems))
        low = read_returned(blocks, segment).astype(LOW)
        attended[...] = low
        mid = x[...].astype(F32) + mm(low, flat(wo)) + vec[6:7]
        middle[...] = mid
        normed[...], hat, scale, output[...] = feed_rows(
            mid, vec, wf, wp, active, slope, lambda key: None
        )
        wide = jnp.concatenate([first[...], second[...]], axis=0).astype(F32)
        grad_middle[...] = feed_back_rows(
            wide, hat, scale, slope, vec, wo, wf, wp, None, None, blocks, segment
        )[0]
        wait_all(to_seats(blocks, outs, idx, count, out_sems))

    rows = ((tokens, width), LOW, False)
    return call(
        body, 10, [idx, inputs, vec, *weights, *grads, *returned],
        [SMEM] + [VMEM] * 7 + [ANY] * SEATS,
        [((2, short, PAIR), LOW, True)] * SEATS
        + [
            ((tokens, width), LOW, None), rows, ((tokens, width), F32, False), rows,
            ((tokens, 4 * width), LOW, False), ((tokens, 4 * width), LOW, False),
            ((tokens, width), F32, False),
        ],
        [
            pltpu.VMEM((SEATS, 2, short, PAIR), LOW), pltpu.SemaphoreType.DMA((SEATS,)),
            pltpu.SemaphoreType.DMA((SEATS,)),
        ],
    )


def feed_back_kernel(count, segment, grads, hopped, saved, weights, idx):
    width = grads[0].shape[1]
    tokens = 2 * segment
    short = segment + segment // 2

    def body(idx, first, second, hopped, middle, slope, vec, wo, wf, wp, *rest):
        outs, rest = rest[:SEATS], rest[SEATS:]
        grad_middle, mine, theirs, sums, grad_out, blocks, gh, out_sems = rest
        wide = jnp.concatenate([first[...], second[...]], axis=0).astype(F32)
        wide = jnp.where(idx[count + 1] == 1, wide, hopped[...].astype(F32))
        hat, scale = centre(middle[...])
        grad_middle[...], grad_out[...] = feed_back_rows(
            wide, hat, scale, slope, vec, wo, wf, wp, gh, sums, blocks, segment
        )
        copies = to_seats(blocks, outs, idx, count, out_sems)
        branch = wide.astype(LOW)

        def part(values, core):
            half = values.shape[1] // 2
            return values[:, core * half : (core + 1) * half]

        def fill(rep):
            for ref, core in ((mine, rep), (theirs, 1 - rep)):
                ref[:, : 2 * width] = part(gh, core)
                ref[:, 2 * width :] = part(branch, core)

        for rep in range(2):
            pl.when(idx[count] == rep)(functools.partial(fill, rep))

        wait_all(copies)

    return call(
        body, 14,
        [
            idx, *grads, hopped, saved.middle, saved.slope, saved.vec,
            *weights,
        ],
        [SMEM] + [VMEM] * 9,
        [((2, short, PAIR), LOW, True)] * SEATS
        + [
            ((tokens, width), F32, None), ((tokens, 5 * width // 2), LOW, None),
            ((tokens, 5 * width // 2), LOW, None), ((8, width), F32, None), ((tokens, width), LOW, None),
        ],
        [
            pltpu.VMEM((SEATS, 2, short, PAIR), LOW), pltpu.VMEM((tokens, 4 * width), LOW),
            pltpu.SemaphoreType.DMA((SEATS,)),
        ],
    )


def project_back_kernel(count, segment, returned, grad_middle, grad_out, saved, weights, idx, keep):
    tokens, width = grad_middle.shape
    rows = width // count
    tall = block_rows(segment)
    kept = [grad_out] if keep else []

    def body(idx, grad_middle, x, vec, *rest):
        held, rest = rest[: len(kept)], rest[len(kept) :]
        back, rest = rest[:SEATS], rest[SEATS:]
        (wq, wk, wv), rest = rest[:3], rest[3:]
        grad_low, grad_in, mine, theirs, sums, blocks, in_sems = rest
        copies = from_seats(back, blocks, idx, count, in_sems)
        hat, scale = centre(x[...].astype(F32))
        wait_all(copies)
        pairs, singles = [[], [], []], [[], [], []]
        for d in range(SEATS):
            for at in range(3):
                pairs[at].append(
                    jnp.concatenate(
                        [blocks[d, p, at * segment : (at + 1) * segment].astype(F32) for p in range(2)], axis=0
                    )
                )
            both = [split(blocks[d, p, 3 * segment : 4 * segment].astype(F32), d) for p in range(2)]
            for at in range(2):
                singles[at].append(jnp.concatenate([b[at] for b in both], axis=0))
            singles[2].append(
                jnp.concatenate([unfold(blocks[d, p, 4 * segment :].astype(F32), d) for p in range(2)], axis=0)
            )
        gq, gk, gv = [whole_rows(a, b).astype(LOW) for a, b in zip(pairs, singles)]
        total = mm_nt(gq, flat(wq))
        total += mm_nt(gk, flat(wk))
        total += mm_nt(gv, flat(wv))
        result = grad_middle[...] + centre_back(total * vec[0:1], hat, scale)
        grad_low[...] = result.astype(LOW)
        if not keep:
            return
        grad_in[...] = result
        sums[0:1] = jnp.sum(total * hat, axis=0, keepdims=True)
        sums[1:2] = jnp.sum(total, axis=0, keepdims=True)
        sums[2:3] = jnp.sum(gq.astype(F32), axis=0, keepdims=True)
        sums[3:4] = jnp.sum(gv.astype(F32), axis=0, keepdims=True)
        sums[4:8] = jnp.zeros((4, width), F32)
        (grad_out,) = held

        def fill(first, second):
            first[:, :width] = gq
            first[:, width:] = gk
            second[:, :width] = gv
            second[:, width:] = grad_out[...]

        @pl.when(idx[count] == 0)
        def _():
            fill(mine, theirs)

        @pl.when(idx[count] == 1)
        def _():
            fill(theirs, mine)

    return call(
        body, 8, [idx, grad_middle, saved.inputs, saved.vec, *kept, *returned, *weights],
        [SMEM] + [VMEM] * (3 + len(kept)) + [ANY] * SEATS + [VMEM] * 3,
        [((tokens, width), LOW, None)],
        [
            pltpu.VMEM((SEATS, 2, tall, PAIR), LOW), pltpu.SemaphoreType.DMA((SEATS,)),
        ],
        [
            ((tokens, width), F32, None), ((tokens, 2 * width), LOW, None),
            ((tokens, 2 * width), LOW, None), ((8, width), F32, None),
        ],
        keep,
    )


def send_out(scratch, pieces, idx, sems, start):
    for at, (out, to, rows, base, stride, k) in enumerate(pieces):
        source = pl.ds(pl.multiple_of(base + idx[k] * stride, 16), rows)
        copy = pltpu.make_async_copy(scratch.at[source], out.at[pl.ds(to, rows)], sems.at[at])
        copy.start() if start else copy.wait()


def rows_of(refs, span=slice(None)):
    return jnp.concatenate([ref[:, span] for ref in refs], axis=0)


def ffn_terms_kernel(count, normed, active, late, idx):
    width = normed[0].shape[1]
    rows, half = width // count, width // 2

    def body(idx, *rest):
        normed, active, late, rest = rest[:2], rest[2:4], rest[4:6], rest[6:]
        outs, (inward, outward, sems) = rest[: 2 * count], rest[2 * count :]
        narrow = rows_of(normed)
        pieces = []
        for b in range(2):
            inward[b * width : (b + 1) * width] = mm_tn(
                narrow, rows_of(late, slice(b * width, (b + 1) * width))
            ).astype(LOW)
            pieces.append([(outs[k], b * rows, rows, b * width, rows, k) for k in range(count)])
            send_out(inward, pieces[b], idx, sems.at[pl.ds(b * count, count)], True)
        branch = rows_of(late, slice(2 * width, 2 * width + half))
        for b in range(4):
            span = slice(b * width, (b + 1) * width)
            outward[span] = mm_tn(rows_of(active, span), branch).astype(LOW)
        pieces.append([(outs[count + k], 0, 4 * rows, 0, 4 * rows, k) for k in range(count)])
        send_out(outward, pieces[2], idx, sems.at[pl.ds(2 * count, count)], True)
        for b, scratch in enumerate((inward, inward, outward)):
            send_out(scratch, pieces[b], idx, sems.at[pl.ds(b * count, count)], False)

    outs = call(
        body, 5, [idx, *normed, *active, *late], [SMEM] + [VMEM] * 6,
        [((2 * rows, width), LOW, True)] * count + [((4 * rows, half), LOW, True)] * count,
        [
            pltpu.VMEM((2 * width, width), LOW), pltpu.VMEM((4 * width, half), LOW),
            pltpu.SemaphoreType.DMA((3 * count,)),
        ],
    )
    return outs[:count], outs[count:]


def attn_terms_kernel(count, normed, attended, late, sums_one, sums_two, idx):
    width = normed[0].shape[1]
    rows = width // count

    def body(idx, *rest):
        normed, attended, late, (one, two), rest = rest[:2], rest[2:4], rest[4:6], rest[6:8], rest[8:]
        outs, (scratch, notes, sems, note_sems) = rest[: 2 * count], rest[2 * count :]

        def pieces(b):
            return [(outs[b * count + k], 0, rows, b * width, rows, k) for k in range(count)]

        flatly = jnp.concatenate(
            [
                one[0:1], two[0:1], one[1:2], two[1:2], one[2:3], one[3:4], two[2:3], two[7:8],
                jnp.zeros((NOTE - 8, width), F32),
            ],
            axis=0,
        )
        lane = lax.broadcasted_iota(jnp.int32, (NOTE, width), 1)
        line = lax.broadcasted_iota(jnp.int32, (NOTE, width), 0)
        for s in range(count):
            note = pltpu.roll(flatly, width - s * rows, 1) if s else flatly
            start = 4 * rows * s
            hidden = two[3 + start // width : 4 + start // width]
            hidden = pltpu.roll(
                jnp.broadcast_to(hidden, (8, width)), (width - start % width) % width, 1
            )
            hidden = jnp.concatenate([hidden, hidden], axis=0)
            note = jnp.where(
                (line < 8) & (lane < rows), note,
                jnp.where((line == NOTE - 1) & (lane < 4 * rows), hidden, 0.0),
            )
            notes[s] = note.astype(LOW)
        copies = start_all(
            [
                pltpu.make_async_copy(
                    notes.at[idx[k]], outs[k].at[pl.ds(rows, NOTE)], note_sems.at[k]
                )
                for k in range(count)
            ]
        )
        for b in range(2):
            grads = rows_of(late, slice(b * width, (b + 1) * width))
            if b == 0:
                scratch[:width] = mm_tn(rows_of(normed), grads).astype(LOW)
            else:

                @pl.when(idx[count] == 0)
                def _():
                    scratch[width:] = mm_tn(rows_of(normed), grads).astype(LOW)

                @pl.when(idx[count] == 1)
                def _():
                    scratch[width:] = mm_tn(rows_of(attended), grads).astype(LOW)

            send_out(scratch, pieces(b), idx, sems.at[pl.ds(b * count, count)], True)
        for b in range(2):
            send_out(scratch, pieces(b), idx, sems.at[pl.ds(b * count, count)], False)
        wait_all(copies)

    outs = call(
        body, 5, [idx, *normed, *attended, *late, sums_one, sums_two], [SMEM] + [VMEM] * 8,
        [((rows + NOTE, width), LOW, True)] * count + [((rows, width), LOW, True)] * count,
        [
            pltpu.VMEM((2 * width, width), LOW), pltpu.VMEM((count, NOTE, width), LOW),
            pltpu.SemaphoreType.DMA((2 * count,)), pltpu.SemaphoreType.DMA((count,)),
        ],
    )
    return outs[:count], outs[count:]


class Rings:
    def __init__(self, rings):
        self.rings = rings

    def step(self, *after):
        for ring in self.rings:
            ring.step(*after)

    @property
    def last(self):
        return [v for ring in self.rings for v in ring.last if v is not None]


def hold(values, *after):
    return lax.optimization_barrier((values, after))[0] if len(after) else values


class GatherRing:
    def __init__(self, chunk, count, rightward):
        self.right, self.left = ring_pairs(count)
        self.count, self.rightward, self.at = count, rightward, 0
        self.last = (chunk, chunk)
        self.own = {0: chunk}
        self.twin = {}

    def pass_on(self, *after):
        places = [k for k in self.own if k not in self.twin]
        for k, value in zip(places, hold([self.own[k] for k in places], *after)):
            self.twin[k] = swap(value, REPLICA)

    def step(self, *after):
        near, far = hold(self.last, *after)
        self.at += 1
        if self.at < self.count // 2:
            near = lax.ppermute(near, SHARD, self.right)
            far = lax.ppermute(far, SHARD, self.left)
            self.own[self.count - self.at], self.own[self.at] = near, far
            self.last = (near, far)
        else:
            if self.rightward:
                last = lax.ppermute(near, SHARD, self.right)
            else:
                last = lax.ppermute(far, SHARD, self.left)
            self.own[self.at] = last
            self.last = (last,)

    def lists(self):
        self.pass_on()
        return [[side[k] for k in range(self.count)] for side in (self.own, self.twin)]


class ScatterRing:
    def __init__(self, pieces, count, rightward):
        self.right, self.left = ring_pairs(count)
        self.pieces, self.count, self.rightward = pieces, count, rightward
        self.at = count // 2
        self.last = None

    def step(self, *after):
        pieces, half = self.pieces, self.count // 2
        if self.at == half:
            far = hold(pieces[half], *after)
            if self.rightward:
                self.last = (lax.ppermute(far, SHARD, self.right), None)
            else:
                self.last = (None, lax.ppermute(far, SHARD, self.left))
        else:
            last = hold([v for v in self.last if v is not None], *after)
            sides = []
            for piece, term in zip((pieces[self.at], pieces[self.count - self.at]), self.last):
                sides.append(piece if term is None else add_low(piece, last.pop(0)))
            if len(after) > 0 and None in self.last:
                sides = hold(sides, *after)
            self.last = (
                lax.ppermute(sides[0], SHARD, self.right), lax.ppermute(sides[1], SHARD, self.left)
            )
        self.at -= 1

    def total(self):
        return self.pieces[0].astype(F32) + self.last[0].astype(F32) + self.last[1].astype(F32)


def fast_device(
    tokens, cotangent, group_order, norm_gains, norm_biases, w_qkv, qv_bias, w_out, out_bias,
    w_fc, fc_bias, w_proj, proj_bias,
):
    count = lax.axis_size(SHARD)
    section = lax.axis_index(SECTION)
    replica = lax.axis_index(REPLICA)
    shard = lax.axis_index(SHARD)
    segment, width = tokens.shape[1], tokens.shape[2]
    rows = w_qkv.shape[1]
    half = count // 2
    order = ring_order(count)
    position = jnp.asarray(np.argsort(np.array(order)), jnp.int32)[shard]
    around = lax.rem(position + jnp.arange(count, dtype=jnp.int32), count)
    seat = 2 * replica + lax.rem(shard, 2)
    others = seat ^ jnp.arange(SEATS, dtype=jnp.int32)
    idx = jnp.concatenate(
        [jnp.asarray(order, jnp.int32)[around], jnp.stack([replica, section]).astype(jnp.int32), others]
    )

    ways = [
        [
            (r * count + 2 * z + y, (z // 2) * count + 2 * (2 * r + (z + j) % 2) + y)
            for r in range(2) for z in range(half) for y in range(2)
        ]
        for j in range(2)
    ]
    odd = lax.rem(shard // 2, 2)

    def gather_in(x, j, *more):
        own = lax.dynamic_index_in_dim(x, lax.rem(odd + j, 2), 0, keepdims=False)
        own = jnp.concatenate([own, *more], axis=0) if more else own
        return lax.ppermute(own, (REPLICA, SHARD), ways[j])

    def give_back(x):
        return [
            lax.ppermute(
                x[j * segment : (j + 1) * segment], (REPLICA, SHARD), [(b, a) for a, b in ways[j]]
            )
            for j in range(2)
        ]

    def by_sequence(parts):
        return jnp.stack([jnp.where(even, *parts), jnp.where(even, *parts[::-1])])[None]

    def exchange(parts):
        diagonal = [(r * count + s, (1 - r) * count + (s ^ 1)) for r in range(2) for s in range(count)]
        return [
            pltpu.with_memory_space_constraint(parts[0], pltpu.HBM),
            lax.ppermute(parts[1], SHARD, [(s, s ^ 1) for s in range(count)]),
            swap(parts[2], REPLICA),
            lax.ppermute(parts[3], (REPLICA, SHARD), diagonal),
        ]

    small = jnp.concatenate(
        [norm_gains[0], norm_biases[0], qv_bias[0], out_bias, fc_bias.reshape(4, rows), proj_bias],
        axis=0,
    )
    qkv = w_qkv[0]
    attn_own = [
        jnp.concatenate(
            [jnp.where(replica == 0, qkv[:, :width], qkv[:, 2 * width :]), note_rows(small, width)], axis=0
        ),
        jnp.where(replica == 0, qkv[:, width : 2 * width], w_out[0]),
    ]
    ffn_own = [
        jnp.where(
            replica == 0,
            jnp.concatenate([w_fc[0][:, b * width : (b + 1) * width] for b in (2 * i, 2 * i + 1)], axis=0),
            w_proj[0][2 * i * rows : 2 * (i + 1) * rows],
        )
        for i in range(2)
    ]

    attn_ring = Rings([GatherRing(own, count, i == 0) for i, own in enumerate(attn_own)])
    attn_ring.step()
    order_row = lax.dynamic_index_in_dim(group_order, odd, 0).astype(LOW)
    order_rows = jnp.pad(order_row, ((0, NOTE - 1), (0, width - count)))
    tokens = hold(tokens, attn_ring.last)
    packed = [gather_in(tokens, 0, order_rows), gather_in(tokens, 1)]
    slot = lax.rem(shard // 2 + jnp.arange(2, dtype=jnp.int32), 2)
    which = ((4 * (others // 2) + others % 2)[:, None] + 2 * slot[None, :]).reshape(-1)
    chosen = (which[:, None] == jnp.arange(count, dtype=jnp.int32)[None, :]).astype(jnp.int32)
    packed, chosen, even = lax.optimization_barrier((packed, chosen, odd == 0))
    blocks_at = packed[0][segment, :count].astype(jnp.int32)
    at = jnp.sum(chosen * blocks_at[None, :], axis=1)
    attn_ring.step()
    attn_ring.step()
    ffn_ring = Rings(
        [GatherRing(hold(own, attn_ring.last), count, i == 0) for i, own in enumerate(ffn_own)]
    )
    ffn_ring.step()
    attn_ring.step()
    for ring in attn_ring.rings:
        ring.pass_on(attn_ring.last)
    attn_lists = [ring.lists() for ring in attn_ring.rings]

    def forward(hopped, attn, before):
        sent, inputs, normed, attn = project_kernel(count, segment, packed, hopped, attn, idx)
        arrived = exchange(before[0](sent))
        back = attend_kernel(count, segment, before[1](arrived), at, hopped is not None)
        state = Bag(vec=attn[3], inputs=inputs, normed=normed, arrived=arrived)
        return state, attn, exchange(before[2](back[:SEATS])), back[SEATS:]

    def ring_sent(sent):
        ffn_ring.step(sent[1])
        return sent

    def ring_arrived(arrived):
        ffn_ring.step(arrived[1])
        return arrived

    def ring_back(back):
        ffn_ring.step(back[1])
        return back

    def ring_feed():
        for ring in ffn_ring.rings:
            ring.pass_on(ffn_ring.last)
        return [ring.lists() for ring in ffn_ring.rings]

    def same(values):
        return values

    first, attn, returned, _ = forward(None, attn_lists, [ring_sent, ring_arrived, ring_back])
    output, *ffn = feed_kernel(
        count, segment, returned, first.inputs, first.vec,
        attn_lists + ring_feed(), idx,
    )

    def hop(values, backward):
        return lax.ppermute(values, SECTION, [(1, 0)] if backward else [(0, 1)])

    upstream = [gather_in(hold(cotangent, output), j) for j in range(2)]
    state, attn, returned, kept = forward(
        hop(output, False), attn, [same, lambda arrived: hold(arrived, upstream), same]
    )
    state.attended, state.total = kept
    *sent, output, state.attended_low, state.middle, state.normed_two, state.slope, state.active, grad_middle = (
        turn_kernel(count, segment, returned, state.inputs, state.vec, ffn, upstream, idx)
    )
    kept_rows = state.normed_two, state.active, state.normed, state.attended_low
    pairs, acts = [], []

    def aside(back):
        pairs.extend([own, swap(hold(own, back[0]), REPLICA)] for own in kept_rows)
        acts.extend(give_back(hold(output, back[0])))
        return back

    def backward(sent, grad_middle, grad_out, keep, ties, between):
        arrived = exchange(sent)
        ties = ties + between[0](arrived)
        back = attend_back_kernel(
            count, segment, state.arrived, arrived, state.attended, state.total, at, ties
        )
        returned = exchange(between[1](back))
        return project_back_kernel(
            count, segment, between[2](returned), grad_middle, grad_out, state, attn[:3], idx, keep
        )

    early = backward(
        sent, grad_middle, None, False, [],
        [lambda arrived: [], aside, same],
    )
    hopped, acts, pairs = lax.optimization_barrier((hop(early[0], True), acts, pairs))
    acts = by_sequence(acts)
    rings = []
    *sent, grad_middle, mine, theirs, sums_two, grad_out = feed_back_kernel(
        count, segment, upstream, hopped, state, ffn, idx
    )

    def ffn_terms(arrived):
        terms = ffn_terms_kernel(
            count, pairs[0], pairs[1], hold([mine, swap(theirs, REPLICA)], arrived), idx
        )
        rings.append(Rings([ScatterRing(t, count, i == 0) for i, t in enumerate(terms)]))
        rings[0].step()
        return [terms[0][0]]

    def ring_back(back):
        back = hold(back, rings[0].last)
        rings[0].step(back[0])
        return back

    low, *last = backward(sent, grad_middle, grad_out, True, [], [ffn_terms, ring_back, same])
    own, got, sums_one = hold((last[1], swap(last[2], REPLICA), last[3]), rings[0].last)
    terms = attn_terms_kernel(count, pairs[2], pairs[3], [own, got], sums_one, sums_two, idx)
    rings.append(Rings([ScatterRing(t, count, i == 0) for i, t in enumerate(terms)]))
    rings[0].step()
    rings[1].step()
    rings[1].step()
    rings[0].step()
    in_grads = give_back(hold(last[0].astype(LOW), rings[1].last))
    rings[1].step()
    rings[1].step()
    in_grads = by_sequence(hold(in_grads, rings[1].last)).astype(F32)

    def finished(ring):
        total = ring.total().astype(LOW)
        twin = swap(total, REPLICA)
        return (
            jnp.where(replica == 0, total, twin).astype(F32),
            jnp.where(replica == 0, twin, total).astype(F32),
        )

    feed_totals, totals = [[finished(ring) for ring in pair.rings] for pair in rings]
    fc_grad = jnp.concatenate(
        [part[b * rows : (b + 1) * rows] for part in feed_totals[0] for b in range(2)], axis=1
    )
    proj_grad = jnp.concatenate(feed_totals[1], axis=1)
    qkv_grad = jnp.concatenate([totals[0][0][:rows], totals[1][0], totals[0][1][:rows]], axis=1)
    note = totals[0][0][rows:] + totals[0][1][rows:]
    vec = note[:8, :rows]
    return (
        acts, in_grads, vec[0:2][None], vec[2:4][None], qkv_grad[None], vec[4:6][None],
        totals[1][1][None], vec[6][None], fc_grad[None], note[NOTE - 1, : 4 * rows][None],
        proj_grad[None], vec[7][None],
    )


def on_each(tokens, *others):
    count = lax.axis_size(SHARD)
    tiles = (tokens.shape[2] // count) % 32 == 0 and tokens.shape[1] % 64 == 0
    seats = count == 2 * SEATS and tokens.shape[0] == 2 and HEADS == 3 * SEATS
    return (fast_device if tiles and seats else on_device)(tokens, *others)


def solution(mesh):
    in_specs = (
        P(REPLICA, SHARD, None),
        P(REPLICA, SHARD, None),
        P(REPLICA, None),
        P(SECTION, None, SHARD),
        P(SECTION, None, SHARD),
        P(SECTION, SHARD, None),
        P(SECTION, None, SHARD),
        P(SECTION, SHARD, None),
        P(SECTION, SHARD),
        P(SECTION, SHARD, None),
        P(SECTION, SHARD),
        P(SECTION, SHARD, None),
        P(SECTION, SHARD),
    )
    out_specs = (
        P(SECTION, REPLICA, SHARD, None),
        P(SECTION, REPLICA, SHARD, None),
        P(SECTION, None, SHARD),
        P(SECTION, None, SHARD),
        P(SECTION, SHARD, None),
        P(SECTION, None, SHARD),
        P(SECTION, SHARD, None),
        P(SECTION, SHARD),
        P(SECTION, SHARD, None),
        P(SECTION, SHARD),
        P(SECTION, SHARD, None),
        P(SECTION, SHARD),
    )
    return jax.shard_map(
        on_each, mesh=mesh, in_specs=in_specs, out_specs=out_specs, check_vma=False
    )
```

```python
import functools
import math
from types import SimpleNamespace as Bag

import jax
import jax.numpy as jnp
import numpy as np
from jax import lax
from jax.experimental import pallas as pl
from jax.experimental.pallas import tpu as pltpu
from jax.sharding import PartitionSpec as P

HEADS = 12
HEAD = 64
EPSILON = 1e-05
SCALING = 0.125
FLOOR = -1e30
SECTION, REPLICA, SHARD = "section", "replica", "shard"
LOW = jnp.bfloat16
F32 = jnp.float32


def ring_order(count):
    return list(range(0, count, 2)) + list(range(count - 1, 0, -2))


def ring_pairs(count):
    order = ring_order(count)
    right = [(order[i], order[(i + 1) % count]) for i in range(count)]
    return right, [(b, a) for a, b in right]


def ring_gather(chunk, count):
    right, left = ring_pairs(count)
    got = {0: chunk}
    from_left = from_right = chunk
    cut = chunk.shape[0] // 32 * 16
    for step in range(1, count // 2 + 1):
        if step == count // 2:
            got[step] = jnp.concatenate(
                [
                    lax.ppermute(from_left[:cut], SHARD, right),
                    lax.ppermute(from_right[cut:], SHARD, left),
                ],
                axis=0,
            )
        else:
            from_left = lax.ppermute(from_left, SHARD, right)
            from_right = lax.ppermute(from_right, SHARD, left)
            got[count - step] = from_left
            got[step] = from_right
    return [got[k] for k in range(count)]


def ring_scatter(piece, rows, count):
    right, left = ring_pairs(count)
    cut = rows // 32 * 16
    half = count // 2
    far = piece(half)
    to_right = lax.ppermute(far[:cut], SHARD, right)
    to_left = lax.ppermute(far[cut:], SHARD, left)
    for distance in range(half - 1, 0, -1):
        first, second = piece(distance), piece(count - distance)
        if distance == half - 1:
            first = jnp.concatenate([add_low(first[:cut], to_right), first[cut:]], axis=0)
            second = jnp.concatenate([second[:cut], add_low(second[cut:], to_left)], axis=0)
        else:
            first = add_low(first, to_right)
            second = add_low(second, to_left)
        to_right = lax.ppermute(first, SHARD, right)
        to_left = lax.ppermute(second, SHARD, left)
    return piece(0).astype(F32) + to_right.astype(F32) + to_left.astype(F32)


def add_low(a, b):
    return (a.astype(F32) + b.astype(F32)).astype(LOW)


def swap(x, axis):
    return lax.ppermute(x, axis, [(0, 1), (1, 0)])


def normalize(values, gain_row, offset):
    average = jnp.mean(values, axis=-1, keepdims=True)
    centred = values - average
    variance = jnp.mean(centred * centred, axis=-1, keepdims=True)
    return centred * lax.rsqrt(variance + EPSILON) * gain_row + offset


def gelu_tanh(values):
    return jax.nn.gelu(values, approximate=True)


def dot(a, b):
    return jnp.dot(a, b, preferred_element_type=F32)


def dot_t(a, b):
    return lax.dot_general(a, b, (((1,), (1,)), ((), ())), preferred_element_type=F32)


def dot_rows(a, b):
    return lax.dot_general(a, b, (((0,), (0,)), ((), ())), preferred_element_type=F32)


class Plan:
    def __init__(self, count, segment):
        self.count = count
        self.segment = segment
        self.splits = count // math.gcd(HEADS, count)
        self.units = HEADS * self.splits // count
        self.part = segment // self.splits
        self.first = [self.units * q // self.splits for q in range(count)]
        self.slots = max(
            (self.units * q + self.units - 1) // self.splits - self.first[q] + 1
            for q in range(count)
        )
        self.groups = [
            [r * count + h * (count // 2) + i for r in range(2) for i in range(count // 2)]
            for h in range(2)
        ]

    def exchange(self, blocks):
        return lax.all_to_all(
            blocks, (REPLICA, SHARD), 0, 0, tiled=True, axis_index_groups=self.groups
        )

    def pack_units(self, heads):
        parts = heads.reshape(self.splits, self.part, HEADS, HEAD)
        parts = parts.transpose(2, 0, 1, 3).reshape(
            self.count, self.units * self.part, HEAD
        )
        return self.fold(parts)

    def fold(self, parts):
        rows = parts.shape[1] // 2
        return jnp.concatenate([parts[:, :rows], parts[:, rows:]], axis=2)

    def unfold(self, folded):
        return jnp.concatenate([folded[..., :HEAD], folded[..., HEAD:]], axis=1)

    def unpack_units(self, folded):
        parts = self.unfold(folded).reshape(HEADS, self.splits, self.part, HEAD)
        return parts.transpose(1, 2, 0, 3).reshape(self.segment, HEADS * HEAD)

    def gather_units(self, folded):
        parts = self.unfold(folded).reshape(self.count, self.units, self.part, HEAD)
        return parts.transpose(1, 0, 2, 3).reshape(self.units, self.count * self.part, HEAD)

    def scatter_units(self, values):
        parts = values.reshape(self.units, self.count, self.part, HEAD).transpose(1, 0, 2, 3)
        return self.fold(parts.reshape(self.count, self.units * self.part, HEAD))

    def head_slots(self, rows):
        blocks = []
        for q in range(self.count):
            cols = []
            for slot in range(self.slots):
                head = min(self.first[q] + slot, HEADS - 1)
                cols.append(rows[:, head * HEAD : (head + 1) * HEAD])
            blocks.append(jnp.concatenate(cols, axis=1))
        return jnp.stack(blocks)

    def sum_slots(self, blocks):
        cols = []
        for head in range(HEADS):
            total = None
            for q in range(self.count):
                last = (self.units * (q + 1) - 1) // self.splits
                if self.first[q] <= head <= last:
                    slot = head - self.first[q]
                    term = blocks[q, :, slot * HEAD : (slot + 1) * HEAD].astype(F32)
                    total = term if total is None else total + term
            cols.append(total)
        return jnp.concatenate(cols, axis=1)


def over(a, b, dim_a, dim_b):
    return lax.dot_general(a, b, (((dim_a,), (dim_b,)), ((), ())), preferred_element_type=F32)


def over_units(a, b):
    return lax.dot_general(a, b, (((0, 1), (0, 1)), ((), ())), preferred_element_type=F32)


def widen(units, slot, slots):
    wide = jnp.concatenate([units] * slots, axis=2)
    lane_slot = jnp.arange(slots * HEAD, dtype=jnp.int32) // HEAD
    return jnp.where(lane_slot[None, None, :] == slot[:, None, None], wide, jnp.zeros_like(wide))


def narrow(wide, slot, slots):
    lane_slot = jnp.arange(slots * HEAD, dtype=jnp.int32) // HEAD
    wide = jnp.where(lane_slot[None, None, :] == slot[:, None, None], wide, jnp.zeros_like(wide))
    return sum(wide[:, :, s * HEAD : (s + 1) * HEAD] for s in range(slots))


def attend_forward(queries, keys, values, query_pos, key_pos):
    scores = over(queries, keys, 2, 1) * SCALING
    visible = key_pos[None, None, :] <= query_pos[:, :, None]
    scores = jnp.where(visible, scores, FLOOR)
    highest = jnp.max(scores, axis=-1, keepdims=True)
    terms = jnp.exp(scores - highest)
    total = jnp.sum(terms, axis=-1, keepdims=True)
    weights = (terms / total).astype(LOW)
    attended = over(weights, values, 2, 0)
    return attended, highest + jnp.log(total)


def attend_backward(queries, keys, values, query_pos, key_pos, log_total, grad, row_dots):
    scores = over(queries, keys, 2, 1) * SCALING
    visible = key_pos[None, None, :] <= query_pos[:, :, None]
    weights = jnp.where(visible, jnp.exp(scores - log_total), 0.0)
    grad_weights = over(grad, values, 2, 1)
    grad_scores = (weights * (grad_weights - row_dots)).astype(LOW)
    grad_queries = (
        over(grad_scores, keys, 2, 0) * SCALING
    )
    grad_keys = (
        over_units(grad_scores, queries) * SCALING
    )
    grad_values = over_units(weights.astype(LOW), grad)
    return grad_queries, grad_keys, grad_values


def layer_forward(inputs, weights, plan, place):
    normed = normalize(inputs, weights.gains[0], weights.offsets[0]).astype(LOW)
    queries = (dot(normed, weights.q) + weights.q_bias).astype(LOW)
    keys = dot(normed, weights.k).astype(LOW)
    values = (dot(normed, weights.v) + weights.v_bias).astype(LOW)
    segment = inputs.shape[0]
    width = plan.slots * HEAD
    sent = jnp.concatenate(
        [
            plan.head_slots(keys),
            plan.head_slots(values),
            plan.pack_units(queries.reshape(segment, HEADS, HEAD)).reshape(
                plan.count, -1, width
            ),
        ],
        axis=1,
    )
    arrived = plan.exchange(sent)
    length = plan.count * segment
    all_keys = arrived[:, :segment].reshape(length, width)
    all_values = arrived[:, segment : 2 * segment].reshape(length, width)
    units = plan.gather_units(arrived[:, 2 * segment :].reshape(plan.count, -1, 2 * HEAD))
    units = widen(units, place.slot, plan.slots)
    attended, log_total = attend_forward(
        units, all_keys, all_values, place.query_pos, place.key_pos
    )
    attended = narrow(attended, place.slot, plan.slots)
    returned = plan.exchange(plan.scatter_units(attended.astype(LOW)))
    attended_low = plan.unpack_units(returned)
    middle = inputs + dot(attended_low, weights.o) + weights.out_bias
    normed_two = normalize(middle, weights.gains[1], weights.offsets[1]).astype(LOW)
    hidden = dot(normed_two, weights.fc) + weights.fc_bias
    active = gelu_tanh(hidden).astype(LOW)
    output = middle + dot(active, weights.proj) + weights.proj_bias
    saved = Bag(
        inputs=inputs, normed=normed, units=units, keys=all_keys, values=all_values,
        attended=attended, log_total=log_total, attended_low=attended_low, middle=middle,
        normed_two=normed_two, hidden=hidden, active=active,
    )
    return output, saved


def layer_backward(arriving, saved, weights, plan, place):
    segment, model_width = arriving.shape
    grad_branch = arriving.astype(LOW)
    grad_active = dot_t(grad_branch, weights.proj)
    grad_hidden = jax.vjp(gelu_tanh, saved.hidden)[1](grad_active)[0].astype(LOW)
    grad_normed_two = dot_t(grad_hidden, weights.fc)
    grad_middle_norm, gain_two, offset_two = jax.vjp(
        normalize, saved.middle, weights.gains[1], weights.offsets[1]
    )[1](grad_normed_two)
    grads = Bag(
        proj=dot_rows(saved.active, grad_branch),
        proj_bias=jnp.sum(grad_branch.astype(F32), axis=0),
        fc=dot_rows(saved.normed_two, grad_hidden),
        fc_bias=jnp.sum(grad_hidden.astype(F32), axis=0),
    )
    grad_middle = arriving + grad_middle_norm
    grad_out = grad_middle.astype(LOW)
    grad_attended = dot_t(grad_out, weights.o).astype(LOW)
    arrived = plan.exchange(plan.pack_units(grad_attended.reshape(segment, HEADS, HEAD)))
    grad_units = plan.gather_units(arrived)
    row_dots = jnp.sum(grad_units.astype(F32) * saved.attended, axis=-1, keepdims=True)
    grad_queries, grad_keys, grad_values = attend_backward(
        saved.units, saved.keys, saved.values, place.query_pos, place.key_pos,
        saved.log_total, widen(grad_units, place.slot, plan.slots), row_dots,
    )
    grad_queries = narrow(grad_queries, place.slot, plan.slots).astype(LOW)
    width = plan.slots * HEAD
    sent = jnp.concatenate(
        [
            grad_keys.astype(LOW).reshape(plan.count, segment, width),
            grad_values.astype(LOW).reshape(plan.count, segment, width),
            plan.scatter_units(grad_queries).reshape(plan.count, -1, width),
        ],
        axis=1,
    )
    returned = plan.exchange(sent)
    grad_k = plan.sum_slots(returned[:, :segment]).astype(LOW)
    grad_v = plan.sum_slots(returned[:, segment : 2 * segment]).astype(LOW)
    grad_q = plan.unpack_units(returned[:, 2 * segment :].reshape(plan.count, -1, 2 * HEAD))
    grad_normed = (
        dot_t(grad_q, weights.q) + dot_t(grad_k, weights.k) + dot_t(grad_v, weights.v)
    )
    grad_input_norm, gain_one, offset_one = jax.vjp(
        normalize, saved.inputs, weights.gains[0], weights.offsets[0]
    )[1](grad_normed)
    grads = Bag(
        proj=grads.proj, proj_bias=grads.proj_bias, fc=grads.fc, fc_bias=grads.fc_bias,
        gains=jnp.stack([gain_one, gain_two]),
        offsets=jnp.stack([offset_one, offset_two]),
        q=dot_rows(saved.normed, grad_q),
        k=dot_rows(saved.normed, grad_k),
        v=dot_rows(saved.normed, grad_v),
        qv_bias=jnp.stack([jnp.sum(grad_q.astype(F32), axis=0), jnp.sum(grad_v.astype(F32), axis=0)]),
        o=dot_rows(saved.attended_low, grad_out),
        out_bias=jnp.sum(grad_out.astype(F32), axis=0),
    )
    return grad_middle + grad_input_norm, grads


def on_device(
    tokens, cotangent, group_order, norm_gains, norm_biases, w_qkv, qv_bias, w_out, out_bias,
    w_fc, fc_bias, w_proj, proj_bias,
):
    count = lax.axis_size(SHARD)
    section = lax.axis_index(SECTION)
    replica = lax.axis_index(REPLICA)
    shard = lax.axis_index(SHARD)
    segment, model_width = tokens.shape[1], tokens.shape[2]
    rows = w_qkv.shape[1]
    half = count // 2
    plan = Plan(count, segment)
    order = ring_order(count)
    position_of = np.argsort(np.array(order))
    position = jnp.asarray(position_of, jnp.int32)[shard]
    order_table = jnp.asarray(order, jnp.int32)

    def owner(offset):
        return order_table[lax.rem(position + offset, count)]

    home = shard // half
    keeps = home == replica
    crossing = []
    for s in range(half):
        crossing += [(count + s, s + half), (s + half, count + s)]

    def reshard(x):
        moved = lax.ppermute(x, (REPLICA, SHARD), crossing)
        return jnp.where(keeps, x, moved)

    def pick(x):
        return lax.dynamic_index_in_dim(x, section, 0, keepdims=False)

    order_row = pick(group_order).astype(LOW)
    order_row = jnp.broadcast_to(
        jnp.concatenate([order_row, jnp.zeros((model_width - count,), LOW)])[None], (16, model_width)
    )
    packed = reshard(jnp.concatenate([pick(tokens), order_row], axis=0))
    current = packed[:segment].astype(F32)
    blocks_at = packed[segment, :count].astype(jnp.int32)
    upstream = reshard(pick(cotangent))
    seat = replica * half + lax.rem(shard, half)
    key_pos = (
        blocks_at[:, None] * segment + jnp.arange(segment, dtype=jnp.int32)[None, :]
    )
    unit_ids = plan.units * seat + jnp.arange(plan.units, dtype=jnp.int32)
    unit_part = lax.rem(unit_ids, plan.splits)
    parts_pos = key_pos.reshape(count, plan.splits, plan.part)
    query_pos = jnp.stack(
        [
            lax.dynamic_index_in_dim(parts_pos, unit_part[u], 1, keepdims=False).reshape(-1)
            for u in range(plan.units)
        ]
    )
    place = Bag(
        slot=unit_ids // plan.splits - (plan.units * seat) // plan.splits,
        query_pos=query_pos,
        key_pos=key_pos.reshape(-1),
    )

    small = jnp.concatenate(
        [
            norm_gains[0], norm_biases[0], qv_bias[0], out_bias, fc_bias.reshape(4, rows), proj_bias,
        ],
        axis=0,
    ).reshape(-1)
    small_rows = -(-small.shape[0] // (16 * model_width)) * 16
    small = jnp.concatenate(
        [small, jnp.zeros((small_rows * model_width - small.shape[0],), LOW)]
    ).reshape(small_rows, model_width)
    qkv = w_qkv[0]
    attn_sets = (
        jnp.concatenate([qkv[:, :model_width], qkv[:, model_width : 2 * model_width], small], axis=0),
        jnp.concatenate([qkv[:, 2 * model_width :], w_out[0], small], axis=0),
    )
    fc_blocks = w_fc[0].reshape(rows, 4, model_width).transpose(1, 0, 2).reshape(4 * rows, model_width)
    ffn_sets = (fc_blocks, w_proj[0])

    def gathered(sets):
        own = jnp.where(replica == 0, sets[0], sets[1])
        other_layer = swap(own, SECTION)
        layers = []
        for layer in range(2):
            chunk = jnp.where(section == layer, own, other_layer)
            chunks = ring_gather(chunk, count)
            buffer = jnp.zeros((2, count) + chunk.shape, LOW)
            for offset in range(count):
                twin = swap(chunks[offset], REPLICA)
                at = owner(offset)
                buffer = lax.dynamic_update_slice(buffer, chunks[offset][None, None], (replica, at, 0, 0))
                buffer = lax.dynamic_update_slice(buffer, twin[None, None], (1 - replica, at, 0, 0))
            layers.append(buffer)
        return layers

    attn = gathered(attn_sets)
    ffn = gathered(ffn_sets)

    def block(buffer, which, at):
        return buffer[which, :, at * rows : (at + 1) * rows].reshape(count * rows, model_width)

    def unpacked(layer):
        a, f = attn[layer], ffn[layer]
        vec = a[0, :, 2 * rows :].reshape(count, -1)[:, : 12 * rows].reshape(count, 12, rows).astype(F32)

        def row(i):
            return vec[:, i].reshape(-1)

        return Bag(
            q=block(a, 0, 0), k=block(a, 0, 1), v=block(a, 1, 0), o=block(a, 1, 1),
            fc=jnp.concatenate([block(f, 0, i) for i in range(4)], axis=1),
            proj=f[1].reshape(count * 4 * rows, model_width),
            gains=(row(0), row(1)), offsets=(row(2), row(3)), q_bias=row(4), v_bias=row(5),
            out_bias=row(6), fc_bias=vec[:, 7:11].reshape(-1), proj_bias=row(11),
        )

    weights = [unpacked(0), unpacked(1)]
    outputs, states = [], []
    for layer in range(2):
        output, saved = layer_forward(current, weights[layer], plan, place)
        outputs.append(output.astype(LOW))
        states.append(saved)
        current = outputs[-1].astype(F32)
    grad_inputs, totals = [None, None], [None, None]
    arriving = upstream.astype(F32)

    def pieces(attn_rows, layer_grads, which):
        pass

    def blocks_of(grad, cols):
        return grad.astype(LOW).reshape(count, -1, cols)

    def scattered(sets):
        own = jnp.where(replica == 0, sets[0], sets[1])
        other = jnp.where(replica == 0, sets[1], sets[0])
        paired = add_low(own, swap(other, REPLICA))
        return ring_scatter(
            lambda k: lax.dynamic_index_in_dim(paired, owner(k), 0, keepdims=False),
            paired.shape[1], count,
        )

    scattered_attn, scattered_ffn = [None, None], [None, None]
    for layer in (1, 0):
        grad_input, grads = layer_backward(arriving, states[layer], weights[layer], plan, place)
        grad_inputs[layer] = grad_input
        arriving = grad_input.astype(LOW).astype(F32)
        vec = jnp.concatenate(
            [
                grads.gains, grads.offsets, grads.qv_bias, grads.out_bias[None],
            ], axis=0,
        ).reshape(7, count, rows).transpose(1, 0, 2)
        vec = jnp.concatenate(
            [vec, grads.fc_bias.reshape(count, 4, rows), grads.proj_bias.reshape(count, 1, rows)],
            axis=1,
        ).astype(LOW).reshape(count, 12 * rows)
        vec = jnp.concatenate(
            [vec, jnp.zeros((count, small_rows * model_width - 12 * rows), LOW)], axis=1
        ).reshape(count, small_rows, model_width)
        scattered_ffn[layer] = scattered(
            (
                jnp.concatenate(
                    [blocks_of(grads.fc[:, i * model_width : (i + 1) * model_width], model_width) for i in range(4)],
                    axis=1,
                ),
                blocks_of(grads.proj, model_width),
            )
        )
        scattered_attn[layer] = scattered(
            (
                jnp.concatenate([blocks_of(grads.q, model_width), blocks_of(grads.k, model_width), vec], axis=1),
                jnp.concatenate([blocks_of(grads.v, model_width), blocks_of(grads.o, model_width), vec], axis=1),
            )
        )

    def finished(parts):
        own = jnp.where(section == 0, parts[0], parts[1])
        other = jnp.where(section == 0, parts[1], parts[0]).astype(LOW)
        total = (own + swap(other, SECTION).astype(F32)).astype(LOW)
        twin = swap(total, REPLICA)
        return (
            jnp.where(replica == 0, total, twin).astype(F32),
            jnp.where(replica == 0, twin, total).astype(F32),
        )

    ffn_total = finished(scattered_ffn)
    attn_total = finished(scattered_attn)
    fc_grad = ffn_total[0].reshape(4, rows, model_width).transpose(1, 0, 2).reshape(rows, 4 * model_width)
    proj_grad = ffn_total[1]
    qkv_grad = jnp.concatenate(
        [attn_total[0][:rows], attn_total[0][rows : 2 * rows], attn_total[1][:rows]], axis=1
    )
    out_grad = attn_total[1][rows : 2 * rows]
    vec = attn_total[0][2 * rows :].reshape(-1)[: 12 * rows].reshape(12, rows)

    def by_owner(per_layer):
        low = [reshard(v.astype(LOW)) for v in per_layer]
        own = jnp.where(section == 0, low[0], low[1])
        other = jnp.where(section == 0, low[1], low[0])
        got = swap(other, SECTION)
        return jnp.stack([jnp.where(section == 0, own, got), jnp.where(section == 0, got, own)])[None]

    acts = by_owner(outputs)
    in_grads = by_owner(grad_inputs).astype(F32)
    return (
        acts,
        in_grads,
        vec[0:2][None],
        vec[2:4][None],
        qkv_grad[None],
        vec[4:6][None],
        out_grad[None],
        vec[6][None],
        fc_grad[None],
        vec[7:11].reshape(1, 4 * rows),
        proj_grad[None],
        vec[11][None],
    )


ANY = pl.BlockSpec(memory_space=pl.ANY)
VMEM = pl.BlockSpec(memory_space=pltpu.VMEM)
SMEM = pl.BlockSpec(memory_space=pltpu.SMEM)
PAIR = 2 * HEAD
VMEM_LIMIT = 24 * 2**20
MEMORY_RATE = 3.69e6


def mm(a, b):
    return lax.dot_general(a, b, (((1,), (0,)), ((), ())), preferred_element_type=F32)


def mm_nt(a, b):
    return lax.dot_general(a, b, (((1,), (1,)), ((), ())), preferred_element_type=F32)


def mm_tn(a, b):
    return lax.dot_general(a, b, (((0,), (0,)), ((), ())), preferred_element_type=F32)


def call(body, micros, operands, specs, outs, scratch, saves=(), keep=True):
    outs = list(outs) + (list(saves) if keep else [])
    spare = [] if keep else [pltpu.VMEM(shape, kind) for shape, kind, _ in saves]
    return pl.pallas_call(
        body,
        in_specs=specs,
        out_specs=[ANY if space is True else VMEM for _, _, space in outs],
        out_shape=[
            {None: jax.ShapeDtypeStruct, True: pltpu.HBM, False: pltpu.VMEM}[space](shape, kind)
            for shape, kind, space in outs
        ],
        scratch_shapes=spare + scratch,
        compiler_params=pltpu.CompilerParams(vmem_limit_bytes=VMEM_LIMIT),
        cost_estimate=pl.CostEstimate(
            flops=0, bytes_accessed=int(micros * MEMORY_RATE), transcendentals=0
        ),
    )(*operands)


SEATS = 4


def low_lanes(shape):
    return lax.broadcasted_iota(jnp.int32, shape, len(shape) - 1) % PAIR < HEAD


def turn(tile):
    return pltpu.roll(tile, HEAD, 1)


def tiles_of(values, seat):
    at = 3 * seat // 2
    pair, single = (at, at + 1) if seat % 2 == 0 else (at + 1, at)
    return [values[:, t * PAIR : (t + 1) * PAIR] for t in (pair, single)]


def join(first, second, seat):
    low = low_lanes(first.shape)
    if seat % 2 == 0:
        return jnp.where(low, first, turn(second))
    return jnp.where(low, turn(first), second)


def fold(tile, seat):
    half = tile.shape[0] // 2
    return join(tile[:half], tile[half:], seat)


def split(tile, seat):
    low = low_lanes(tile.shape)
    turned = turn(tile)
    if seat % 2 == 0:
        return jnp.where(low, tile, 0.0), jnp.where(low, turned, 0.0)
    return jnp.where(low, 0.0, turned), jnp.where(low, 0.0, tile)


def unfold(tile, seat):
    return jnp.concatenate(split(tile, seat), axis=0)


def whole_rows(pairs, singles):
    tiles = []
    for even in range(0, SEATS, 2):
        tiles += [pairs[even], singles[even] + singles[even + 1], pairs[even + 1]]
    return jnp.concatenate(tiles, axis=1)


def start_all(copies):
    for copy in copies:
        copy.start()
    return copies


def wait_all(copies):
    for copy in copies:
        copy.wait()


def to_seats(scratch, outs, idx, count, sems):
    return start_all(
        [
            pltpu.make_async_copy(scratch.at[idx[count + 2 + k]], outs[k], sems.at[k])
            for k in range(SEATS)
        ]
    )


def from_seats(ins, scratch, idx, count, sems):
    return start_all(
        [
            pltpu.make_async_copy(ins[k], scratch.at[idx[count + 2 + k]], sems.at[k])
            for k in range(SEATS)
        ]
    )


def in_order(refs, scratch, at, sems, outward):
    copies = []
    for k in range(SEATS):
        for p in range(2):
            ends = refs[k].at[p], scratch.at[at[2 * k + p]]
            if outward:
                ends = ends[::-1]
            copies.append(pltpu.make_async_copy(*ends, sems.at[2 * k + p]))
    return start_all(copies)


def block_rows(segment):
    return 4 * segment + segment // 2


class Loader:
    def __init__(self, sems):
        self.sems = sems
        self.used = 0
        self.waits = {}

    def load(self, idx, count, own, twin, targets):
        slots = {}
        for which in (0, 1):
            for at, (offset, rows, ref, key) in enumerate(targets[which]):
                for k in range(count):
                    slots[which, at, k] = self.used
                    self.waits.setdefault(key, []).append((ref, self.used))
                    self.used += 1
        for rep in (0, 1):
            @pl.when(idx[count] == rep)
            def _():
                for which in (0, 1):
                    chunks = own if which == rep else twin
                    for at, (offset, rows, ref, key) in enumerate(targets[which]):
                        for k in range(count):
                            if len(chunks) == 1:
                                chunk, place = chunks[0].at[k], k
                            else:
                                chunk, place = chunks[k], idx[k]
                            pltpu.make_async_copy(
                                chunk.at[pl.ds(offset, rows)], ref.at[place],
                                self.sems.at[slots[which, at, k]],
                            ).start()

    def wait(self, key):
        for ref, slot in self.waits[key]:
            pltpu.make_async_copy(ref.at[0], ref.at[0], self.sems.at[slot]).wait()


def flat(ref):
    return ref[...].reshape(-1, ref.shape[-1])


def centre(values):
    average = jnp.mean(values, axis=-1, keepdims=True)
    centred = values - average
    scale = lax.rsqrt(jnp.mean(centred * centred, axis=-1, keepdims=True) + EPSILON)
    return centred * scale, scale


def centre_back(grad, hat, scale):
    return scale * (
        grad
        - jnp.mean(grad, axis=-1, keepdims=True)
        - hat * jnp.mean(grad * hat, axis=-1, keepdims=True)
    )


GELU_A, GELU_B = math.sqrt(2 / math.pi), 0.044715


NOTE = 16


def note_rows(small, width):
    rows = small.shape[1]
    hidden = jnp.pad(small[7:11].reshape(1, 4 * rows), ((0, 0), (0, width - 4 * rows)))
    others = jnp.concatenate([small[:7], small[11:]], axis=0)
    others = jnp.pad(others, ((0, NOTE - 9), (0, width - rows)))
    return jnp.concatenate([others, hidden], axis=0)


def read_notes(notes, count, width):
    rows = width // count
    total = None
    hidden = []
    for s in range(count):
        note = notes[s].astype(F32)
        moved = pltpu.roll(note, s * rows, 1) if s else note
        total = moved if total is None else total + moved
        at = (4 * rows * s) % width
        hidden.append(pltpu.roll(note[8:], at, 1)[NOTE - 9 :] if at else note[8:][NOTE - 9 :])
    per = width // (4 * rows)
    lines = [sum(hidden[b * per + i] for i in range(per)) for b in range(4)]
    return [total[:8]] + lines


def flatten(rings):
    chunks = [chunk for lists in rings for chunks in lists for chunk in chunks]
    return [pltpu.with_memory_space_constraint(chunk, pltpu.HBM) for chunk in chunks]


def load_projections(loader, idx, count, rows, chunks, wq, wk, wv, notes):
    first = [(0, rows, wq, 0), (rows, NOTE, notes, 3)]
    loader.load(idx, count, chunks[:count], chunks[count : 2 * count], [first, [(0, rows, wv, 2)]])
    loader.load(idx, count, chunks[2 * count : 3 * count], chunks[3 * count :], [[(0, rows, wk, 1)], []])


def load_output(loader, idx, count, rows, chunks, wo):
    loader.load(idx, count, chunks[2 * count : 3 * count], chunks[3 * count : 4 * count], [[], [(0, rows, wo, 5)]])


def load_feed(loader, idx, count, rows, chunks, wf, wp):
    for pair in range(2):
        own, twin = [chunks[(2 * pair + i) * count : (2 * pair + i + 1) * count] for i in range(2)]
        loader.load(
            idx, count, own, twin,
            [
                [(i * rows, rows, wf.at[2 * pair + i], 2 * pair + i) for i in range(2)],
                [(i * rows, rows, wp.at[:, 2 * pair + i], 4) for i in range(2)],
            ],
        )


def project_kernel(count, segment, inputs, hopped, attn, idx):
    width = inputs[0].shape[1]
    rows = width // count
    given = [] if hopped is None else [hopped]
    tall = block_rows(segment)
    loading = hopped is None

    def body(idx, first, second, *rest):
        arrived, rest = rest[: len(given)], rest[len(given) :]
        if loading:
            chunks, rest = rest[: 4 * count], rest[4 * count :]
            outs, (chosen, wq, wk, wv, vec, blocks, normed, notes, sems, out_sems) = rest[:SEATS], rest[SEATS:]
            loader = Loader(sems)
            load_projections(loader, idx, count, rows, chunks, wq, wk, wv, notes)
        else:
            (wq, wk, wv, vec), rest = rest[:4], rest[4:]
            outs, (chosen, normed, blocks, out_sems) = rest[:SEATS], rest[SEATS:]
        values = jnp.concatenate([first[:segment], second[:segment]], axis=0).astype(F32)
        if given:
            values = jnp.where(idx[count + 1] == 0, values, arrived[0][...].astype(F32))
        chosen[...] = values.astype(LOW)
        hat, _ = centre(values)
        if loading:
            loader.wait(3)
            lines = read_notes([notes[s] for s in range(count)], count, width)
            vec[0:8] = lines[0]
            for b in range(4):
                vec[8 + b : 9 + b] = lines[1 + b]
        low = (hat * vec[0:1] + vec[2:3]).astype(LOW)
        normed[...] = low
        if loading:
            loader.wait(0)
        queries = mm(low, flat(wq)) + vec[4:5]
        if loading:
            loader.wait(1)
        keys = mm(low, flat(wk))
        if loading:
            loader.wait(2)
        values = mm(low, flat(wv)) + vec[5:6]
        for d in range(SEATS):
            (qp, qs), (kp, ks), (vp, vs) = [tiles_of(x, d) for x in (queries, keys, values)]
            both = join(qs, ks, d)
            for p in range(2):
                span = slice(p * segment, (p + 1) * segment)
                for at, tile in enumerate((qp, kp, vp, both)):
                    blocks[d, p, at * segment : (at + 1) * segment] = tile[span].astype(LOW)
                blocks[d, p, 4 * segment :] = fold(vs[span], d).astype(LOW)
        wait_all(to_seats(blocks, outs, idx, count, out_sems))

    weight = ((count, rows, width), LOW, False)
    tokens = ((2 * segment, width), LOW, None)
    stay = ((2 * segment, width), LOW, False)
    blocks = pltpu.VMEM((SEATS, 2, tall, PAIR), LOW)
    sent = [((2, tall, PAIR), LOW, True)] * SEATS
    if loading:
        out = call(
            body, 7, [idx, *inputs, *flatten(attn)], [SMEM, VMEM, VMEM] + [ANY] * (4 * count),
            sent + [tokens, weight, weight, weight, ((12, width), F32, None)],
            [
                blocks, pltpu.VMEM((2 * segment, width), LOW), pltpu.VMEM((count, NOTE, width), LOW),
                pltpu.SemaphoreType.DMA((4 * count,)), pltpu.SemaphoreType.DMA((SEATS,)),
            ],
        )
        return out[:SEATS], out[SEATS], None, out[SEATS + 1 :]
    out = call(
        body, 7, [idx, *inputs, *given, *attn], [SMEM] + [VMEM] * (2 + len(given) + 4),
        sent + [stay, stay], [blocks, pltpu.SemaphoreType.DMA((SEATS,))],
    )
    return out[:SEATS], out[SEATS], out[SEATS + 1], attn


def read_heads(blocks, segment):
    def joined(at):
        return jnp.concatenate(
            [blocks[i, at * segment : (at + 1) * segment] for i in range(blocks.shape[0])], axis=0
        )

    third = joined(3).astype(F32)
    low = low_lanes(third.shape)
    values = [unfold(blocks[i, 4 * segment :].astype(F32), 0) for i in range(blocks.shape[0])]
    return (
        (joined(0), joined(1), joined(2)),
        (
            jnp.where(low, third, 0.0).astype(LOW), turn(third).astype(LOW),
            jnp.concatenate(values, axis=0).astype(LOW),
        ),
    )


def stacked(rows):
    low = low_lanes(rows.shape)
    zero = jnp.zeros_like(rows)
    return jnp.concatenate([jnp.where(low, rows, zero), jnp.where(low, zero, rows)], axis=0)


def unstacked(rows):
    half = rows.shape[0] // 2
    return jnp.where(low_lanes((half, PAIR)), rows[:half], rows[half:])


def earlier(rows, step):
    row = lax.broadcasted_iota(jnp.int32, (rows, step), 0) % step
    return lax.broadcasted_iota(jnp.int32, (rows, step), 1) <= row


def attend_kernel(count, segment, arrived, at, keep):
    length, step = count * segment, 2 * segment
    tall = block_rows(segment)
    short = segment + segment // 2

    def body(at, *rest):
        ins, outs, rest = rest[:SEATS], rest[SEATS : 2 * SEATS], rest[2 * SEATS :]
        attended, total, blocks, backs, sems, out_sems = rest
        wait_all(in_order(ins, blocks, at, sems, False))
        heads = read_heads(blocks, segment)
        for i in range(length // step):
            span = slice(i * step, (i + 1) * step)
            logs = []
            for g, (queries, keys, values) in enumerate(heads):
                query = queries[span] * SCALING
                if g == 0:
                    query = stacked(query)
                mask = earlier(query.shape[0], step)
                near = jnp.where(mask, mm_nt(query, keys[span]), FLOOR)
                highest = jnp.max(near, axis=-1, keepdims=True)
                if i > 0:
                    far = mm_nt(query, keys[: i * step])
                    highest = jnp.maximum(highest, jnp.max(far, axis=-1, keepdims=True))
                    far = jnp.exp(far - highest)
                near = jnp.exp(near - highest)
                denominator = jnp.sum(near, axis=-1, keepdims=True)
                result = mm(near.astype(LOW), values[span])
                if i > 0:
                    denominator += jnp.sum(far, axis=-1, keepdims=True)
                    result += mm(far.astype(LOW), values[: i * step])
                result = result * (1.0 / denominator)
                log = highest + jnp.log(denominator)
                if g == 0:
                    result = unstacked(result)
                    logs += [log[:step], log[step:]]
                else:
                    logs.append(log)
                attended[g, span] = result
                for p in range(2):
                    tile = result[p * segment : (p + 1) * segment]
                    if g == 0:
                        backs[2 * i + p, :segment] = tile.astype(LOW)
                    else:
                        backs[2 * i + p, segment:] = fold(tile, 0).astype(LOW)
            lane = lax.broadcasted_iota(jnp.int32, (step, PAIR), 1)
            total[span] = jnp.where(lane == 0, logs[0], jnp.where(lane == 1, logs[1], logs[2]))
        wait_all(in_order(outs, backs, at, out_sems, True))

    return call(
        body, 9, [at, *arrived], [SMEM] + [ANY] * SEATS,
        [((2, short, PAIR), LOW, True)] * SEATS,
        [
            pltpu.VMEM((count, tall, PAIR), LOW), pltpu.VMEM((count, short, PAIR), LOW),
            pltpu.SemaphoreType.DMA((2 * SEATS,)), pltpu.SemaphoreType.DMA((2 * SEATS,)),
        ],
        [((2, length, PAIR), F32, False), ((length, PAIR), F32, False)], keep,
    )


def attend_back_kernel(count, segment, arrived, grads, attended, total, at, ties):
    length, step = count * segment, 2 * segment
    tall = block_rows(segment)
    short = segment + segment // 2

    def body(at, attended, total, *rest):
        ins, grad_ins, rest = rest[:SEATS], rest[SEATS : 2 * SEATS], rest[2 * SEATS + len(ties) :]
        outs, rest = rest[:SEATS], rest[SEATS:]
        blocks, grads, backs, of_keys, of_values, sems, grad_sems, out_sems = rest
        first = in_order(ins, blocks, at, sems, False)
        second = in_order(grad_ins, grads, at, grad_sems, False)
        wait_all(first)
        heads = read_heads(blocks, segment)
        wait_all(second)
        for i in reversed(range(length // step)):
            span = slice(i * step, (i + 1) * step)
            third = None
            for g, (queries, keys, values) in enumerate(heads):
                query = queries[span] * SCALING
                if g == 0:
                    grad = jnp.concatenate([grads[2 * i + p, :segment] for p in range(2)], axis=0)
                    dots = grad.astype(F32) * attended[0, span]
                    low = low_lanes(dots.shape)
                    dots = jnp.concatenate([jnp.where(low, dots, 0.0), jnp.where(low, 0.0, dots)], axis=0)
                    log = jnp.concatenate([total[span, 0:1], total[span, 1:2]], axis=0)
                    query, grad = stacked(query), stacked(grad)
                else:
                    grad = jnp.concatenate(
                        [unfold(grads[2 * i + p, segment:].astype(F32), 0) for p in range(2)], axis=0
                    )
                    dots = grad * attended[1, span]
                    grad = grad.astype(LOW)
                    log = total[span, 2:3]
                dots = jnp.sum(dots, axis=-1, keepdims=True)
                parts = [(span, True)] + ([(slice(0, i * step), False)] if i > 0 else [])
                of_queries = None
                for keyed, near in parts:
                    weights = jnp.exp(mm_nt(query, keys[keyed]) - log)
                    if near:
                        weights = jnp.where(earlier(query.shape[0], step), weights, 0.0)
                    grad_scores = (weights * (mm_nt(grad, values[keyed]) - dots)).astype(LOW)
                    term = mm(grad_scores, keys[keyed])
                    of_queries = term if of_queries is None else of_queries + term
                    key_term = mm_tn(grad_scores, query)
                    value_term = mm_tn(weights.astype(LOW), grad)
                    if i == length // step - 1:
                        of_keys[g, keyed] = key_term
                        of_values[g, keyed] = value_term
                    else:
                        of_keys[g, keyed] += key_term
                        of_values[g, keyed] += value_term
                of_queries = of_queries * SCALING
                if g == 0:
                    of_queries = unstacked(of_queries)
                    for p in range(2):
                        backs[2 * i + p, :segment] = of_queries[p * segment : (p + 1) * segment].astype(LOW)
                else:
                    third = of_queries
            low = low_lanes((segment, PAIR))
            for p in range(2):
                own = slice(i * step + p * segment, i * step + (p + 1) * segment)
                block = backs.at[2 * i + p]
                block[segment : 2 * segment] = of_keys[0, own].astype(LOW)
                block[2 * segment : 3 * segment] = of_values[0, own].astype(LOW)
                block[3 * segment : 4 * segment] = join(
                    third[p * segment : (p + 1) * segment], of_keys[1, own], 0
                ).astype(LOW)
                block[4 * segment :] = fold(of_values[1, own], 0).astype(LOW)
        wait_all(in_order(outs, backs, at, out_sems, True))

    return call(
        body, 14, [at, attended, total, *arrived, *grads, *ties],
        [SMEM, VMEM, VMEM] + [ANY] * (2 * SEATS + len(ties)),
        [((2, tall, PAIR), LOW, True)] * SEATS,
        [
            pltpu.VMEM((count, tall, PAIR), LOW), pltpu.VMEM((count, short, PAIR), LOW),
            pltpu.VMEM((count, tall, PAIR), LOW), pltpu.VMEM((2, length, PAIR), F32),
            pltpu.VMEM((2, length, PAIR), F32), pltpu.SemaphoreType.DMA((2 * SEATS,)),
            pltpu.SemaphoreType.DMA((2 * SEATS,)), pltpu.SemaphoreType.DMA((2 * SEATS,)),
        ],
    )


def feed_rows(mid, vec, wf, wp, active, slope, wait):
    width = mid.shape[1]
    hat, scale = centre(mid)
    low = (hat * vec[1:2] + vec[3:4]).astype(LOW)
    for b in range(4):
        wait(b)
        span = slice(b * width, (b + 1) * width)
        u = mm(low, flat(wf.at[b])) + vec[8 + b : 9 + b]
        square = u * u
        t = jnp.tanh(u * (GELU_A + GELU_A * GELU_B * square))
        half = 0.5 + 0.5 * t
        active[:, span] = (u * half).astype(LOW)
        if slope is not None:
            slope[:, span] = (
                half + u * (0.5 - 0.5 * t * t) * (GELU_A + 3.0 * GELU_A * GELU_B * square)
            ).astype(LOW)
    wait(4)
    return low, hat, scale, (mid + mm(active[...], flat(wp)) + vec[7:8]).astype(LOW)


def feed_kernel(count, segment, returned, inputs, vec, rings, idx):
    width = inputs.shape[1]
    rows, tokens = width // count, 2 * segment
    short = segment + segment // 2

    def body(idx, x, vec, *rest):
        back, chunks, rest = rest[:SEATS], rest[SEATS : SEATS + 8 * count], rest[SEATS + 8 * count :]
        output, wo, wf, wp, blocks, active, sems, in_sems = rest
        loader = Loader(sems)
        copies = from_seats(back, blocks, idx, count, in_sems)
        load_output(loader, idx, count, rows, chunks, wo)
        load_feed(loader, idx, count, rows, chunks[4 * count :], wf, wp)
        wait_all(copies)
        low = read_returned(blocks, segment).astype(LOW)
        loader.wait(5)
        mid = x[...].astype(F32) + mm(low, flat(wo)) + vec[6:7]
        output[...] = feed_rows(mid, vec, wf, wp, active, None, loader.wait)[3]

    return call(
        body, 10, [idx, inputs, vec, *returned, *flatten(rings)],
        [SMEM, VMEM, VMEM] + [ANY] * (SEATS + 8 * count),
        [
            ((tokens, width), LOW, None), ((count, rows, width), LOW, False),
            ((4, count, rows, width), LOW, False), ((count, 4, rows, width), LOW, False),
        ],
        [
            pltpu.VMEM((SEATS, 2, short, PAIR), LOW), pltpu.VMEM((tokens, 4 * width), LOW),
            pltpu.SemaphoreType.DMA((9 * count,)), pltpu.SemaphoreType.DMA((SEATS,)),
        ],
    )


def read_returned(blocks, segment):
    pairs, singles = [], []
    for d in range(SEATS):
        pairs.append(jnp.concatenate([blocks[d, p, :segment].astype(F32) for p in range(2)], axis=0))
        singles.append(
            jnp.concatenate([unfold(blocks[d, p, segment:].astype(F32), d) for p in range(2)], axis=0)
        )
    return whole_rows(pairs, singles)


def feed_back_rows(wide, hat, scale, slope, vec, wo, wf, wp, gh, sums, blocks, segment):
    width = wide.shape[1]
    branch = wide.astype(LOW)
    weight = flat(wp)
    back = jnp.zeros(wide.shape, F32)
    for b in range(4):
        span = slice(b * width, (b + 1) * width)
        ga = mm_nt(branch, weight[span])
        low = (ga * slope[:, span].astype(F32)).astype(LOW)
        if sums is not None:
            gh[:, span] = low
            sums[3 + b : 4 + b] = jnp.sum(low.astype(F32), axis=0, keepdims=True)
        back += mm_nt(low, flat(wf.at[b]))
    total = wide + centre_back(back * vec[1:2], hat, scale)
    low = total.astype(LOW)
    values = mm_nt(low, flat(wo))
    for d in range(SEATS):
        pair, single = tiles_of(values, d)
        for p in range(2):
            part = slice(p * segment, (p + 1) * segment)
            blocks[d, p, :segment] = pair[part].astype(LOW)
            blocks[d, p, segment:] = fold(single[part], d).astype(LOW)
    if sums is not None:
        sums[0:1] = jnp.sum(back * hat, axis=0, keepdims=True)
        sums[1:2] = jnp.sum(back, axis=0, keepdims=True)
        sums[2:3] = jnp.sum(low.astype(F32), axis=0, keepdims=True)
        sums[7:8] = jnp.sum(wide, axis=0, keepdims=True)
    return total, low


def turn_kernel(count, segment, returned, inputs, vec, weights, grads, idx):
    width = inputs.shape[1]
    tokens = 2 * segment
    short = segment + segment // 2

    def body(idx, x, vec, wo, wf, wp, first, second, *rest):
        back, outs, rest = rest[:SEATS], rest[SEATS : 2 * SEATS], rest[2 * SEATS :]
        output, attended, middle, normed, slope, active, grad_middle, blocks, in_sems, out_sems = rest
        wait_all(from_seats(back, blocks, idx, count, in_sems))
        low = read_returned(blocks, segment).astype(LOW)
        attended[...] = low
        mid = x[...].astype(F32) + mm(low, flat(wo)) + vec[6:7]
        middle[...] = mid
        normed[...], hat, scale, output[...] = feed_rows(
            mid, vec, wf, wp, active, slope, lambda key: None
        )
        wide = jnp.concatenate([first[...], second[...]], axis=0).astype(F32)
        grad_middle[...] = feed_back_rows(
            wide, hat, scale, slope, vec, wo, wf, wp, None, None, blocks, segment
        )[0]
        wait_all(to_seats(blocks, outs, idx, count, out_sems))

    rows = ((tokens, width), LOW, False)
    return call(
        body, 10, [idx, inputs, vec, *weights, *grads, *returned],
        [SMEM] + [VMEM] * 7 + [ANY] * SEATS,
        [((2, short, PAIR), LOW, True)] * SEATS
        + [
            ((tokens, width), LOW, None), rows, ((tokens, width), F32, False), rows,
            ((tokens, 4 * width), LOW, False), ((tokens, 4 * width), LOW, False),
            ((tokens, width), F32, False),
        ],
        [
            pltpu.VMEM((SEATS, 2, short, PAIR), LOW), pltpu.SemaphoreType.DMA((SEATS,)),
            pltpu.SemaphoreType.DMA((SEATS,)),
        ],
    )


def feed_back_kernel(count, segment, grads, hopped, saved, weights, idx):
    width = grads[0].shape[1]
    tokens = 2 * segment
    short = segment + segment // 2

    def body(idx, first, second, hopped, middle, slope, vec, wo, wf, wp, *rest):
        outs, rest = rest[:SEATS], rest[SEATS:]
        grad_middle, mine, theirs, sums, grad_out, blocks, gh, out_sems = rest
        wide = jnp.concatenate([first[...], second[...]], axis=0).astype(F32)
        wide = jnp.where(idx[count + 1] == 1, wide, hopped[...].astype(F32))
        hat, scale = centre(middle[...])
        grad_middle[...], grad_out[...] = feed_back_rows(
            wide, hat, scale, slope, vec, wo, wf, wp, gh, sums, blocks, segment
        )
        copies = to_seats(blocks, outs, idx, count, out_sems)
        branch = wide.astype(LOW)

        def part(values, core):
            half = values.shape[1] // 2
            return values[:, core * half : (core + 1) * half]

        def fill(rep):
            for ref, core in ((mine, rep), (theirs, 1 - rep)):
                ref[:, : 2 * width] = part(gh, core)
                ref[:, 2 * width :] = part(branch, core)

        for rep in range(2):
            pl.when(idx[count] == rep)(functools.partial(fill, rep))

        wait_all(copies)

    return call(
        body, 14,
        [
            idx, *grads, hopped, saved.middle, saved.slope, saved.vec,
            *weights,
        ],
        [SMEM] + [VMEM] * 9,
        [((2, short, PAIR), LOW, True)] * SEATS
        + [
            ((tokens, width), F32, None), ((tokens, 5 * width // 2), LOW, None),
            ((tokens, 5 * width // 2), LOW, None), ((8, width), F32, None), ((tokens, width), LOW, None),
        ],
        [
            pltpu.VMEM((SEATS, 2, short, PAIR), LOW), pltpu.VMEM((tokens, 4 * width), LOW),
            pltpu.SemaphoreType.DMA((SEATS,)),
        ],
    )


def project_back_kernel(count, segment, returned, grad_middle, grad_out, saved, weights, idx, keep):
    tokens, width = grad_middle.shape
    rows = width // count
    tall = block_rows(segment)
    kept = [grad_out] if keep else []

    def body(idx, grad_middle, x, vec, *rest):
        held, rest = rest[: len(kept)], rest[len(kept) :]
        back, rest = rest[:SEATS], rest[SEATS:]
        (wq, wk, wv), rest = rest[:3], rest[3:]
        grad_low, grad_in, mine, theirs, sums, blocks, in_sems = rest
        copies = from_seats(back, blocks, idx, count, in_sems)
        hat, scale = centre(x[...].astype(F32))
        wait_all(copies)
        pairs, singles = [[], [], []], [[], [], []]
        for d in range(SEATS):
            for at in range(3):
                pairs[at].append(
                    jnp.concatenate(
                        [blocks[d, p, at * segment : (at + 1) * segment].astype(F32) for p in range(2)], axis=0
                    )
                )
            both = [split(blocks[d, p, 3 * segment : 4 * segment].astype(F32), d) for p in range(2)]
            for at in range(2):
                singles[at].append(jnp.concatenate([b[at] for b in both], axis=0))
            singles[2].append(
                jnp.concatenate([unfold(blocks[d, p, 4 * segment :].astype(F32), d) for p in range(2)], axis=0)
            )
        gq, gk, gv = [whole_rows(a, b).astype(LOW) for a, b in zip(pairs, singles)]
        total = mm_nt(gq, flat(wq))
        total += mm_nt(gk, flat(wk))
        total += mm_nt(gv, flat(wv))
        result = grad_middle[...] + centre_back(total * vec[0:1], hat, scale)
        grad_low[...] = result.astype(LOW)
        if not keep:
            return
        grad_in[...] = result
        sums[0:1] = jnp.sum(total * hat, axis=0, keepdims=True)
        sums[1:2] = jnp.sum(total, axis=0, keepdims=True)
        sums[2:3] = jnp.sum(gq.astype(F32), axis=0, keepdims=True)
        sums[3:4] = jnp.sum(gv.astype(F32), axis=0, keepdims=True)
        sums[4:8] = jnp.zeros((4, width), F32)
        (grad_out,) = held

        def fill(first, second):
            first[:, :width] = gq
            first[:, width:] = gk
            second[:, :width] = gv
            second[:, width:] = grad_out[...]

        @pl.when(idx[count] == 0)
        def _():
            fill(mine, theirs)

        @pl.when(idx[count] == 1)
        def _():
            fill(theirs, mine)

    return call(
        body, 8, [idx, grad_middle, saved.inputs, saved.vec, *kept, *returned, *weights],
        [SMEM] + [VMEM] * (3 + len(kept)) + [ANY] * SEATS + [VMEM] * 3,
        [((tokens, width), LOW, None)],
        [
            pltpu.VMEM((SEATS, 2, tall, PAIR), LOW), pltpu.SemaphoreType.DMA((SEATS,)),
        ],
        [
            ((tokens, width), F32, None), ((tokens, 2 * width), LOW, None),
            ((tokens, 2 * width), LOW, None), ((8, width), F32, None),
        ],
        keep,
    )


def send_out(scratch, pieces, idx, sems, start):
    for at, (out, to, rows, base, stride, k) in enumerate(pieces):
        source = pl.ds(pl.multiple_of(base + idx[k] * stride, 16), rows)
        copy = pltpu.make_async_copy(scratch.at[source], out.at[pl.ds(to, rows)], sems.at[at])
        copy.start() if start else copy.wait()


def rows_of(refs, span=slice(None)):
    return jnp.concatenate([ref[:, span] for ref in refs], axis=0)


def ffn_terms_kernel(count, normed, active, late, idx):
    width = normed[0].shape[1]
    rows, half = width // count, width // 2

    def body(idx, *rest):
        normed, active, late, rest = rest[:2], rest[2:4], rest[4:6], rest[6:]
        outs, (inward, outward, sems) = rest[: 2 * count], rest[2 * count :]
        narrow = rows_of(normed)
        pieces = []
        for b in range(2):
            inward[b * width : (b + 1) * width] = mm_tn(
                narrow, rows_of(late, slice(b * width, (b + 1) * width))
            ).astype(LOW)
            pieces.append([(outs[k], b * rows, rows, b * width, rows, k) for k in range(count)])
            send_out(inward, pieces[b], idx, sems.at[pl.ds(b * count, count)], True)
        branch = rows_of(late, slice(2 * width, 2 * width + half))
        for b in range(4):
            span = slice(b * width, (b + 1) * width)
            outward[span] = mm_tn(rows_of(active, span), branch).astype(LOW)
        pieces.append([(outs[count + k], 0, 4 * rows, 0, 4 * rows, k) for k in range(count)])
        send_out(outward, pieces[2], idx, sems.at[pl.ds(2 * count, count)], True)
        for b, scratch in enumerate((inward, inward, outward)):
            send_out(scratch, pieces[b], idx, sems.at[pl.ds(b * count, count)], False)

    outs = call(
        body, 5, [idx, *normed, *active, *late], [SMEM] + [VMEM] * 6,
        [((2 * rows, width), LOW, True)] * count + [((4 * rows, half), LOW, True)] * count,
        [
            pltpu.VMEM((2 * width, width), LOW), pltpu.VMEM((4 * width, half), LOW),
            pltpu.SemaphoreType.DMA((3 * count,)),
        ],
    )
    return outs[:count], outs[count:]


def attn_terms_kernel(count, normed, attended, late, sums_one, sums_two, idx):
    width = normed[0].shape[1]
    rows = width // count

    def body(idx, *rest):
        normed, attended, late, (one, two), rest = rest[:2], rest[2:4], rest[4:6], rest[6:8], rest[8:]
        outs, (scratch, notes, sems, note_sems) = rest[: 2 * count], rest[2 * count :]

        def pieces(b):
            return [(outs[b * count + k], 0, rows, b * width, rows, k) for k in range(count)]

        flatly = jnp.concatenate(
            [
                one[0:1], two[0:1], one[1:2], two[1:2], one[2:3], one[3:4], two[2:3], two[7:8],
                jnp.zeros((NOTE - 8, width), F32),
            ],
            axis=0,
        )
        lane = lax.broadcasted_iota(jnp.int32, (NOTE, width), 1)
        line = lax.broadcasted_iota(jnp.int32, (NOTE, width), 0)
        for s in range(count):
            note = pltpu.roll(flatly, width - s * rows, 1) if s else flatly
            start = 4 * rows * s
            hidden = two[3 + start // width : 4 + start // width]
            hidden = pltpu.roll(
                jnp.broadcast_to(hidden, (8, width)), (width - start % width) % width, 1
            )
            hidden = jnp.concatenate([hidden, hidden], axis=0)
            note = jnp.where(
                (line < 8) & (lane < rows), note,
                jnp.where((line == NOTE - 1) & (lane < 4 * rows), hidden, 0.0),
            )
            notes[s] = note.astype(LOW)
        copies = start_all(
            [
                pltpu.make_async_copy(
                    notes.at[idx[k]], outs[k].at[pl.ds(rows, NOTE)], note_sems.at[k]
                )
                for k in range(count)
            ]
        )
        for b in range(2):
            grads = rows_of(late, slice(b * width, (b + 1) * width))
            if b == 0:
                scratch[:width] = mm_tn(rows_of(normed), grads).astype(LOW)
            else:

                @pl.when(idx[count] == 0)
                def _():
                    scratch[width:] = mm_tn(rows_of(normed), grads).astype(LOW)

                @pl.when(idx[count] == 1)
                def _():
                    scratch[width:] = mm_tn(rows_of(attended), grads).astype(LOW)

            send_out(scratch, pieces(b), idx, sems.at[pl.ds(b * count, count)], True)
        for b in range(2):
            send_out(scratch, pieces(b), idx, sems.at[pl.ds(b * count, count)], False)
        wait_all(copies)

    outs = call(
        body, 5, [idx, *normed, *attended, *late, sums_one, sums_two], [SMEM] + [VMEM] * 8,
        [((rows + NOTE, width), LOW, True)] * count + [((rows, width), LOW, True)] * count,
        [
            pltpu.VMEM((2 * width, width), LOW), pltpu.VMEM((count, NOTE, width), LOW),
            pltpu.SemaphoreType.DMA((2 * count,)), pltpu.SemaphoreType.DMA((count,)),
        ],
    )
    return outs[:count], outs[count:]


def lay_out(count, pairs, idx, shapes, columns):
    flat_pairs = [value for pair in pairs for value in pair]

    def body(idx, *rest):
        refs, outs = rest[: len(flat_pairs)], rest[len(flat_pairs) :]

        def fill(rep):
            cores = [(refs[2 * i + rep], refs[2 * i + 1 - rep]) for i in range(len(pairs))]
            for out, parts in zip(outs, columns(*cores)):
                at = 0
                for part in parts:
                    out[:, at : at + part.shape[1]] = part.astype(F32)
                    at += part.shape[1]

        for rep in range(2):
            pl.when(idx[count] == rep)(functools.partial(fill, rep))

    return call(
        body, 3, [idx, *flat_pairs], [SMEM] + [VMEM] * len(flat_pairs),
        [(shape, F32, None) for shape in shapes], [],
    )


class Rings:
    def __init__(self, rings):
        self.rings = rings

    def step(self, *after):
        for ring in self.rings:
            ring.step(*after)

    @property
    def last(self):
        return [v for ring in self.rings for v in ring.last if v is not None]


def hold(values, *after):
    return lax.optimization_barrier((values, after))[0] if len(after) else values


class GatherRing:
    def __init__(self, chunk, count, rightward):
        self.right, self.left = ring_pairs(count)
        self.count, self.rightward, self.at = count, rightward, 0
        self.last = (chunk, chunk)
        self.own = {0: chunk}
        self.twin = {}

    def pass_on(self, *after):
        places = [k for k in self.own if k not in self.twin]
        for k, value in zip(places, hold([self.own[k] for k in places], *after)):
            self.twin[k] = swap(value, REPLICA)

    def step(self, *after):
        near, far = hold(self.last, *after)
        self.at += 1
        if self.at < self.count // 2:
            near = lax.ppermute(near, SHARD, self.right)
            far = lax.ppermute(far, SHARD, self.left)
            self.own[self.count - self.at], self.own[self.at] = near, far
            self.last = (near, far)
        else:
            if self.rightward:
                last = lax.ppermute(near, SHARD, self.right)
            else:
                last = lax.ppermute(far, SHARD, self.left)
            self.own[self.at] = last
            self.last = (last,)

    def lists(self):
        self.pass_on()
        return [[side[k] for k in range(self.count)] for side in (self.own, self.twin)]


class ScatterRing:
    def __init__(self, pieces, count, rightward):
        self.right, self.left = ring_pairs(count)
        self.pieces, self.count, self.rightward = pieces, count, rightward
        self.at = count // 2
        self.last = None

    def step(self, *after):
        pieces, half = self.pieces, self.count // 2
        if self.at == half:
            far = hold(pieces[half], *after)
            if self.rightward:
                self.last = (lax.ppermute(far, SHARD, self.right), None)
            else:
                self.last = (None, lax.ppermute(far, SHARD, self.left))
        else:
            last = hold([v for v in self.last if v is not None], *after)
            sides = []
            for piece, term in zip((pieces[self.at], pieces[self.count - self.at]), self.last):
                sides.append(piece if term is None else add_low(piece, last.pop(0)))
            if len(after) > 0 and None in self.last:
                sides = hold(sides, *after)
            self.last = (
                lax.ppermute(sides[0], SHARD, self.right), lax.ppermute(sides[1], SHARD, self.left)
            )
        self.at -= 1

    def total(self):
        return self.pieces[0].astype(F32) + self.last[0].astype(F32) + self.last[1].astype(F32)


def fast_device(
    tokens, cotangent, group_order, norm_gains, norm_biases, w_qkv, qv_bias, w_out, out_bias,
    w_fc, fc_bias, w_proj, proj_bias,
):
    count = lax.axis_size(SHARD)
    section = lax.axis_index(SECTION)
    replica = lax.axis_index(REPLICA)
    shard = lax.axis_index(SHARD)
    segment, width = tokens.shape[1], tokens.shape[2]
    rows = w_qkv.shape[1]
    half = count // 2
    order = ring_order(count)
    position = jnp.asarray(np.argsort(np.array(order)), jnp.int32)[shard]
    around = lax.rem(position + jnp.arange(count, dtype=jnp.int32), count)
    seat = 2 * replica + lax.rem(shard, 2)
    others = seat ^ jnp.arange(SEATS, dtype=jnp.int32)
    idx = jnp.concatenate(
        [jnp.asarray(order, jnp.int32)[around], jnp.stack([replica, section]).astype(jnp.int32), others]
    )

    ways = [
        [
            (r * count + 2 * z + y, (z // 2) * count + 2 * (2 * r + (z + j) % 2) + y)
            for r in range(2) for z in range(half) for y in range(2)
        ]
        for j in range(2)
    ]
    odd = lax.rem(shard // 2, 2)

    def gather_in(x, j, *more):
        own = lax.dynamic_index_in_dim(x, lax.rem(odd + j, 2), 0, keepdims=False)
        own = jnp.concatenate([own, *more], axis=0) if more else own
        return lax.ppermute(own, (REPLICA, SHARD), ways[j])

    def give_back(x):
        return [
            lax.ppermute(
                x[j * segment : (j + 1) * segment], (REPLICA, SHARD), [(b, a) for a, b in ways[j]]
            )
            for j in range(2)
        ]

    def by_sequence(parts):
        return jnp.stack([jnp.where(even, *parts), jnp.where(even, *parts[::-1])])[None]

    def exchange(parts):
        diagonal = [(r * count + s, (1 - r) * count + (s ^ 1)) for r in range(2) for s in range(count)]
        return [
            pltpu.with_memory_space_constraint(parts[0], pltpu.HBM),
            lax.ppermute(parts[1], SHARD, [(s, s ^ 1) for s in range(count)]),
            swap(parts[2], REPLICA),
            lax.ppermute(parts[3], (REPLICA, SHARD), diagonal),
        ]

    small = jnp.concatenate(
        [norm_gains[0], norm_biases[0], qv_bias[0], out_bias, fc_bias.reshape(4, rows), proj_bias],
        axis=0,
    )
    qkv = w_qkv[0]
    attn_own = [
        jnp.concatenate(
            [jnp.where(replica == 0, qkv[:, :width], qkv[:, 2 * width :]), note_rows(small, width)], axis=0
        ),
        jnp.where(replica == 0, qkv[:, width : 2 * width], w_out[0]),
    ]
    ffn_own = [
        jnp.where(
            replica == 0,
            jnp.concatenate([w_fc[0][:, b * width : (b + 1) * width] for b in (2 * i, 2 * i + 1)], axis=0),
            w_proj[0][2 * i * rows : 2 * (i + 1) * rows],
        )
        for i in range(2)
    ]

    attn_ring = Rings([GatherRing(own, count, i == 0) for i, own in enumerate(attn_own)])
    attn_ring.step()
    order_row = lax.dynamic_index_in_dim(group_order, odd, 0).astype(LOW)
    order_rows = jnp.pad(order_row, ((0, NOTE - 1), (0, width - count)))
    tokens = hold(tokens, attn_ring.last)
    packed = [gather_in(tokens, 0, order_rows), gather_in(tokens, 1)]
    slot = lax.rem(shard // 2 + jnp.arange(2, dtype=jnp.int32), 2)
    which = ((4 * (others // 2) + others % 2)[:, None] + 2 * slot[None, :]).reshape(-1)
    chosen = (which[:, None] == jnp.arange(count, dtype=jnp.int32)[None, :]).astype(jnp.int32)
    packed, chosen, even = lax.optimization_barrier((packed, chosen, odd == 0))
    blocks_at = packed[0][segment, :count].astype(jnp.int32)
    at = jnp.sum(chosen * blocks_at[None, :], axis=1)
    attn_ring.step()
    attn_ring.step()
    ffn_ring = Rings(
        [GatherRing(hold(own, attn_ring.last), count, i == 0) for i, own in enumerate(ffn_own)]
    )
    ffn_ring.step()
    attn_ring.step()
    for ring in attn_ring.rings:
        ring.pass_on(attn_ring.last)
    attn_lists = [ring.lists() for ring in attn_ring.rings]

    def forward(hopped, attn, before):
        sent, inputs, normed, attn = project_kernel(count, segment, packed, hopped, attn, idx)
        arrived = exchange(before[0](sent))
        back = attend_kernel(count, segment, before[1](arrived), at, hopped is not None)
        state = Bag(vec=attn[3], inputs=inputs, normed=normed, arrived=arrived)
        return state, attn, exchange(before[2](back[:SEATS])), back[SEATS:]

    def ring_sent(sent):
        ffn_ring.step(sent[1])
        return sent

    def ring_arrived(arrived):
        ffn_ring.step(arrived[1])
        return arrived

    def ring_back(back):
        ffn_ring.step(back[1])
        return back

    def ring_feed():
        for ring in ffn_ring.rings:
            ring.pass_on(ffn_ring.last)
        return [ring.lists() for ring in ffn_ring.rings]

    def same(values):
        return values

    first, attn, returned, _ = forward(None, attn_lists, [ring_sent, ring_arrived, ring_back])
    output, *ffn = feed_kernel(
        count, segment, returned, first.inputs, first.vec,
        attn_lists + ring_feed(), idx,
    )

    def hop(values, backward):
        return lax.ppermute(values, SECTION, [(1, 0)] if backward else [(0, 1)])

    upstream = [gather_in(hold(cotangent, output), j) for j in range(2)]
    state, attn, returned, kept = forward(
        hop(output, False), attn, [same, lambda arrived: hold(arrived, upstream), same]
    )
    state.attended, state.total = kept
    *sent, output, state.attended_low, state.middle, state.normed_two, state.slope, state.active, grad_middle = (
        turn_kernel(count, segment, returned, state.inputs, state.vec, ffn, upstream, idx)
    )
    kept_rows = state.normed_two, state.active, state.normed, state.attended_low
    pairs, acts = [], []

    def aside(back):
        pairs.extend([own, swap(hold(own, back[0]), REPLICA)] for own in kept_rows)
        acts.extend(give_back(hold(output, back[0])))
        return back

    def backward(sent, grad_middle, grad_out, keep, ties, between):
        arrived = exchange(sent)
        ties = ties + between[0](arrived)
        back = attend_back_kernel(
            count, segment, state.arrived, arrived, state.attended, state.total, at, ties
        )
        returned = exchange(between[1](back))
        return project_back_kernel(
            count, segment, between[2](returned), grad_middle, grad_out, state, attn[:3], idx, keep
        )

    early = backward(
        sent, grad_middle, None, False, [],
        [lambda arrived: [], aside, same],
    )
    hopped, acts, pairs = lax.optimization_barrier((hop(early[0], True), acts, pairs))
    acts = by_sequence(acts)
    rings = []
    *sent, grad_middle, mine, theirs, sums_two, grad_out = feed_back_kernel(
        count, segment, upstream, hopped, state, ffn, idx
    )

    def ffn_terms(arrived):
        terms = ffn_terms_kernel(
            count, pairs[0], pairs[1], hold([mine, swap(theirs, REPLICA)], arrived), idx
        )
        rings.append(Rings([ScatterRing(t, count, i == 0) for i, t in enumerate(terms)]))
        rings[0].step()
        return [terms[0][0]]

    def ring_back(back):
        back = hold(back, rings[0].last)
        rings[0].step(back[0])
        return back

    low, *last = backward(sent, grad_middle, grad_out, True, [], [ffn_terms, ring_back, same])
    own, got, sums_one = hold((last[1], swap(last[2], REPLICA), last[3]), rings[0].last)
    terms = attn_terms_kernel(count, pairs[2], pairs[3], [own, got], sums_one, sums_two, idx)
    rings.append(Rings([ScatterRing(t, count, i == 0) for i, t in enumerate(terms)]))
    rings[0].step()
    rings[1].step()
    rings[1].step()
    rings[0].step()
    in_grads = give_back(hold(last[0].astype(LOW), rings[1].last))
    rings[1].step()
    rings[1].step()
    in_grads = by_sequence(hold(in_grads, rings[1].last)).astype(F32)

    def finished(ring):
        total = ring.total().astype(LOW)
        return [total, swap(total, REPLICA)]

    feed_totals, totals = [[finished(ring) for ring in pair.rings] for pair in rings]
    fc_grad, proj_grad = lay_out(
        count, feed_totals, idx, ((rows, 4 * width), (4 * rows, width)),
        lambda inward, outward: (
            [inward[core][b * rows : (b + 1) * rows] for core in range(2) for b in range(2)],
            [outward[core][...] for core in range(2)],
        ),
    )

    def vectors(first):
        note = first[0][rows:].astype(F32) + first[1][rows:].astype(F32)
        lines = [(0, 2), (2, 4), (4, 6), (6, 7), (7, 8)]
        return [[note[a:b, :rows]] for a, b in lines] + [[note[NOTE - 1 :, : 4 * rows]]]

    qkv_grad, out_grad, *vecs = lay_out(
        count, totals, idx,
        ((rows, 3 * width), (rows, width)) + ((2, rows),) * 3 + ((1, rows),) * 2 + ((1, 4 * rows),),
        lambda first, second: (
            [first[0][:rows], second[0][...], first[1][:rows]], [second[1][...]], *vectors(first),
        ),
    )
    return (
        acts, in_grads, vecs[0][None], vecs[1][None], qkv_grad[None], vecs[2][None],
        out_grad[None], vecs[3], fc_grad[None], vecs[5], proj_grad[None], vecs[4],
    )


def on_each(tokens, *others):
    count = lax.axis_size(SHARD)
    tiles = (tokens.shape[2] // count) % 32 == 0 and tokens.shape[1] % 64 == 0
    seats = count == 2 * SEATS and tokens.shape[0] == 2 and HEADS == 3 * SEATS
    return (fast_device if tiles and seats else on_device)(tokens, *others)


def solution(mesh):
    in_specs = (
        P(REPLICA, SHARD, None),
        P(REPLICA, SHARD, None),
        P(REPLICA, None),
        P(SECTION, None, SHARD),
        P(SECTION, None, SHARD),
        P(SECTION, SHARD, None),
        P(SECTION, None, SHARD),
        P(SECTION, SHARD, None),
        P(SECTION, SHARD),
        P(SECTION, SHARD, None),
        P(SECTION, SHARD),
        P(SECTION, SHARD, None),
        P(SECTION, SHARD),
    )
    out_specs = (
        P(SECTION, REPLICA, SHARD, None),
        P(SECTION, REPLICA, SHARD, None),
        P(SECTION, None, SHARD),
        P(SECTION, None, SHARD),
        P(SECTION, SHARD, None),
        P(SECTION, None, SHARD),
        P(SECTION, SHARD, None),
        P(SECTION, SHARD),
        P(SECTION, SHARD, None),
        P(SECTION, SHARD),
        P(SECTION, SHARD, None),
        P(SECTION, SHARD),
    )
    return jax.shard_map(
        on_each, mesh=mesh, in_specs=in_specs, out_specs=out_specs, check_vma=False
    )
```
